32 devices in a mesh: section: 2 (over core), tp: 16 (over z, y, x).
Axes of the slice: x: 2, y: 2, z: 4, core: 2. Of those that a mesh axis runs over, the one named last changes fastest.
Arguments:
- start_tokens: bfloat16 [2, 32, 8192], P(None, None, 'tp'), may hold values from -6 to 6
- target_weight: bfloat16 [2, 8192, 8192], P('section', None, 'tp'), may hold values from -0.0625 to 0.0625
- online_weight: bfloat16 [2, 8192, 8192], P('section', 'tp'), may hold values from -0.0625 to 0.0625
- head_weight: bfloat16 [8192, 256], P('tp'), may hold values from -0.0625 to 0.0625
- reward: float32 [2, 32], P(None, 'section'), may hold values from -6 to 6
- action_bin: int32 [2, 32], P(None, 'section'), may hold values from 0 to 255
Outputs:
- target_value: float32 [2, 32], P(None, 'section')
- q_taken: float32 [2, 32], P(None, 'section')
The draws below stay inside these ranges and needn't reach their ends.
All inputs are finite; a program needn't handle non-finite values.
Results may differ from the reference program's by a relative error of at most 0.018.
Values may be sent and summed in bfloat16 or wider, within the bound.
No kernel may reach another device: no remote copies, remote signals or barrier semaphores. Data moves between devices by JAX's collectives and lax.ppermute only.
A program may use at most 128 MiB of HBM per device.

```python
import jax
import jax.numpy as jnp
from jax import lax

D = 8192
BINS = 256
ROWS = 32
MICRO = 2
LAYERS = 2


def touch_ends(drawn, rng, smallest, high):
    extent = drawn.shape
    spot = [jax.random.randint(jax.random.fold_in(rng, axis), (), 0, extent[axis]) for axis in range(len(extent))]
    drawn = drawn.at[tuple(spot)].set(smallest)
    longest = extent.index(max(extent))
    spot[longest] = (spot[longest] + 1) % extent[longest]
    return drawn.at[tuple(spot)].set(high)


def steps_of(key, dims, shards, low, high):
    level = 1.0
    for dim, parts in shards:
        draws = jax.random.uniform(jax.random.fold_in(jax.random.fold_in(key, 6), dim), (parts,), jnp.float32, low / len(shards), high / len(shards))
        level = level * jnp.repeat(jnp.exp(draws), dims[dim] // parts).reshape((-1,) + (1,) * (len(dims) - 1 - dim))
    return level


def normal_values(stream_key, extent, width, most, shards=(), held_as=jnp.bfloat16):
    values = jax.random.normal(stream_key, extent, jnp.float32) * width
    if len(shards) > 0:
        values = steps_of(stream_key, extent, shards, -0.22, 0.18) * values
    return jnp.clip(values, min=-most, max=most).astype(held_as)


def setup_inputs(seed: int = 0) -> dict:
    keys = jax.random.split(jax.random.key(seed), 7)
    return {
        "start_tokens": normal_values(keys[0], (MICRO, ROWS, D), 1.0, 6.0, ((2, 16),)),
        "target_weight": normal_values(keys[1], (LAYERS, D, D), D ** -0.5, 0.0625, ((0, 2), (2, 16))),
        "online_weight": normal_values(keys[2], (LAYERS, D, D), D ** -0.5, 0.0625, ((0, 2), (1, 16))),
        "head_weight": normal_values(keys[3], (D, BINS), D ** -0.5, 0.0625, ((0, 16),)),
        "reward": normal_values(keys[4], (MICRO, ROWS), 1.0, 6.0, ((1, 2),), jnp.float32),
        "action_bin": touch_ends(jax.random.randint(keys[5], (MICRO, ROWS), 0, BINS), jax.random.fold_in(keys[5], 1), 0, BINS - 1).astype(jnp.int32),
    }


def reference(start_tokens, target_weight, online_weight, head_weight, reward, action_bin):
    hidden = start_tokens.reshape(MICRO * ROWS, D)
    for layer in range(LAYERS):
        blended = (0.25 * online_weight[layer].astype(jnp.float32) + 0.75 * target_weight[layer].astype(jnp.float32)).astype(jnp.bfloat16)
        wide = hidden.astype(jnp.float32)
        normed = (wide * lax.rsqrt(lax.optimization_barrier(jnp.mean(wide * wide, axis=1, keepdims=True)) + 1e-06)).astype(jnp.bfloat16)
        hidden = (wide + jnp.dot(normed, blended, preferred_element_type=jnp.float32)).astype(jnp.bfloat16)
    values = jnp.dot(hidden, head_weight, preferred_element_type=jnp.float32)
    best = lax.optimization_barrier(jnp.max(values, axis=1)).reshape(MICRO, ROWS)
    chosen = (jnp.arange(BINS, dtype=jnp.int32)[None, :] == action_bin.reshape(MICRO * ROWS, 1)).astype(jnp.float32)
    taken = lax.optimization_barrier(jnp.sum(values * chosen, axis=1)).reshape(MICRO, ROWS)
    return (reward + 0.98 * best, taken)
```

```python
import functools

import jax
import jax.numpy as jnp
from jax import lax
from jax.experimental import pallas as pl
from jax.experimental.pallas import tpu as pltpu
from jax.sharding import PartitionSpec as P


def digits_of(size, most):
    radices = []
    left = size
    while left > 1:
        radix = next((r for r in range(min(most, left), 1, -1) if left % r == 0), None)
        if radix is None:
            radix = next(r for r in range(2, left + 1) if left % r == 0)
        radices.insert(0, radix)
        left //= radix
    strides = []
    stride = size
    for radix in radices:
        stride //= radix
        strides.append(stride)
    return list(zip(radices, strides))


def peer(digit, step, radix):
    if radix & (radix - 1) == 0:
        return digit ^ step
    return (digit + step) % radix


def exchange(value, sections, tp, section, radix, stride, step, forward=False):
    route = []
    for t in range(tp):
        digit = t // stride % radix
        other = t + (peer(digit, step, radix) - digit) * stride
        pair = (t, other) if forward else (other, t)
        route.append((section * tp + pair[0], section * tp + pair[1]))
    return lax.ppermute(value, ("section", "tp"), route)


def relative(tp, digits, position):
    found = [position]
    for radix, stride in digits:
        digit = position // stride % radix
        found = [
            one + (peer(digit, step, radix) - digit) * stride for step in range(radix) for one in found
        ]
    return jnp.stack(found).astype(jnp.int32)


def spread_kernel(where, x, weight, *rest, groups):
    outs, (held, arrived) = rest[:groups], rest[groups:]
    count, _, width = held.shape
    share = count // groups
    copies = []
    for j in range(count):
        columns = pl.ds(pl.multiple_of(where[j] * width, width), width)
        copies.append(pltpu.make_async_copy(weight.at[0, :, columns], held.at[j], arrived.at[j]))
        copies[-1].start()
    for j in range(count):
        copies[j].wait()
        part = jnp.dot(x[...], held[j], preferred_element_type=jnp.float32)
        outs[j // share][j % share] = part.astype(jnp.bfloat16)


def spread(where, x, weight, groups):
    rows, depth = x.shape
    count = where.shape[0]
    width = weight.shape[2] // count
    share = count // groups
    return pl.pallas_call(
        functools.partial(spread_kernel, groups=groups),
        out_shape=[jax.ShapeDtypeStruct((share, rows, width), jnp.bfloat16)] * groups,
        in_specs=[
            pl.BlockSpec(memory_space=pltpu.SMEM),
            pl.BlockSpec(memory_space=pltpu.VMEM),
            pl.BlockSpec(memory_space=pl.ANY),
        ],
        out_specs=[pl.BlockSpec(memory_space=pltpu.VMEM)] * groups,
        scratch_shapes=[
            pltpu.VMEM((count, depth, width), jnp.bfloat16),
            pltpu.SemaphoreType.DMA((count,)),
        ],
        compiler_params=pltpu.CompilerParams(vmem_limit_bytes=40 * 2**20),
        name="spread",
    )(where, x, weight)


def meet_kernel(where, total_in, square_in, weight, *rest):
    blocks, (total, square, held, arrived) = rest[:-4], rest[-4:]
    count, depth, _ = held.shape
    copies = []
    for j in range(count):
        rows = pl.ds(pl.multiple_of(where[j] * depth, depth), depth)
        copies.append(pltpu.make_async_copy(weight.at[0, rows, :], held.at[j], arrived.at[j]))
        copies[-1].start()
    sum_of = total_in[...]
    squares = square_in[...]
    j = 0
    for block in blocks:
        for i in range(block.shape[0]):
            x = block[i]
            wide = x.astype(jnp.float32)
            squares = squares + jnp.sum(wide * wide, axis=1, keepdims=True)
            copies[j].wait()
            sum_of = sum_of + jnp.dot(x, held[j], preferred_element_type=jnp.float32)
            j += 1
    total[...] = sum_of
    square[...] = squares


def meet(where, total, square, weight, blocks):
    depth = blocks[0].shape[2]
    width = weight.shape[2]
    count = where.shape[0]
    vmem = pl.BlockSpec(memory_space=pltpu.VMEM)
    return pl.pallas_call(
        meet_kernel,
        out_shape=[
            jax.ShapeDtypeStruct(total.shape, jnp.float32),
            jax.ShapeDtypeStruct(square.shape, jnp.float32),
        ],
        in_specs=[pl.BlockSpec(memory_space=pltpu.SMEM), vmem, vmem, pl.BlockSpec(memory_space=pl.ANY)]
        + [vmem] * len(blocks),
        out_specs=[vmem, vmem],
        scratch_shapes=[
            pltpu.VMEM((count, depth, width), jnp.bfloat16),
            pltpu.SemaphoreType.DMA((count,)),
        ],
        compiler_params=pltpu.CompilerParams(vmem_limit_bytes=40 * 2**20),
        name="meet",
    )(where, total, square, weight, *blocks)


def per_device(start_tokens, target_weight, online_weight, head_weight, reward, action_bin, sections, tp):
    micro, tokens, width = start_tokens.shape
    rows = micro * tokens
    features = width * tp
    section = lax.axis_index("section")
    position = lax.axis_index("tp")
    digits = digits_of(tp, 4)
    where_gathered = relative(tp, digits, position)
    where_spread = relative(tp, digits, position)
    hidden = start_tokens.reshape(rows, width)
    for layer in range(sections):
        swap = functools.partial(exchange, sections=sections, tp=tp, section=layer)
        inner_radix = digits[-1][0] if digits else 1
        parts = spread(where_spread, hidden, online_weight, inner_radix)
        stack = hidden[None]
        total = jnp.zeros((rows, width), jnp.float32)
        square = jnp.zeros((rows, 1), jnp.float32)
        for number, (radix, stride) in enumerate(digits):
            got = [swap(stack, radix=radix, stride=stride, step=step) for step in range(1, radix)]
            if number == len(digits) - 1:
                total, square = meet(where_gathered[: stack.shape[0]], total, square, target_weight, [stack])
                total, square = meet(where_gathered[stack.shape[0] :], total, square, target_weight, got)
            else:
                stack = jnp.concatenate([stack] + got, axis=0)
        for number in range(len(digits) - 1, -1, -1):
            radix, stride = digits[number]
            got = [
                swap(parts[step], radix=radix, stride=stride, step=step, forward=True) for step in range(1, radix)
            ]
            wide = parts[0].astype(jnp.float32)
            for one in got:
                wide = wide + one.astype(jnp.float32)
            if number > 0:
                following = digits[number - 1][0]
                share = wide.shape[0] // following
                parts = [
                    wide[step * share : (step + 1) * share].astype(jnp.bfloat16) for step in range(following)
                ]
        scale = lax.rsqrt(square / features + 1e-06)
        update = scale * (0.25 * wide[0] + 0.75 * total)
        hidden = (hidden.astype(jnp.float32) + update).astype(jnp.bfloat16)
        if layer + 1 < sections:
            hop = [(layer * tp + t, (layer + 1) * tp + t) for t in range(tp)]
            hidden = lax.ppermute(hidden, ("section", "tp"), hop)
    values = jnp.dot(hidden, head_weight, preferred_element_type=jnp.float32)
    last = sections - 1
    for radix, stride in digits:
        got = [exchange(values, sections, tp, last, radix, stride, step) for step in range(1, radix)]
        for one in got:
            values = values + one
    share_rows = reward.shape[1]
    values = values.reshape(micro, tokens, values.shape[1])
    mine = values[:, last * share_rows :]
    for other in range(last):
        hop = [(last * tp + t, other * tp + t) for t in range(tp)]
        sent = values[:, other * share_rows : (other + 1) * share_rows]
        mine = jnp.where(section == other, lax.ppermute(sent, ("section", "tp"), hop), mine)
    best = jnp.max(mine, axis=2)
    bins = lax.broadcasted_iota(jnp.int32, mine.shape, 2)
    taken = jnp.sum(jnp.where(bins == action_bin[:, :, None], mine, 0.0), axis=2)
    return (reward + 0.98 * best, taken)


def solution(mesh):
    in_specs = (
        P(None, None, "tp"),
        P("section", None, "tp"),
        P("section", "tp", None),
        P("tp", None),
        P(None, "section"),
        P(None, "section"),
    )
    out_specs = (P(None, "section"), P(None, "section"))
    body = functools.partial(per_device, sections=mesh.shape["section"], tp=mesh.shape["tp"])
    return jax.shard_map(body, mesh=mesh, in_specs=in_specs, out_specs=out_specs, check_vma=False)
```

```python
import functools

import jax
import jax.numpy as jnp
from jax import lax
from jax.experimental import pallas as pl
from jax.experimental.pallas import tpu as pltpu
from jax.sharding import PartitionSpec as P


def digits_of(size, most):
    radices = []
    left = size
    while left > 1:
        radix = next((r for r in range(min(most, left), 1, -1) if left % r == 0), None)
        if radix is None:
            radix = next(r for r in range(2, left + 1) if left % r == 0)
        radices.insert(0, radix)
        left //= radix
    strides = []
    stride = size
    for radix in radices:
        stride //= radix
        strides.append(stride)
    return list(zip(radices, strides))


def peer(digit, step, radix):
    if radix & (radix - 1) == 0:
        return digit ^ step
    return (digit + step) % radix


def exchange(value, axes, tp, section, radix, stride, step):
    route = []
    for t in range(tp):
        digit = t // stride % radix
        other = t + (peer(digit, step, radix) - digit) * stride
        route.append((section * tp + t, section * tp + other))
    return lax.ppermute(value, axes, route)


def relative(digits, position):
    found = [position]
    for radix, stride in digits:
        digit = position // stride % radix
        found = [
            one + (peer(digit, step, radix) - digit) * stride for step in range(radix) for one in found
        ]
    return found


def spread_kernel(where, x, weight, *rest, groups):
    outs, (held, arrived) = rest[:groups], rest[groups:]
    count, _, width = held.shape
    share = count // groups

    @pl.when(where[count] != 0)
    def _():
        copies = []
        for j in range(count):
            columns = pl.ds(pl.multiple_of(where[j] * width, width), width)
            copies.append(pltpu.make_async_copy(weight.at[0, :, columns], held.at[j], arrived.at[j]))
            copies[-1].start()
        for j in range(count):
            copies[j].wait()
            part = jnp.dot(x[...], held[j], preferred_element_type=jnp.float32)
            outs[j // share][j % share] = part.astype(outs[0].dtype)


def spread(where, active, x, weight, tp, groups, dtype):
    rows, depth = x.shape
    count = len(where)
    width = weight.shape[2] // tp
    share = count // groups
    return pl.pallas_call(
        functools.partial(spread_kernel, groups=groups),
        out_shape=[jax.ShapeDtypeStruct((share, rows, width), dtype)] * groups,
        in_specs=[
            pl.BlockSpec(memory_space=pltpu.SMEM),
            pl.BlockSpec(memory_space=pltpu.VMEM),
            pl.BlockSpec(memory_space=pltpu.HBM),
        ],
        out_specs=[pl.BlockSpec(memory_space=pltpu.VMEM)] * groups,
        scratch_shapes=[
            pltpu.VMEM((count, depth, width), jnp.bfloat16),
            pltpu.SemaphoreType.DMA((count,)),
        ],
        compiler_params=pltpu.CompilerParams(vmem_limit_bytes=40 * 2**20),
        name="spread",
    )(jnp.stack(where + [active]), x, pltpu.with_memory_space_constraint(weight, pltpu.HBM))


def meet_kernel(active, blocks, weight, total, square, held, arrived):
    count, depth, _ = held.shape

    @pl.when(active[0] != 0)
    def _():
        copies = []
        for j in range(count):
            copies.append(
                pltpu.make_async_copy(weight.at[0, pl.ds(j * depth, depth), :], held.at[j], arrived.at[j])
            )
            copies[-1].start()
        sum_of = jnp.zeros(total.shape, jnp.float32)
        squares = jnp.zeros(square.shape, jnp.float32)
        for j in range(count):
            x = blocks[j]
            wide = x.astype(jnp.float32)
            squares = squares + jnp.sum(wide * wide, axis=1, keepdims=True)
            copies[j].wait()
            sum_of = sum_of + jnp.dot(x, held[j], preferred_element_type=jnp.float32)
        total[...] = sum_of
        square[...] = squares


def meet(active, blocks, weight):
    count, rows, depth = blocks.shape
    width = weight.shape[2]
    vmem = pl.BlockSpec(memory_space=pltpu.VMEM)
    return pl.pallas_call(
        meet_kernel,
        out_shape=[
            jax.ShapeDtypeStruct((rows, width), jnp.float32),
            jax.ShapeDtypeStruct((rows, 1), jnp.float32),
        ],
        in_specs=[pl.BlockSpec(memory_space=pltpu.SMEM), vmem, pl.BlockSpec(memory_space=pltpu.HBM)],
        out_specs=[vmem, vmem],
        scratch_shapes=[
            pltpu.VMEM((count, depth, width), jnp.bfloat16),
            pltpu.SemaphoreType.DMA((count,)),
        ],
        compiler_params=pltpu.CompilerParams(vmem_limit_bytes=40 * 2**20),
        name="meet",
    )(active[None], blocks, pltpu.with_memory_space_constraint(weight, pltpu.HBM))


def per_device(start_tokens, target_weight, online_weight, head_weight, reward, action_bin, sections, digits, names):
    micro, tokens, width = start_tokens.shape
    tp = 1
    for radix, _ in digits:
        tp *= radix
    everyone = ("section",) + names
    rows = micro * tokens
    features = width * tp
    section = lax.axis_index("section")
    position = lax.axis_index(names)
    where = relative(digits, position)
    hidden = start_tokens.reshape(rows, width)
    for layer in range(sections):
        swap = functools.partial(exchange, axes=everyone, tp=tp, section=layer)
        active = (section == layer).astype(jnp.int32)
        inner_radix = digits[-1][0]
        share = tp // inner_radix
        sent = spread(where[share:], active, hidden, online_weight, tp, inner_radix - 1, jnp.bfloat16)
        kept = spread(where[:share], active, hidden, online_weight, tp, 1, jnp.float32)
        blocks = lax.all_gather(hidden, names, axis=0)
        total, square = meet(active, blocks, target_weight)
        wide = kept[0]
        for number in range(len(digits) - 1, -1, -1):
            radix, stride = digits[number]
            got = [swap(sent[step - 1], radix=radix, stride=stride, step=step) for step in range(1, radix)]
            for one in got:
                wide = wide + one.astype(jnp.float32)
            if number > 0:
                following = digits[number - 1][0]
                share = wide.shape[0] // following
                sent = [
                    wide[step * share : (step + 1) * share].astype(jnp.bfloat16) for step in range(1, following)
                ]
                wide = wide[:share]
        scale = lax.rsqrt(square / features + 1e-06)
        update = scale * (0.25 * wide[0] + 0.75 * total)
        hidden = (hidden.astype(jnp.float32) + update).astype(jnp.bfloat16)
        if layer + 1 < sections:
            hop = [(layer * tp + t, (layer + 1) * tp + t) for t in range(tp)]
            hidden = lax.ppermute(hidden, everyone, hop)
    values = jnp.dot(hidden, head_weight, preferred_element_type=jnp.float32)
    values = values.reshape(micro, tokens, values.shape[1])
    last = sections - 1
    share_rows = reward.shape[1]
    mine = values[:, last * share_rows :]
    for other in range(last):
        hop = [(last * tp + t, other * tp + t) for t in range(tp)]
        part = values[:, other * share_rows : (other + 1) * share_rows]
        mine = jnp.where(section == other, lax.ppermute(part, everyone, hop), mine)
    for (radix, _), name in zip(digits, names):
        told = jnp.broadcast_to(mine[None], (radix,) + mine.shape)
        mine = jnp.sum(lax.all_to_all(told, name, split_axis=0, concat_axis=0, tiled=True), axis=0)
    best = jnp.max(mine, axis=2)
    bins = lax.broadcasted_iota(jnp.int32, mine.shape, 2)
    taken = jnp.sum(jnp.where(bins == action_bin[:, :, None], mine, 0.0), axis=2)
    return (reward + 0.98 * best, taken)


def solution(mesh):
    sections, tp = mesh.shape["section"], mesh.shape["tp"]
    digits = digits_of(tp, 4)
    names = tuple(f"tp{number}" for number in range(len(digits)))
    cut = jax.sharding.Mesh(
        mesh.devices.reshape([sections] + [radix for radix, _ in digits]), ("section",) + names
    )
    in_specs = (
        P(None, None, names),
        P("section", None, names),
        P("section", names, None),
        P(names, None),
        P(None, "section"),
        P(None, "section"),
    )
    out_specs = (P(None, "section"), P(None, "section"))
    body = functools.partial(per_device, sections=sections, digits=digits, names=names)
    return jax.shard_map(body, mesh=cut, in_specs=in_specs, out_specs=out_specs, check_vma=False)
```

```python
import functools

import jax
import jax.numpy as jnp
from jax import lax
from jax.experimental import pallas as pl
from jax.experimental.pallas import tpu as pltpu
from jax.sharding import PartitionSpec as P


def digits_of(size, most):
    radices = []
    left = size
    while left > 1:
        radix = next((r for r in range(min(most, left), 1, -1) if left % r == 0), None)
        if radix is None:
            radix = next(r for r in range(2, left + 1) if left % r == 0)
        radices.insert(0, radix)
        left //= radix
    strides = []
    stride = size
    for radix in radices:
        stride //= radix
        strides.append(stride)
    return list(zip(radices, strides))


def peer(digit, step, radix):
    if radix & (radix - 1) == 0:
        return digit ^ step
    return (digit + step) % radix


def exchange(value, axes, tp, route, radix, stride, step):
    pairs = []
    for t in range(tp):
        digit = t // stride % radix
        other = t + (peer(digit, step, radix) - digit) * stride
        pairs.append((route[0] * tp + t, route[1] * tp + other))
    return lax.ppermute(value, axes, pairs)


def relative(digits, position):
    found = [position]
    for radix, stride in digits:
        digit = position // stride % radix
        found = [
            one + (peer(digit, step, radix) - digit) * stride for step in range(radix) for one in found
        ]
    return found


def spread_kernel(where, x, weight, *rest, groups):
    outs, (held, arrived) = rest[:groups], rest[groups:]
    count, _, width = held.shape
    share = count // groups

    @pl.when(where[count] != 0)
    def _():
        copies = []
        for j in range(count):
            columns = pl.ds(pl.multiple_of(where[j] * width, width), width)
            copies.append(pltpu.make_async_copy(weight.at[0, :, columns], held.at[j], arrived.at[j]))
            copies[-1].start()
        for j in range(count):
            copies[j].wait()
            part = jnp.dot(x[...], held[j], preferred_element_type=jnp.float32)
            outs[j // share][j % share] = part.astype(outs[0].dtype)


def spread(where, active, x, weight, tp, groups, dtype):
    rows, depth = x.shape
    count = len(where)
    width = weight.shape[2] // tp
    share = count // groups
    return pl.pallas_call(
        functools.partial(spread_kernel, groups=groups),
        out_shape=[jax.ShapeDtypeStruct((share, rows, width), dtype)] * groups,
        in_specs=[
            pl.BlockSpec(memory_space=pltpu.SMEM),
            pl.BlockSpec(memory_space=pltpu.VMEM),
            pl.BlockSpec(memory_space=pltpu.HBM),
        ],
        out_specs=[pl.BlockSpec(memory_space=pltpu.VMEM)] * groups,
        scratch_shapes=[
            pltpu.VMEM((count, depth, width), jnp.bfloat16),
            pltpu.SemaphoreType.DMA((count,)),
        ],
        compiler_params=pltpu.CompilerParams(vmem_limit_bytes=40 * 2**20),
        name="spread",
    )(jnp.stack(where + [active]), x, pltpu.with_memory_space_constraint(weight, pltpu.HBM))


def meet_kernel(where, total_in, square_in, weight, *rest):
    blocks, (total, square, held, arrived) = rest[:-4], rest[-4:]
    count, depth, _ = held.shape

    @pl.when(where[count] != 0)
    def _():
        copies = []
        for j in range(count):
            rows = pl.ds(pl.multiple_of(where[j] * depth, depth), depth)
            copies.append(pltpu.make_async_copy(weight.at[0, rows, :], held.at[j], arrived.at[j]))
            copies[-1].start()
        sum_of = total_in[...]
        squares = square_in[...]
        j = 0
        for block in blocks:
            for i in range(block.shape[0]):
                x = block[i]
                wide = x.astype(jnp.float32)
                squares = squares + jnp.sum(wide * wide, axis=1, keepdims=True)
                copies[j].wait()
                sum_of = sum_of + jnp.dot(x, held[j], preferred_element_type=jnp.float32)
                j += 1
        total[...] = sum_of
        square[...] = squares


def meet(where, active, total, square, blocks, weight):
    count = len(where)
    depth = blocks[0].shape[2]
    width = weight.shape[2]
    vmem = pl.BlockSpec(memory_space=pltpu.VMEM)
    return pl.pallas_call(
        meet_kernel,
        out_shape=[
            jax.ShapeDtypeStruct(total.shape, jnp.float32),
            jax.ShapeDtypeStruct(square.shape, jnp.float32),
        ],
        in_specs=[pl.BlockSpec(memory_space=pltpu.SMEM), vmem, vmem, pl.BlockSpec(memory_space=pltpu.HBM)]
        + [vmem] * len(blocks),
        out_specs=[vmem, vmem],
        scratch_shapes=[
            pltpu.VMEM((count, depth, width), jnp.bfloat16),
            pltpu.SemaphoreType.DMA((count,)),
        ],
        compiler_params=pltpu.CompilerParams(vmem_limit_bytes=40 * 2**20),
        name="meet",
    )(
        jnp.stack(where + [active]),
        total,
        square,
        pltpu.with_memory_space_constraint(weight, pltpu.HBM),
        *blocks,
    )


def per_device(start_tokens, target_weight, online_weight, head_weight, reward, action_bin, sections, digits, names):
    micro, tokens, width = start_tokens.shape
    tp = 1
    for radix, _ in digits:
        tp *= radix
    everyone = ("section",) + names
    rows = micro * tokens
    features = width * tp
    section = lax.axis_index("section")
    position = lax.axis_index(names)
    where = relative(digits, position)
    inner, inner_stride = digits[-1]
    share = tp // inner
    hidden = start_tokens.reshape(rows, width)
    for layer in range(sections):
        helper = layer - 1 if layer > 0 else min(1, sections - 1)
        own = hidden
        if layer > 0:
            own = exchange(hidden, everyone, tp, (helper, layer), 1, 1, 0)
        active = (section == layer).astype(jnp.int32)

        stack = hidden[None]
        for radix, stride in digits[:-1]:
            got = [
                exchange(stack, everyone, tp, (helper, helper), radix, stride, step) for step in range(1, radix)
            ]
            stack = jnp.concatenate([stack] + got, axis=0)
        sent = spread(where[share:], active, own, online_weight, tp, inner - 1, jnp.bfloat16)
        gathered = []
        for step in range(inner):
            if step == 0 and helper == layer:
                gathered.append(stack)
            else:
                gathered.append(
                    exchange(stack, everyone, tp, (helper, layer), inner, inner_stride, step)
                )
        kept = spread(where[:share], active, own, online_weight, tp, 1, jnp.float32)
        wide = kept[0]
        for number in range(len(digits) - 1, -1, -1):
            radix, stride = digits[number]
            for step in range(1, radix):
                one = exchange(sent[step - 1], everyone, tp, (layer, layer), radix, stride, step)
                wide = wide + one.astype(jnp.float32)
            if number > 0:
                following = digits[number - 1][0]
                part = wide.shape[0] // following
                sent = [
                    wide[step * part : (step + 1) * part].astype(jnp.bfloat16) for step in range(1, following)
                ]
                wide = wide[:part]

        total = jnp.zeros((rows, width), jnp.float32)
        square = jnp.zeros((rows, 1), jnp.float32)
        half = max(1, inner // 2)
        for first in range(0, inner, half):
            groups = gathered[first : first + half]
            ids = where[first * share : (first + len(groups)) * share]
            total, square = meet(ids, active, total, square, groups, target_weight)
        scale = lax.rsqrt(square / features + 1e-06)
        update = scale * (0.25 * wide[0] + 0.75 * total)
        hidden = (own.astype(jnp.float32) + update).astype(jnp.bfloat16)
    values = jnp.dot(hidden, head_weight, preferred_element_type=jnp.float32)

    bins = values.shape[1]
    share_rows = reward.shape[1]
    values = values.reshape(micro, sections, share_rows, bins).transpose(1, 0, 2, 3)
    values = values.reshape(sections, micro * share_rows, bins).astype(jnp.bfloat16)
    told = jnp.broadcast_to(values[:, None], (sections, inner) + values.shape[1:])
    told = told.reshape((sections * inner,) + values.shape[1:])
    told = lax.all_to_all(told, ("section", names[-1]), split_axis=0, concat_axis=0, tiled=True)
    mine = jnp.sum(told[(sections - 1) * inner :].astype(jnp.float32), axis=0)
    for (radix, _), name in zip(digits[:-1], names):
        told = jnp.broadcast_to(mine.astype(jnp.bfloat16)[None], (radix,) + mine.shape)
        told = lax.all_to_all(told, name, split_axis=0, concat_axis=0, tiled=True)
        mine = jnp.sum(told.astype(jnp.float32), axis=0)
    mine = mine.reshape(micro, share_rows, bins)
    best = jnp.max(mine, axis=2)
    bin_ids = lax.broadcasted_iota(jnp.int32, mine.shape, 2)
    taken = jnp.sum(jnp.where(bin_ids == action_bin[:, :, None], mine, 0.0), axis=2)
    return (reward + 0.98 * best, taken)


def solution(mesh):
    sections, tp = mesh.shape["section"], mesh.shape["tp"]
    digits = digits_of(tp, 4)
    names = tuple(f"tp{number}" for number in range(len(digits)))
    cut = jax.sharding.Mesh(
        mesh.devices.reshape([sections] + [radix for radix, _ in digits]), ("section",) + names
    )
    in_specs = (
        P(None, None, names),
        P("section", None, names),
        P("section", names, None),
        P(names, None),
        P(None, "section"),
        P(None, "section"),
    )
    out_specs = (P(None, "section"), P(None, "section"))
    body = functools.partial(per_device, sections=sections, digits=digits, names=names)
    return jax.shard_map(body, mesh=cut, in_specs=in_specs, out_specs=out_specs, check_vma=False)
```

```python
import functools

import jax
import jax.numpy as jnp
from jax import lax
from jax.experimental import pallas as pl
from jax.experimental.pallas import tpu as pltpu
from jax.sharding import PartitionSpec as P


def digits_of(size, most):
    radices = []
    left = size
    while left > 1:
        radix = next((r for r in range(min(most, left), 1, -1) if left % r == 0), None)
        if radix is None:
            radix = next(r for r in range(2, left + 1) if left % r == 0)
        radices.insert(0, radix)
        left //= radix
    strides = []
    stride = size
    for radix in radices:
        stride //= radix
        strides.append(stride)
    return list(zip(radices, strides))


def peer(digit, step, radix):
    if radix & (radix - 1) == 0:
        return digit ^ step
    return (digit + step) % radix


def exchange(value, axes, tp, route, radix, stride, step):
    pairs = []
    for t in range(tp):
        digit = t // stride % radix
        other = t + (peer(digit, step, radix) - digit) * stride
        pairs.append((route[0] * tp + t, route[1] * tp + other))
    return lax.ppermute(value, axes, pairs)


def relative(digits, position):
    found = [position]
    for radix, stride in digits:
        digit = position // stride % radix
        found = [
            one + (peer(digit, step, radix) - digit) * stride for step in range(radix) for one in found
        ]
    return found


def spread_kernel(where, x, weight, *outs):
    share, _, width = outs[0].shape
    count = share * len(outs)

    @pl.when(where[count] != 0)
    def _():
        for j in range(count):
            columns = pl.ds(pl.multiple_of(where[j] * width, width), width)
            part = jnp.dot(x[...], weight[0, :, columns], preferred_element_type=jnp.float32)
            outs[j // share][j % share] = part.astype(outs[0].dtype)


def spread(where, active, x, weight, groups):
    rows, _ = x.shape
    count = len(where)
    width = weight.shape[2] // count
    share = count // groups
    vmem = pl.BlockSpec(memory_space=pltpu.VMEM)
    return pl.pallas_call(
        spread_kernel,
        out_shape=[jax.ShapeDtypeStruct((share, rows, width), jnp.bfloat16)] * groups,
        in_specs=[pl.BlockSpec(memory_space=pltpu.SMEM), vmem, vmem],
        out_specs=[vmem] * groups,
        compiler_params=pltpu.CompilerParams(vmem_limit_bytes=8 * 2**20),
        name="spread",
    )(jnp.stack(where + [active]), x, weight)


def meet_kernel(where, total_in, square_in, weight, *rest):
    blocks, (total, square) = rest[:-2], rest[-2:]
    share, _, depth = blocks[0].shape
    count = share * len(blocks)

    @pl.when(where[count] != 0)
    def _():
        sum_of = total_in[...]
        squares = square_in[...]
        for j in range(count):
            x = blocks[j // share][j % share]
            wide = x.astype(jnp.float32)
            squares = squares + jnp.sum(wide * wide, axis=1, keepdims=True)
            rows = pl.ds(pl.multiple_of(where[j] * depth, depth), depth)
            sum_of = sum_of + jnp.dot(x, weight[0, rows, :], preferred_element_type=jnp.float32)
        total[...] = sum_of
        square[...] = squares


def meet(where, active, total, square, blocks, weight):
    vmem = pl.BlockSpec(memory_space=pltpu.VMEM)
    return pl.pallas_call(
        meet_kernel,
        out_shape=[
            jax.ShapeDtypeStruct(total.shape, jnp.float32),
            jax.ShapeDtypeStruct(square.shape, jnp.float32),
        ],
        in_specs=[pl.BlockSpec(memory_space=pltpu.SMEM), vmem, vmem, vmem] + [vmem] * len(blocks),
        out_specs=[vmem, vmem],
        compiler_params=pltpu.CompilerParams(vmem_limit_bytes=8 * 2**20),
        name="meet",
    )(jnp.stack(where + [active]), total, square, weight, *blocks)


def per_device(start_tokens, target_weight, online_weight, head_weight, reward, action_bin, sections, digits, names):
    micro, tokens, width = start_tokens.shape
    tp = 1
    for radix, _ in digits:
        tp *= radix
    everyone = ("section",) + names
    rows = micro * tokens
    features = width * tp
    section = lax.axis_index("section")
    position = lax.axis_index(names)
    where = relative(digits, position)
    rounds = len(digits)
    send = functools.partial(exchange, axes=everyone, tp=tp)
    online_weight = pltpu.with_memory_space_constraint(online_weight, pltpu.VMEM)
    target_weight = pltpu.with_memory_space_constraint(target_weight, pltpu.VMEM)
    hidden = start_tokens.reshape(rows, width)
    for layer in range(sections):
        helper = layer - 1 if layer > 0 else min(1, sections - 1)
        own = hidden
        if layer > 0:
            own = send(hidden, route=(helper, layer), radix=1, stride=1, step=0)
        active = (section == layer).astype(jnp.int32)

        parts = spread(where, active, own, online_weight, digits[-1][0])
        stack, mine = (own[None], hidden[None]) if rounds % 2 == 0 else (hidden[None], own[None])
        gathered = [mine]
        for number, (radix, stride) in enumerate(digits):
            route = (helper, layer) if (rounds - number) % 2 == 1 else (layer, helper)
            if number > 0 and helper != layer:
                gathered = [send(stack, route=route, radix=radix, stride=stride, step=0)]
            else:
                gathered = [mine]
            for step in range(1, radix):
                gathered.append(send(stack, route=route, radix=radix, stride=stride, step=step))
            if number < rounds - 1:
                gathered, parts = lax.optimization_barrier((gathered, parts))
                stack = mine = jnp.concatenate(gathered, axis=0)
        at = layer
        for number in range(rounds - 1, -1, -1):
            radix, stride = digits[number]
            to = at if (number + 1) % 2 == 1 and at == layer else (helper if at == layer else layer)
            wide = parts[0] if to == at else send(parts[0], route=(at, to), radix=radix, stride=stride, step=0)
            wide = wide.astype(jnp.float32)
            for step in range(1, radix):
                one = send(parts[step], route=(at, to), radix=radix, stride=stride, step=step)
                wide = wide + one.astype(jnp.float32)
            at = to
            if number > 0:
                following = digits[number - 1][0]
                part = wide.shape[0] // following
                parts = [wide[step * part : (step + 1) * part].astype(jnp.bfloat16) for step in range(following)]

        total = jnp.zeros((rows, width), jnp.float32)
        square = jnp.zeros((rows, 1), jnp.float32)
        share = tp // len(gathered)
        half = max(1, len(gathered) // 2)
        for first in range(0, len(gathered), half):
            groups = gathered[first : first + half]
            ids = where[first * share : (first + len(groups)) * share]
            total, square = meet(ids, active, total, square, groups, target_weight)
        scale = lax.rsqrt(square / features + 1e-06)
        update = scale * (0.25 * wide[0] + 0.75 * total)
        hidden = (own.astype(jnp.float32) + update).astype(jnp.bfloat16)
    values = jnp.dot(hidden, head_weight, preferred_element_type=jnp.float32)

    values = values.reshape(micro, tokens, values.shape[1])
    last = sections - 1
    share_rows = reward.shape[1]
    mine = values[:, last * share_rows :]
    for other in range(last):
        part = values[:, other * share_rows : (other + 1) * share_rows]
        part = send(part, route=(last, other), radix=1, stride=1, step=0)
        mine = jnp.where(section == other, part, mine)
    for (radix, _), name in zip(digits, names):
        told = jnp.broadcast_to(mine[None], (radix,) + mine.shape)
        mine = jnp.sum(lax.all_to_all(told, name, split_axis=0, concat_axis=0, tiled=True), axis=0)
    best = jnp.max(mine, axis=2)
    bin_ids = lax.broadcasted_iota(jnp.int32, mine.shape, 2)
    taken = jnp.sum(jnp.where(bin_ids == action_bin[:, :, None], mine, 0.0), axis=2)
    return (reward + 0.98 * best, taken)


def solution(mesh):
    sections, tp = mesh.shape["section"], mesh.shape["tp"]
    digits = digits_of(tp, 4)
    names = tuple(f"tp{number}" for number in range(len(digits)))
    cut = jax.sharding.Mesh(
        mesh.devices.reshape([sections] + [radix for radix, _ in digits]), ("section",) + names
    )
    in_specs = (
        P(None, None, names),
        P("section", None, names),
        P("section", names, None),
        P(names, None),
        P(None, "section"),
        P(None, "section"),
    )
    out_specs = (P(None, "section"), P(None, "section"))
    body = functools.partial(per_device, sections=sections, digits=digits, names=names)
    return jax.shard_map(body, mesh=cut, in_specs=in_specs, out_specs=out_specs, check_vma=False)
```

```python
import functools

import jax
import jax.numpy as jnp
from jax import lax
from jax.experimental import pallas as pl
from jax.experimental.pallas import tpu as pltpu
from jax.sharding import PartitionSpec as P


def digits_of(size, most):
    radices = []
    left = size
    while left > 1:
        radix = next((r for r in range(min(most, left), 1, -1) if left % r == 0), None)
        if radix is None:
            radix = next(r for r in range(2, left + 1) if left % r == 0)
        radices.insert(0, radix)
        left //= radix
    strides = []
    stride = size
    for radix in radices:
        stride //= radix
        strides.append(stride)
    return list(zip(radices, strides))


def peer(digit, step, radix):
    if radix & (radix - 1) == 0:
        return digit ^ step
    return (digit + step) % radix


def exchange(value, axes, tp, route, radix, stride, step):
    pairs = []
    for t in range(tp):
        digit = t // stride % radix
        other = t + (peer(digit, step, radix) - digit) * stride
        pairs.append((route[0] * tp + t, route[1] * tp + other))
    return lax.ppermute(value, axes, pairs)


def relative(digits, position):
    found = [position]
    for radix, stride in digits:
        digit = position // stride % radix
        found = [
            one + (peer(digit, step, radix) - digit) * stride for step in range(radix) for one in found
        ]
    return found


def spread_kernel(where, x, weight, *outs):
    share, _, width = outs[0].shape
    count = share * len(outs)

    @pl.when(where[count] != 0)
    def _():
        for j in range(count):
            columns = pl.ds(pl.multiple_of(where[j] * width, width), width)
            part = jnp.dot(x[...], weight[0, :, columns], preferred_element_type=jnp.float32)
            outs[j // share][j % share] = part.astype(outs[0].dtype)


def first_spread_kernel(where, x, weight, *rest, groups):
    outs, (held, x_here, arrived, x_arrived) = rest[:groups], rest[groups:]
    share, _, width = outs[0].shape
    count = share * groups
    copies = [pltpu.make_async_copy(x, x_here, x_arrived)]
    for j in range(count):
        columns = pl.ds(pl.multiple_of(where[j] * width, width), width)
        copies.append(pltpu.make_async_copy(weight.at[0, :, columns], held.at[0, :, columns], arrived.at[j]))
    for copy in copies:
        copy.start()
    copies[0].wait()

    @pl.when(where[count] != 0)
    def _():
        for j in range(count):
            copies[1 + j].wait()
            columns = pl.ds(pl.multiple_of(where[j] * width, width), width)
            part = jnp.dot(x_here[...], held[0, :, columns], preferred_element_type=jnp.float32)
            outs[j // share][j % share] = part.astype(outs[0].dtype)

    @pl.when(where[count] == 0)
    def _():
        for j in range(count):
            copies[1 + j].wait()


def spread(where, active, x, weight, groups, first):
    rows, _ = x.shape
    count = len(where)
    width = weight.shape[2] // count
    share = count // groups
    vmem = pl.BlockSpec(memory_space=pltpu.VMEM)
    hbm = pl.BlockSpec(memory_space=pltpu.HBM)
    smem = pl.BlockSpec(memory_space=pltpu.SMEM)
    outs = [jax.ShapeDtypeStruct((share, rows, width), jnp.bfloat16)] * groups
    where = jnp.stack(where + [active])
    if not first:
        return pl.pallas_call(
            spread_kernel,
            out_shape=outs,
            in_specs=[smem, vmem, vmem],
            out_specs=[vmem] * groups,
            compiler_params=pltpu.CompilerParams(vmem_limit_bytes=8 * 2**20),
            name="spread",
        )(where, x, weight), weight
    *outs, held = pl.pallas_call(
        functools.partial(first_spread_kernel, groups=groups),
        out_shape=outs + [pltpu.VMEM(weight.shape, weight.dtype)],
        in_specs=[smem, hbm, hbm],
        out_specs=[vmem] * (groups + 1),
        scratch_shapes=[
            pltpu.VMEM(x.shape, x.dtype),
            pltpu.SemaphoreType.DMA((count,)),
            pltpu.SemaphoreType.DMA,
        ],
        compiler_params=pltpu.CompilerParams(vmem_limit_bytes=8 * 2**20),
        name="first_spread",
    )(
        where,
        pltpu.with_memory_space_constraint(x, pltpu.HBM),
        pltpu.with_memory_space_constraint(weight, pltpu.HBM),
    )
    return outs, held


def bring_kernel(wanted, weight, held, token, arrived):
    chunks = arrived.shape[0]
    depth = weight.shape[1] // chunks
    token[...] = jnp.zeros_like(token)

    @pl.when(wanted[0] != 0)
    def _():
        copies = []
        for j in range(chunks):
            rows = pl.ds(j * depth, depth)
            copies.append(pltpu.make_async_copy(weight.at[0, rows, :], held.at[0, rows, :], arrived.at[j]))
        for copy in copies:
            copy.start()
        for copy in copies:
            copy.wait()


def bring(wanted, weight, chunks):
    return pl.pallas_call(
        bring_kernel,
        out_shape=[pltpu.VMEM(weight.shape, weight.dtype), jax.ShapeDtypeStruct((8, 128), jnp.float32)],
        in_specs=[pl.BlockSpec(memory_space=pltpu.SMEM), pl.BlockSpec(memory_space=pltpu.HBM)],
        out_specs=[pl.BlockSpec(memory_space=pltpu.VMEM)] * 2,
        scratch_shapes=[pltpu.SemaphoreType.DMA((chunks,))],
        compiler_params=pltpu.CompilerParams(vmem_limit_bytes=8 * 2**20),
        name="bring",
    )(wanted, pltpu.with_memory_space_constraint(weight, pltpu.HBM))


def meet_kernel(where, total_in, square_in, weight, *rest):
    blocks, (total, square) = rest[:-2], rest[-2:]
    share, _, depth = blocks[0].shape
    count = share * len(blocks)

    @pl.when(where[count] != 0)
    def _():
        sum_of = total_in[...]
        squares = square_in[...]
        for j in range(count):
            x = blocks[j // share][j % share]
            wide = x.astype(jnp.float32)
            squares = squares + jnp.sum(wide * wide, axis=1, keepdims=True)
            rows = pl.ds(pl.multiple_of(where[j] * depth, depth), depth)
            sum_of = sum_of + jnp.dot(x, weight[0, rows, :], preferred_element_type=jnp.float32)
        total[...] = sum_of
        square[...] = squares


def meet(where, active, total, square, blocks, weight):
    vmem = pl.BlockSpec(memory_space=pltpu.VMEM)
    return pl.pallas_call(
        meet_kernel,
        out_shape=[
            jax.ShapeDtypeStruct(total.shape, jnp.float32),
            jax.ShapeDtypeStruct(square.shape, jnp.float32),
        ],
        in_specs=[pl.BlockSpec(memory_space=pltpu.SMEM), vmem, vmem, vmem] + [vmem] * len(blocks),
        out_specs=[vmem, vmem],
        compiler_params=pltpu.CompilerParams(vmem_limit_bytes=8 * 2**20),
        name="meet",
    )(jnp.stack(where + [active]), total, square, weight, *blocks)


def per_device(start_tokens, target_weight, online_weight, head_weight, reward, action_bin, sections, digits, names):
    micro, tokens, width = start_tokens.shape
    tp = 1
    for radix, _ in digits:
        tp *= radix
    everyone = ("section",) + names
    rows = micro * tokens
    features = width * tp
    section = lax.axis_index("section")
    position = lax.axis_index(names)
    where = relative(digits, position)
    rounds = len(digits)
    send = functools.partial(exchange, axes=everyone, tp=tp)
    target_held = pltpu.with_memory_space_constraint(target_weight, pltpu.VMEM)
    hidden = start_tokens.reshape(rows, width)
    for layer in range(sections):
        helper = layer - 1 if layer > 0 else min(1, sections - 1)
        own = hidden
        if layer > 0:
            own = send(hidden, route=(helper, layer), radix=1, stride=1, step=0)
        active = (section == layer).astype(jnp.int32)

        parts, online_weight = spread(where, active, own, online_weight, digits[-1][0], layer == 0)
        stack, mine = (own[None], hidden[None]) if rounds % 2 == 0 else (hidden[None], own[None])
        gathered = [mine]
        for number, (radix, stride) in enumerate(digits):
            route = (helper, layer) if (rounds - number) % 2 == 1 else (layer, helper)
            if number > 0 and helper != layer:
                gathered = [send(stack, route=route, radix=radix, stride=stride, step=0)]
            else:
                gathered = [mine]
            for step in range(1, radix):
                gathered.append(send(stack, route=route, radix=radix, stride=stride, step=step))
            if number < rounds - 1:
                gathered, parts = lax.optimization_barrier((gathered, parts))
                stack = mine = jnp.concatenate(gathered, axis=0)
        at = layer
        for number in range(rounds - 1, -1, -1):
            radix, stride = digits[number]
            to = at if (number + 1) % 2 == 1 and at == layer else (helper if at == layer else layer)
            wide = parts[0] if to == at else send(parts[0], route=(at, to), radix=radix, stride=stride, step=0)
            wide = wide.astype(jnp.float32)
            for step in range(1, radix):
                one = send(parts[step], route=(at, to), radix=radix, stride=stride, step=step)
                wide = wide + one.astype(jnp.float32)
            at = to
            if number > 0:
                following = digits[number - 1][0]
                part = wide.shape[0] // following
                parts = [wide[step * part : (step + 1) * part].astype(jnp.bfloat16) for step in range(following)]
                if layer == 0 and number == 1 and sections > 1:
                    wanted, parts = lax.optimization_barrier(((section > 0).astype(jnp.int32)[None], parts))
                    later_target, token = bring(wanted, target_weight, 4)

        total = jnp.zeros((rows, width), jnp.float32)
        square = jnp.zeros((rows, 1), jnp.float32)
        share = tp // len(gathered)
        half = max(1, len(gathered) // 2)
        for first in range(0, len(gathered), half):
            groups = gathered[first : first + half]
            ids = where[first * share : (first + len(groups)) * share]
            total, square = meet(ids, active, total, square, groups, target_held)
        scale = lax.rsqrt(square / features + 1e-06)
        update = scale * (0.25 * wide[0] + 0.75 * total)
        hidden = (own.astype(jnp.float32) + update).astype(jnp.bfloat16)
        if layer == 0 and sections > 1 and rounds > 1:
            target_held = later_target
            hidden, _ = lax.optimization_barrier((hidden, token))
    values = jnp.dot(hidden, head_weight, preferred_element_type=jnp.float32)

    values = values.reshape(micro, tokens, values.shape[1])
    last = sections - 1
    share_rows = reward.shape[1]
    mine = values[:, last * share_rows :]
    for other in range(last):
        part = values[:, other * share_rows : (other + 1) * share_rows]
        part = send(part, route=(last, other), radix=1, stride=1, step=0)
        mine = jnp.where(section == other, part, mine)
    for (radix, _), name in zip(digits, names):
        told = jnp.broadcast_to(mine[None], (radix,) + mine.shape)
        mine = jnp.sum(lax.all_to_all(told, name, split_axis=0, concat_axis=0, tiled=True), axis=0)
    best = jnp.max(mine, axis=2)
    bin_ids = lax.broadcasted_iota(jnp.int32, mine.shape, 2)
    taken = jnp.sum(jnp.where(bin_ids == action_bin[:, :, None], mine, 0.0), axis=2)
    return (reward + 0.98 * best, taken)


def solution(mesh):
    sections, tp = mesh.shape["section"], mesh.shape["tp"]
    digits = digits_of(tp, 4)
    names = tuple(f"tp{number}" for number in range(len(digits)))
    cut = jax.sharding.Mesh(
        mesh.devices.reshape([sections] + [radix for radix, _ in digits]), ("section",) + names
    )
    in_specs = (
        P(None, None, names),
        P("section", None, names),
        P("section", names, None),
        P(names, None),
        P(None, "section"),
        P(None, "section"),
    )
    out_specs = (P(None, "section"), P(None, "section"))
    body = functools.partial(per_device, sections=sections, digits=digits, names=names)
    return jax.shard_map(body, mesh=cut, in_specs=in_specs, out_specs=out_specs, check_vma=False)
```

```python
import functools

import jax
import jax.numpy as jnp
from jax import lax
from jax.experimental import pallas as pl
from jax.experimental.pallas import tpu as pltpu
from jax.sharding import PartitionSpec as P


def digits_of(size, most):
    radices = []
    left = size
    while left > 1:
        radix = next((r for r in range(min(most, left), 1, -1) if left % r == 0), None)
        if radix is None:
            radix = next(r for r in range(2, left + 1) if left % r == 0)
        radices.insert(0, radix)
        left //= radix
    strides = []
    stride = size
    for radix in radices:
        stride //= radix
        strides.append(stride)
    return list(zip(radices, strides))


def peer(digit, step, radix):
    if radix & (radix - 1) == 0:
        return digit ^ step
    return (digit + step) % radix


def exchange(value, axes, tp, route, radix, stride, step):
    pairs = []
    for t in range(tp):
        digit = t // stride % radix
        other = t + (peer(digit, step, radix) - digit) * stride
        pairs.append((route[0] * tp + t, route[1] * tp + other))
    return lax.ppermute(value, axes, pairs)


def relative(digits, position):
    found = [position]
    for radix, stride in digits:
        digit = position // stride % radix
        found = [
            one + (peer(digit, step, radix) - digit) * stride for step in range(radix) for one in found
        ]
    return found


def spread_kernel(where, x, weight, *outs):
    share, _, width = outs[0].shape
    count = share * len(outs)

    @pl.when(where[count] != 0)
    def _():
        for j in range(count):
            columns = pl.ds(pl.multiple_of(where[j] * width, width), width)
            part = jnp.dot(x[...], weight[0, :, columns], preferred_element_type=jnp.float32)
            outs[j // share][j % share] = part.astype(outs[0].dtype)


def first_spread_kernel(where, x, weight, *rest, ahead):
    outs, (x_here, held, arrived, x_arrived) = rest[:-4], rest[-4:]
    share, _, width = outs[0].shape
    count = share * len(outs)

    def copy_of(j):
        columns = pl.ds(pl.multiple_of(where[j] * width, width), width)
        return pltpu.make_async_copy(weight.at[0, :, columns], held.at[j], arrived.at[j])

    @pl.when(where[count] != 0)
    def _():
        x_copy = pltpu.make_async_copy(x, x_here, x_arrived)
        x_copy.start()
        for j in range(min(ahead, count)):
            copy_of(j).start()
        x_copy.wait()
        for j in range(count):
            copy_of(j).wait()
            if j + ahead < count:
                copy_of(j + ahead).start()
            part = jnp.dot(x_here[...], held[j], preferred_element_type=jnp.float32)
            outs[j // share][j % share] = part.astype(outs[0].dtype)


def spread(where, active, x, weight, groups, first):
    rows, _ = x.shape
    count = len(where)
    width = weight.shape[2] // count
    share = count // groups
    vmem = pl.BlockSpec(memory_space=pltpu.VMEM)
    hbm = pl.BlockSpec(memory_space=pltpu.HBM)
    smem = pl.BlockSpec(memory_space=pltpu.SMEM)
    outs = [jax.ShapeDtypeStruct((share, rows, width), jnp.bfloat16)] * groups
    where = jnp.stack(where + [active])
    if not first:
        return pl.pallas_call(
            spread_kernel,
            out_shape=outs,
            in_specs=[smem, vmem, vmem],
            out_specs=[vmem] * groups,
            compiler_params=pltpu.CompilerParams(vmem_limit_bytes=8 * 2**20),
            name="spread",
        )(where, x, weight)
    return pl.pallas_call(
        functools.partial(first_spread_kernel, ahead=4),
        out_shape=outs,
        in_specs=[smem, hbm, hbm],
        out_specs=[vmem] * groups,
        scratch_shapes=[
            pltpu.VMEM(x.shape, x.dtype),
            pltpu.VMEM((count, weight.shape[1], width), weight.dtype),
            pltpu.SemaphoreType.DMA((count,)),
            pltpu.SemaphoreType.DMA,
        ],
        compiler_params=pltpu.CompilerParams(vmem_limit_bytes=16 * 2**20),
        name="first_spread",
    )(
        where,
        pltpu.with_memory_space_constraint(x, pltpu.HBM),
        pltpu.with_memory_space_constraint(weight, pltpu.HBM),
    )


def bring_kernel(wanted, *rest):
    count = (len(rest) - 1) // 3
    weights, held, arrived = rest[:count], rest[-count - 1 : -1], rest[-1]
    chunks = arrived.shape[1]

    @pl.when(wanted[0] != 0)
    def _():
        copies = []
        for number, (weight, here) in enumerate(zip(weights, held)):
            depth = weight.shape[1] // chunks
            for j in range(chunks):
                rows = pl.ds(j * depth, depth)
                copies.append(
                    pltpu.make_async_copy(weight.at[0, rows, :], here.at[0, rows, :], arrived.at[number, j])
                )
        for copy in copies:
            copy.start()
        for copy in copies:
            copy.wait()


def bring(wanted, weights, after, chunks=4):
    count = len(weights)
    assert len(after) == count
    anywhere = pl.BlockSpec(memory_space=pl.ANY)
    return pl.pallas_call(
        bring_kernel,
        out_shape=[pltpu.VMEM(weight.shape, weight.dtype) for weight in weights],
        in_specs=[pl.BlockSpec(memory_space=pltpu.SMEM)]
        + [pl.BlockSpec(memory_space=pltpu.HBM)] * count
        + [anywhere] * count,
        out_specs=[pl.BlockSpec(memory_space=pltpu.VMEM)] * count,
        scratch_shapes=[pltpu.SemaphoreType.DMA((count, chunks))],
        compiler_params=pltpu.CompilerParams(vmem_limit_bytes=8 * 2**20),
        name="bring",
    )(wanted, *[pltpu.with_memory_space_constraint(weight, pltpu.HBM) for weight in weights], *after)


def meet_kernel(where, total_in, square_in, weight, *rest):
    blocks, (total, square) = rest[:-2], rest[-2:]
    share, _, depth = blocks[0].shape
    count = share * len(blocks)

    @pl.when(where[count] != 0)
    def _():
        sum_of = total_in[...]
        squares = square_in[...]
        for j in range(count):
            x = blocks[j // share][j % share]
            wide = x.astype(jnp.float32)
            squares = squares + jnp.sum(wide * wide, axis=1, keepdims=True)
            rows = pl.ds(pl.multiple_of(where[j] * depth, depth), depth)
            sum_of = sum_of + jnp.dot(x, weight[0, rows, :], preferred_element_type=jnp.float32)
        total[...] = sum_of
        square[...] = squares


def meet(where, active, total, square, blocks, weight):
    vmem = pl.BlockSpec(memory_space=pltpu.VMEM)
    return pl.pallas_call(
        meet_kernel,
        out_shape=[
            jax.ShapeDtypeStruct(total.shape, jnp.float32),
            jax.ShapeDtypeStruct(square.shape, jnp.float32),
        ],
        in_specs=[pl.BlockSpec(memory_space=pltpu.SMEM), vmem, vmem, vmem] + [vmem] * len(blocks),
        out_specs=[vmem, vmem],
        compiler_params=pltpu.CompilerParams(vmem_limit_bytes=8 * 2**20),
        name="meet",
    )(jnp.stack(where + [active]), total, square, weight, *blocks)


def per_device(start_tokens, target_weight, online_weight, head_weight, reward, action_bin, sections, digits, names):
    micro, tokens, width = start_tokens.shape
    tp = 1
    for radix, _ in digits:
        tp *= radix
    everyone = ("section",) + names
    rows = micro * tokens
    features = width * tp
    section = lax.axis_index("section")
    position = lax.axis_index(names)
    where = relative(digits, position)
    rounds = len(digits)
    send = functools.partial(exchange, axes=everyone, tp=tp)
    target_held = pltpu.with_memory_space_constraint(target_weight, pltpu.VMEM)
    hidden = start_tokens.reshape(rows, width)
    for layer in range(sections):
        helper = layer - 1 if layer > 0 else min(1, sections - 1)
        own = hidden
        if layer > 0:
            own = send(hidden, route=(helper, layer), radix=1, stride=1, step=0)
        active = (section == layer).astype(jnp.int32)

        stack, mine = (own[None], hidden[None]) if rounds % 2 == 0 else (hidden[None], own[None])
        gathered = [mine]
        for number, (radix, stride) in enumerate(digits):
            route = (helper, layer) if (rounds - number) % 2 == 1 else (layer, helper)
            if number > 0 and helper != layer:
                gathered = [send(stack, route=route, radix=radix, stride=stride, step=0)]
            else:
                gathered = [mine]
            for step in range(1, radix):
                gathered.append(send(stack, route=route, radix=radix, stride=stride, step=step))
            if number < rounds - 1:
                stack = mine = jnp.concatenate(gathered, axis=0)
        parts = spread(where, active, own, online_weight, digits[-1][0], layer == 0)
        gathered[0], gathered[1], parts = lax.optimization_barrier((gathered[0], gathered[1], parts))
        at = layer
        for number in range(rounds - 1, -1, -1):
            radix, stride = digits[number]
            to = at if (number + 1) % 2 == 1 and at == layer else (helper if at == layer else layer)
            got = []
            for step in range(radix - 1, -1, -1):
                if step == 0 and to == at:
                    got.append(parts[0])
                else:
                    got.append(send(parts[step], route=(at, to), radix=radix, stride=stride, step=step))
            wide = functools.reduce(jnp.add, [one.astype(jnp.float32) for one in got])
            at = to
            if number > 0:
                following = digits[number - 1][0]
                part = wide.shape[0] // following
                parts = [wide[step * part : (step + 1) * part].astype(jnp.bfloat16) for step in range(following)]

        total = jnp.zeros((rows, width), jnp.float32)
        square = jnp.zeros((rows, 1), jnp.float32)
        share = tp // len(gathered)
        half = max(1, len(gathered) // 2)
        for first in range(0, len(gathered), half):
            groups = gathered[first : first + half]
            ids = where[first * share : (first + len(groups)) * share]
            total, square = meet(ids, active, total, square, groups, target_held)
        scale = lax.rsqrt(square / features + 1e-06)
        update = scale * (0.25 * wide[0] + 0.75 * total)
        hidden = (own.astype(jnp.float32) + update).astype(jnp.bfloat16)
        if layer == 0 and sections > 1:
            wanted = (section > 0).astype(jnp.int32)[None]
            held = bring(wanted, [online_weight, target_weight], got[:2])
            hidden, online_weight, target_held = lax.optimization_barrier((hidden, *held))
    values = jnp.dot(hidden, head_weight, preferred_element_type=jnp.float32)

    values = values.reshape(micro, tokens, values.shape[1])
    last = sections - 1
    share_rows = reward.shape[1]
    mine = values[:, last * share_rows :]
    for other in range(last):
        part = values[:, other * share_rows : (other + 1) * share_rows]
        part = send(part, route=(last, other), radix=1, stride=1, step=0)
        mine = jnp.where(section == other, part, mine)
    for (radix, _), name in zip(digits, names):
        told = jnp.broadcast_to(mine[None], (radix,) + mine.shape)
        mine = jnp.sum(lax.all_to_all(told, name, split_axis=0, concat_axis=0, tiled=True), axis=0)
    best = jnp.max(mine, axis=2)
    bin_ids = lax.broadcasted_iota(jnp.int32, mine.shape, 2)
    taken = jnp.sum(jnp.where(bin_ids == action_bin[:, :, None], mine, 0.0), axis=2)
    return (reward + 0.98 * best, taken)


def solution(mesh):
    sections, tp = mesh.shape["section"], mesh.shape["tp"]
    digits = digits_of(tp, 4)
    names = tuple(f"tp{number}" for number in range(len(digits)))
    cut = jax.sharding.Mesh(
        mesh.devices.reshape([sections] + [radix for radix, _ in digits]), ("section",) + names
    )
    in_specs = (
        P(None, None, names),
        P("section", None, names),
        P("section", names, None),
        P(names, None),
        P(None, "section"),
        P(None, "section"),
    )
    out_specs = (P(None, "section"), P(None, "section"))
    body = functools.partial(per_device, sections=sections, digits=digits, names=names)
    return jax.shard_map(body, mesh=cut, in_specs=in_specs, out_specs=out_specs, check_vma=False)
```

```python
import functools

import jax
import jax.numpy as jnp
from jax import lax
from jax.experimental import pallas as pl
from jax.experimental.pallas import tpu as pltpu
from jax.sharding import PartitionSpec as P


def digits_of(size, most):
    radices = []
    left = size
    while left > 1:
        radix = next((r for r in range(min(most, left), 1, -1) if left % r == 0), None)
        if radix is None:
            radix = next(r for r in range(2, left + 1) if left % r == 0)
        radices.insert(0, radix)
        left //= radix
    strides = []
    stride = size
    for radix in radices:
        stride //= radix
        strides.append(stride)
    return list(zip(radices, strides))


def peer(digit, step, radix):
    if radix & (radix - 1) == 0:
        return digit ^ step
    return (digit + step) % radix


def exchange(value, axes, tp, route, radix, stride, step):
    pairs = []
    for t in range(tp):
        digit = t // stride % radix
        other = t + (peer(digit, step, radix) - digit) * stride
        pairs.append((route[0] * tp + t, route[1] * tp + other))
    return lax.ppermute(value, axes, pairs)


def block_of(steps, digits, names):
    index = 0
    for step, (radix, stride), name in zip(steps, digits, names):
        index = index + peer(lax.axis_index(name), step, radix) * stride
    return index


def relative(digits):
    found = [()]
    for radix, _ in digits:
        found = [one + (step,) for step in range(radix) for one in found]
    return found


def spread_kernel(x, weight, *outs, layer, digits, names):
    share, _, width = outs[0].shape

    @pl.when(lax.axis_index("section") == layer)
    def _():
        for j, steps in enumerate(relative(digits)):
            start = pl.multiple_of(block_of(steps, digits, names) * width, width)
            part = jnp.dot(x[...], weight[0, :, pl.ds(start, width)], preferred_element_type=jnp.float32)
            outs[j // share][j % share] = part.astype(outs[0].dtype)


def spread(x, weight, layer, digits, names):
    rows, _ = x.shape
    count = len(relative(digits))
    groups = digits[-1][0]
    width = weight.shape[2] // count
    vmem = pl.BlockSpec(memory_space=pltpu.VMEM)
    return pl.pallas_call(
        functools.partial(spread_kernel, layer=layer, digits=digits, names=names),
        out_shape=[jax.ShapeDtypeStruct((count // groups, rows, width), jnp.bfloat16)] * groups,
        in_specs=[vmem, vmem],
        out_specs=[vmem] * groups,
        compiler_params=pltpu.CompilerParams(vmem_limit_bytes=8 * 2**20),
        name="spread",
    )(x, weight)


def meet_kernel(weight, *rest, blocks, first, layer, digits, names):
    given, (total, square) = rest[:-2], rest[-2:]
    inputs, before = given[:blocks], given[blocks:]
    share, _, depth = inputs[0].shape
    inside = lax.axis_index("section") == layer

    @pl.when(inside)
    def _():
        sum_of = before[0][...] if before else jnp.zeros(total.shape, jnp.float32)
        squares = before[1][...] if before else jnp.zeros(square.shape, jnp.float32)
        for j, steps in enumerate(relative(digits)[first : first + share * blocks]):
            x = inputs[j // share][j % share]
            wide = x.astype(jnp.float32)
            squares = squares + jnp.sum(wide * wide, axis=1, keepdims=True)
            start = pl.multiple_of(block_of(steps, digits, names) * depth, depth)
            sum_of = sum_of + jnp.dot(x, weight[0, pl.ds(start, depth), :], preferred_element_type=jnp.float32)
        total[...] = sum_of
        square[...] = squares

    @pl.when(jnp.logical_not(inside))
    def _():
        total[...] = jnp.zeros_like(total)
        square[...] = jnp.zeros_like(square)


def meet(weight, groups, first, before, layer, digits, names):
    rows = groups[0].shape[1]
    vmem = pl.BlockSpec(memory_space=pltpu.VMEM)
    return pl.pallas_call(
        functools.partial(
            meet_kernel, blocks=len(groups), first=first, layer=layer, digits=digits, names=names
        ),
        out_shape=[
            jax.ShapeDtypeStruct((rows, weight.shape[2]), jnp.float32),
            jax.ShapeDtypeStruct((rows, 1), jnp.float32),
        ],
        in_specs=[vmem] * (1 + len(groups) + len(before)),
        out_specs=[vmem, vmem],
        compiler_params=pltpu.CompilerParams(vmem_limit_bytes=8 * 2**20),
        name="meet",
    )(weight, *groups, *before)


def per_device(start_tokens, target_weight, online_weight, head_weight, reward, action_bin, sections, digits, names):
    micro, tokens, width = start_tokens.shape
    tp = 1
    for radix, _ in digits:
        tp *= radix
    everyone = ("section",) + names
    rows = micro * tokens
    features = width * tp
    rounds = len(digits)
    send = functools.partial(exchange, axes=everyone, tp=tp)
    online_weight = pltpu.with_memory_space_constraint(online_weight, pltpu.VMEM)
    target_weight = pltpu.with_memory_space_constraint(target_weight, pltpu.VMEM)
    hidden = start_tokens.reshape(rows, width)
    for layer in range(sections):
        place = dict(layer=layer, digits=digits, names=names)
        helper = layer - 1 if layer > 0 else min(1, sections - 1)
        own = hidden
        if layer > 0:
            own = send(hidden, route=(helper, layer), radix=1, stride=1, step=0)

        stack, mine = (own[None], hidden[None]) if rounds % 2 == 0 else (hidden[None], own[None])
        gathered = [mine]
        for number, (radix, stride) in enumerate(digits):
            route = (helper, layer) if (rounds - number) % 2 == 1 else (layer, helper)
            if number > 0 and helper != layer:
                gathered = [send(stack, route=route, radix=radix, stride=stride, step=0)]
            else:
                gathered = [mine]
            for step in range(1, radix):
                gathered.append(send(stack, route=route, radix=radix, stride=stride, step=step))
            if number < rounds - 1:
                stack = mine = jnp.concatenate(gathered, axis=0)
        parts = spread(own, online_weight, **place)
        gathered[0], gathered[1], parts = lax.optimization_barrier((gathered[0], gathered[1], parts))
        at = layer
        for number in range(rounds - 1, -1, -1):
            radix, stride = digits[number]
            to = at if (number + 1) % 2 == 1 and at == layer else (helper if at == layer else layer)
            wide = 0.0
            for step in range(radix - 1, -1, -1):
                one = parts[step]
                if step > 0 or to != at:
                    one = send(one, route=(at, to), radix=radix, stride=stride, step=step)
                wide = wide + one.astype(jnp.float32)
            at = to
            if number > 0:
                following = digits[number - 1][0]
                part = wide.shape[0] // following
                parts = [wide[step * part : (step + 1) * part].astype(jnp.bfloat16) for step in range(following)]

        before = []
        half = max(1, len(gathered) // 2)
        for first in range(0, len(gathered), half):
            groups = gathered[first : first + half]
            before = meet(target_weight, groups, first * groups[0].shape[0], before, **place)
        total, square = before
        update = lax.rsqrt(square / features + 1e-06) * (0.25 * wide[0] + 0.75 * total)
        hidden = (own.astype(jnp.float32) + update).astype(jnp.bfloat16)

    values = jnp.dot(hidden, head_weight, preferred_element_type=jnp.float32)
    values = values.reshape(micro, tokens, values.shape[1])
    last = sections - 1
    share_rows = reward.shape[1]
    mine = values[:, last * share_rows :]
    for other in range(last):
        part = values[:, other * share_rows : (other + 1) * share_rows]
        mine = mine + send(part, route=(last, other), radix=1, stride=1, step=0)
    for (radix, _), name in zip(digits, names):
        told = jnp.broadcast_to(mine[None], (radix,) + mine.shape)
        mine = jnp.sum(lax.all_to_all(told, name, split_axis=0, concat_axis=0, tiled=True), axis=0)
    best = jnp.max(mine, axis=2)
    bin_ids = lax.broadcasted_iota(jnp.int32, mine.shape, 2)
    taken = jnp.sum(jnp.where(bin_ids == action_bin[:, :, None], mine, 0.0), axis=2)
    return (reward + 0.98 * best, taken)


def solution(mesh):
    sections, tp = mesh.shape["section"], mesh.shape["tp"]
    digits = digits_of(tp, 4)
    names = tuple(f"tp{number}" for number in range(len(digits)))
    cut = jax.sharding.Mesh(
        mesh.devices.reshape([sections] + [radix for radix, _ in digits]), ("section",) + names
    )
    in_specs = (
        P(None, None, names),
        P("section", None, names),
        P("section", names, None),
        P(names, None),
        P(None, "section"),
        P(None, "section"),
    )
    out_specs = (P(None, "section"), P(None, "section"))
    body = functools.partial(per_device, sections=sections, digits=digits, names=names)
    return jax.shard_map(body, mesh=cut, in_specs=in_specs, out_specs=out_specs, check_vma=False)
```

```python
import functools

import jax
import jax.numpy as jnp
from jax import lax
from jax.experimental import pallas as pl
from jax.experimental.pallas import tpu as pltpu
from jax.sharding import PartitionSpec as P


def digits_of(size, most):
    radices = []
    left = size
    while left > 1:
        radix = next((r for r in range(min(most, left), 1, -1) if left % r == 0), None)
        if radix is None:
            radix = next(r for r in range(2, left + 1) if left % r == 0)
        radices.insert(0, radix)
        left //= radix
    strides = []
    stride = size
    for radix in radices:
        stride //= radix
        strides.append(stride)
    return list(zip(radices, strides))


def peer(digit, step, radix):
    if radix & (radix - 1) == 0:
        return digit ^ step
    return (digit + step) % radix


def exchange(value, axes, tp, route, radix, stride, step):
    pairs = []
    for t in range(tp):
        digit = t // stride % radix
        other = t + (peer(digit, step, radix) - digit) * stride
        pairs.append((route[0] * tp + t, route[1] * tp + other))
    return lax.ppermute(value, axes, pairs)


def block_of(steps, digits, names):
    index = 0
    for step, (radix, stride), name in zip(steps, digits, names):
        index = index + peer(lax.axis_index(name), step, radix) * stride
    return index


def relative(digits):
    found = [()]
    for radix, _ in digits:
        found = [one + (step,) for step in range(radix) for one in found]
    return found


def spread_kernel(x, weight, *outs, layer, digits, names):
    share, _, width = outs[0].shape

    @pl.when(lax.axis_index("section") == layer)
    def _():
        for j, steps in enumerate(relative(digits)):
            start = pl.multiple_of(block_of(steps, digits, names) * width, width)
            part = jnp.dot(x[...], weight[0, :, pl.ds(start, width)], preferred_element_type=jnp.float32)
            outs[j // share][j % share] = part.astype(outs[0].dtype)


def spread(x, weight, layer, digits, names):
    rows, _ = x.shape
    count = len(relative(digits))
    groups = digits[-1][0]
    width = weight.shape[2] // count
    vmem = pl.BlockSpec(memory_space=pltpu.VMEM)
    return pl.pallas_call(
        functools.partial(spread_kernel, layer=layer, digits=digits, names=names),
        out_shape=[jax.ShapeDtypeStruct((count // groups, rows, width), jnp.bfloat16)] * groups,
        in_specs=[vmem, vmem],
        out_specs=[vmem] * groups,
        compiler_params=pltpu.CompilerParams(vmem_limit_bytes=8 * 2**20),
        name="spread",
    )(x, weight)


def meet_kernel(weight, *rest, blocks, first, layer, digits, names):
    given, (total, square) = rest[:-2], rest[-2:]
    inputs, before = given[:blocks], given[blocks:]
    share, _, depth = inputs[0].shape
    inside = lax.axis_index("section") == layer

    @pl.when(inside)
    def _():
        sum_of = before[0][...] if before else jnp.zeros(total.shape, jnp.float32)
        squares = before[1][...] if before else jnp.zeros(square.shape, jnp.float32)
        for j, steps in enumerate(relative(digits)[first : first + share * blocks]):
            x = inputs[j // share][j % share]
            wide = x.astype(jnp.float32)
            squares = squares + jnp.sum(wide * wide, axis=1, keepdims=True)
            start = pl.multiple_of(block_of(steps, digits, names) * depth, depth)
            sum_of = sum_of + jnp.dot(x, weight[0, pl.ds(start, depth), :], preferred_element_type=jnp.float32)
        total[...] = sum_of
        square[...] = squares

    @pl.when(jnp.logical_not(inside))
    def _():
        total[...] = jnp.zeros_like(total)
        square[...] = jnp.zeros_like(square)


def meet(weight, groups, first, before, layer, digits, names):
    rows = groups[0].shape[1]
    vmem = pl.BlockSpec(memory_space=pltpu.VMEM)
    return pl.pallas_call(
        functools.partial(
            meet_kernel, blocks=len(groups), first=first, layer=layer, digits=digits, names=names
        ),
        out_shape=[
            jax.ShapeDtypeStruct((rows, weight.shape[2]), jnp.float32),
            jax.ShapeDtypeStruct((rows, 1), jnp.float32),
        ],
        in_specs=[vmem] * (1 + len(groups) + len(before)),
        out_specs=[vmem, vmem],
        compiler_params=pltpu.CompilerParams(vmem_limit_bytes=8 * 2**20),
        name="meet",
    )(weight, *groups, *before)


def per_device(start_tokens, target_weight, online_weight, head_weight, reward, action_bin, sections, digits, names):
    micro, tokens, width = start_tokens.shape
    tp = 1
    for radix, _ in digits:
        tp *= radix
    everyone = ("section",) + names
    rows = micro * tokens
    features = width * tp
    rounds = len(digits)
    send = functools.partial(exchange, axes=everyone, tp=tp)
    online_weight = pltpu.with_memory_space_constraint(online_weight, pltpu.VMEM)
    target_weight = pltpu.with_memory_space_constraint(target_weight, pltpu.VMEM)
    hidden = start_tokens.reshape(rows, width)
    for layer in range(sections):
        place = dict(layer=layer, digits=digits, names=names)
        helper = layer - 1 if layer > 0 else min(1, sections - 1)
        own = hidden
        if layer > 0:
            own = send(hidden, route=(helper, layer), radix=1, stride=1, step=0)

        parts = spread(own, online_weight, **place)
        stack, mine = (own[None], hidden[None]) if rounds % 2 == 0 else (hidden[None], own[None])
        gathered = [mine]
        for number, (radix, stride) in enumerate(digits):
            route = (helper, layer) if (rounds - number) % 2 == 1 else (layer, helper)
            if number > 0 and helper != layer:
                gathered = [send(stack, route=route, radix=radix, stride=stride, step=0)]
            else:
                gathered = [mine]
            for step in range(1, radix):
                gathered.append(send(stack, route=route, radix=radix, stride=stride, step=step))
            if number < rounds - 1:
                gathered, parts = lax.optimization_barrier((gathered, parts))
                stack = mine = jnp.concatenate(gathered, axis=0)
        at = layer
        for number in range(rounds - 1, -1, -1):
            radix, stride = digits[number]
            to = at if (number + 1) % 2 == 1 and at == layer else (helper if at == layer else layer)
            wide = 0.0
            for step in range(radix - 1, -1, -1):
                one = parts[step]
                if step > 0 or to != at:
                    one = send(one, route=(at, to), radix=radix, stride=stride, step=step)
                wide = wide + one.astype(jnp.float32)
            at = to
            if number > 0:
                following = digits[number - 1][0]
                part = wide.shape[0] // following
                parts = [wide[step * part : (step + 1) * part].astype(jnp.bfloat16) for step in range(following)]

        before = []
        half = max(1, len(gathered) // 2)
        for first in range(0, len(gathered), half):
            groups = gathered[first : first + half]
            before = meet(target_weight, groups, first * groups[0].shape[0], before, **place)
        total, square = before
        update = lax.rsqrt(square / features + 1e-06) * (0.25 * wide[0] + 0.75 * total)
        hidden = (own.astype(jnp.float32) + update).astype(jnp.bfloat16)

    values = jnp.dot(hidden, head_weight, preferred_element_type=jnp.float32)
    values = values.reshape(micro, tokens, values.shape[1])
    last = sections - 1
    share_rows = reward.shape[1]
    mine = values[:, last * share_rows :]
    for other in range(last):
        part = values[:, other * share_rows : (other + 1) * share_rows]
        mine = mine + send(part, route=(last, other), radix=1, stride=1, step=0)
    told = jnp.broadcast_to(mine.astype(jnp.bfloat16)[None], (tp,) + mine.shape)
    told = lax.all_to_all(told, names, split_axis=0, concat_axis=0, tiled=True)
    mine = jnp.sum(told.astype(jnp.float32), axis=0)
    best = jnp.max(mine, axis=2)
    bin_ids = lax.broadcasted_iota(jnp.int32, mine.shape, 2)
    taken = jnp.sum(jnp.where(bin_ids == action_bin[:, :, None], mine, 0.0), axis=2)
    return (reward + 0.98 * best, taken)


def solution(mesh):
    sections, tp = mesh.shape["section"], mesh.shape["tp"]
    digits = digits_of(tp, 4)
    names = tuple(f"tp{number}" for number in range(len(digits)))
    cut = jax.sharding.Mesh(
        mesh.devices.reshape([sections] + [radix for radix, _ in digits]), ("section",) + names
    )
    in_specs = (
        P(None, None, names),
        P("section", None, names),
        P("section", names, None),
        P(names, None),
        P(None, "section"),
        P(None, "section"),
    )
    out_specs = (P(None, "section"), P(None, "section"))
    body = functools.partial(per_device, sections=sections, digits=digits, names=names)
    return jax.shard_map(body, mesh=cut, in_specs=in_specs, out_specs=out_specs, check_vma=False)
```

```python
import functools

import jax
import jax.numpy as jnp
from jax import lax
from jax.experimental import pallas as pl
from jax.experimental.pallas import tpu as pltpu
from jax.sharding import PartitionSpec as P


def digits_of(size, most):
    radices = []
    left = size
    while left > 1:
        radix = next((r for r in range(min(most, left), 1, -1) if left % r == 0), None)
        if radix is None:
            radix = next(r for r in range(2, left + 1) if left % r == 0)
        radices.insert(0, radix)
        left //= radix
    strides = []
    stride = size
    for radix in radices:
        stride //= radix
        strides.append(stride)
    return list(zip(radices, strides))


def peer(digit, step, radix):
    if radix & (radix - 1) == 0:
        return digit ^ step
    return (digit + step) % radix


def exchange(value, axes, tp, route, radix, stride, step):
    pairs = []
    for t in range(tp):
        digit = t // stride % radix
        other = t + (peer(digit, step, radix) - digit) * stride
        pairs.append((route[0] * tp + t, route[1] * tp + other))
    return lax.ppermute(value, axes, pairs)


def block_of(steps, digits, names):
    index = 0
    for step, (radix, stride), name in zip(steps, digits, names):
        index = index + peer(lax.axis_index(name), step, radix) * stride
    return index


def relative(digits):
    found = [()]
    for radix, _ in digits:
        found = [one + (step,) for step in range(radix) for one in found]
    return found


def spread_kernel(x, weight, *outs, first, layer, digits, names):
    share, _, width = outs[0].shape

    @pl.when(lax.axis_index("section") == layer)
    def _():
        for j, steps in enumerate(relative(digits)[first : first + share * len(outs)]):
            start = pl.multiple_of(block_of(steps, digits, names) * width, width)
            part = jnp.dot(x[...], weight[0, :, pl.ds(start, width)], preferred_element_type=jnp.float32)
            outs[j // share][j % share] = part.astype(outs[0].dtype)


def spread(x, weight, first, groups, layer, digits, names):
    rows, _ = x.shape
    count = len(relative(digits))
    share = count // digits[-1][0]
    width = weight.shape[2] // count
    vmem = pl.BlockSpec(memory_space=pltpu.VMEM)
    return pl.pallas_call(
        functools.partial(spread_kernel, first=first * share, layer=layer, digits=digits, names=names),
        out_shape=[jax.ShapeDtypeStruct((share, rows, width), jnp.bfloat16)] * groups,
        in_specs=[vmem, vmem],
        out_specs=[vmem] * groups,
        compiler_params=pltpu.CompilerParams(vmem_limit_bytes=8 * 2**20),
        name="spread",
    )(x, weight)


def meet_kernel(weight, *rest, layer, digits, names):
    inputs, (total, square) = rest[:-2], rest[-2:]
    share, _, depth = inputs[0].shape
    inside = lax.axis_index("section") == layer

    @pl.when(inside)
    def _():
        sum_of = jnp.zeros(total.shape, jnp.float32)
        squares = jnp.zeros(square.shape, jnp.float32)
        for j, steps in enumerate(relative(digits)):
            x = inputs[j // share][j % share]
            wide = x.astype(jnp.float32)
            squares = squares + jnp.sum(wide * wide, axis=1, keepdims=True)
            start = pl.multiple_of(block_of(steps, digits, names) * depth, depth)
            sum_of = sum_of + jnp.dot(x, weight[0, pl.ds(start, depth), :], preferred_element_type=jnp.float32)
        total[...] = sum_of
        square[...] = squares

    @pl.when(jnp.logical_not(inside))
    def _():
        total[...] = jnp.zeros_like(total)
        square[...] = jnp.zeros_like(square)


def meet(weight, groups, layer, digits, names):
    rows = groups[0].shape[1]
    vmem = pl.BlockSpec(memory_space=pltpu.VMEM)
    return pl.pallas_call(
        functools.partial(meet_kernel, layer=layer, digits=digits, names=names),
        out_shape=[
            jax.ShapeDtypeStruct((rows, weight.shape[2]), jnp.float32),
            jax.ShapeDtypeStruct((rows, 1), jnp.float32),
        ],
        in_specs=[vmem] * (1 + len(groups)),
        out_specs=[vmem, vmem],
        compiler_params=pltpu.CompilerParams(vmem_limit_bytes=8 * 2**20),
        name="meet",
    )(weight, *groups)


def per_device(start_tokens, target_weight, online_weight, head_weight, reward, action_bin, sections, digits, names):
    micro, tokens, width = start_tokens.shape
    tp = 1
    for radix, _ in digits:
        tp *= radix
    everyone = ("section",) + names
    rows = micro * tokens
    features = width * tp
    rounds = len(digits)
    send = functools.partial(exchange, axes=everyone, tp=tp)
    online_weight = pltpu.with_memory_space_constraint(online_weight, pltpu.VMEM)
    target_weight = pltpu.with_memory_space_constraint(target_weight, pltpu.VMEM)
    hidden = start_tokens.reshape(rows, width)
    for layer in range(sections):
        place = dict(layer=layer, digits=digits, names=names)
        helper = layer - 1 if layer > 0 else min(1, sections - 1)
        own = hidden
        if layer > 0:
            own = send(hidden, route=(helper, layer), radix=1, stride=1, step=0)

        inner = digits[-1][0]
        half = inner // 2
        near = spread(own, online_weight, 0, half, **place) if half else []
        parts = near + spread(own, online_weight, half, inner - half, **place)
        stack, mine = (own[None], hidden[None]) if rounds % 2 == 0 else (hidden[None], own[None])
        gathered = [mine]
        for number, (radix, stride) in enumerate(digits):
            route = (helper, layer) if (rounds - number) % 2 == 1 else (layer, helper)
            if number > 0 and helper != layer:
                gathered = [send(stack, route=route, radix=radix, stride=stride, step=0)]
            else:
                gathered = [mine]
            far = [send(stack, route=route, radix=radix, stride=stride, step=step) for step in range(radix - 1, 0, -1)]
            gathered += far[::-1]
            if number < rounds - 1:
                gathered, parts = lax.optimization_barrier((gathered, parts))
                stack = mine = jnp.concatenate(gathered, axis=0)
        at = layer
        for number in range(rounds - 1, -1, -1):
            radix, stride = digits[number]
            to = at if (number + 1) % 2 == 1 and at == layer else (helper if at == layer else layer)
            wide = 0.0
            for step in range(radix - 1, -1, -1):
                one = parts[step]
                if step > 0 or to != at:
                    one = send(one, route=(at, to), radix=radix, stride=stride, step=step)
                wide = wide + one.astype(jnp.float32)
            at = to
            if number > 0:
                following = digits[number - 1][0]
                part = wide.shape[0] // following
                parts = [wide[step * part : (step + 1) * part].astype(jnp.bfloat16) for step in range(following)]

        total, square = meet(target_weight, gathered, **place)
        update = lax.rsqrt(square / features + 1e-06) * (0.25 * wide[0] + 0.75 * total)
        hidden = (own.astype(jnp.float32) + update).astype(jnp.bfloat16)

    values = jnp.dot(hidden, head_weight, preferred_element_type=jnp.float32)
    values = values.reshape(micro, tokens, values.shape[1])
    last = sections - 1
    share_rows = reward.shape[1]
    mine = values[:, last * share_rows :]
    for other in range(last):
        part = values[:, other * share_rows : (other + 1) * share_rows]
        mine = mine + send(part, route=(last, other), radix=1, stride=1, step=0)
    told = jnp.broadcast_to(mine.astype(jnp.bfloat16)[None], (tp,) + mine.shape)
    told = lax.all_to_all(told, names, split_axis=0, concat_axis=0, tiled=True)
    mine = jnp.sum(told.astype(jnp.float32), axis=0)
    best = jnp.max(mine, axis=2)
    bin_ids = lax.broadcasted_iota(jnp.int32, mine.shape, 2)
    taken = jnp.sum(jnp.where(bin_ids == action_bin[:, :, None], mine, 0.0), axis=2)
    return (reward + 0.98 * best, taken)


def solution(mesh):
    sections, tp = mesh.shape["section"], mesh.shape["tp"]
    digits = digits_of(tp, 4)
    names = tuple(f"tp{number}" for number in range(len(digits)))
    cut = jax.sharding.Mesh(
        mesh.devices.reshape([sections] + [radix for radix, _ in digits]), ("section",) + names
    )
    in_specs = (
        P(None, None, names),
        P("section", None, names),
        P("section", names, None),
        P(names, None),
        P(None, "section"),
        P(None, "section"),
    )
    out_specs = (P(None, "section"), P(None, "section"))
    body = functools.partial(per_device, sections=sections, digits=digits, names=names)
    return jax.shard_map(body, mesh=cut, in_specs=in_specs, out_specs=out_specs, check_vma=False)
```

```python
import functools

import jax
import jax.numpy as jnp
from jax import lax
from jax.experimental import pallas as pl
from jax.experimental.pallas import tpu as pltpu
from jax.sharding import PartitionSpec as P


def digits_of(size, most):
    radices = []
    left = size
    while left > 1:
        radix = next((r for r in range(min(most, left), 1, -1) if left % r == 0), None)
        if radix is None:
            radix = next(r for r in range(2, left + 1) if left % r == 0)
        radices.insert(0, radix)
        left //= radix
    strides = []
    stride = size
    for radix in radices:
        stride //= radix
        strides.append(stride)
    return list(zip(radices, strides))


def peer(digit, step, radix):
    if radix & (radix - 1) == 0:
        return digit ^ step
    return (digit + step) % radix


def exchange(value, axes, tp, route, radix, stride, step):
    pairs = []
    for t in range(tp):
        digit = t // stride % radix
        other = t + (peer(digit, step, radix) - digit) * stride
        pairs.append((route[0] * tp + t, route[1] * tp + other))
    return lax.ppermute(value, axes, pairs)


def block_of(steps, digits, names):
    index = 0
    for step, (radix, stride), name in zip(steps, digits, names):
        index = index + peer(lax.axis_index(name), step, radix) * stride
    return index


def order(radix):
    return range(radix - 1, -1, -1)


def relative(digits):
    found = [()]
    for radix, _ in digits:
        found = [one + (step,) for step in order(radix) for one in found]
    return found


def spread_kernel(x, weight, *rest, outputs, first, layer, digits, names):
    outs, scratch = rest[:outputs], rest[outputs:]
    share, _, width = outs[0].shape
    wanted = relative(digits)[first : first + share * outputs]

    @pl.when(lax.axis_index("section") == layer)
    def _():
        here, copies = x, []
        if scratch:
            here, held, x_arrived, arrived = scratch
            copies.append(pltpu.make_async_copy(x, here, x_arrived))
        blocks = []
        for j, steps in enumerate(wanted):
            start = pl.multiple_of(block_of(steps, digits, names) * width, width)
            blocks.append(weight.at[0, :, pl.ds(start, width)])
            if scratch:
                copies.append(pltpu.make_async_copy(blocks[j], held.at[j], arrived.at[j]))
                blocks[j] = held.at[j]
        for copy in copies:
            copy.start()
        if scratch:
            copies[0].wait()
        for j, block in enumerate(blocks):
            if scratch:
                copies[1 + j].wait()
            part = jnp.dot(here[...], block[...], preferred_element_type=jnp.float32)
            outs[j // share][j % share] = part.astype(outs[0].dtype)


def spread(x, weight, first, groups, layer, digits, names):
    rows, depth = x.shape
    count = len(relative(digits))
    share = count // digits[-1][0]
    width = weight.shape[2] // count
    vmem = pl.BlockSpec(memory_space=pltpu.VMEM)
    place = pltpu.HBM if layer == 0 else pltpu.VMEM
    scratch = [
        pltpu.VMEM(x.shape, x.dtype),
        pltpu.VMEM((groups * share, depth, width), weight.dtype),
        pltpu.SemaphoreType.DMA,
        pltpu.SemaphoreType.DMA((groups * share,)),
    ]
    return pl.pallas_call(
        functools.partial(
            spread_kernel, outputs=groups, first=first * share, layer=layer, digits=digits, names=names
        ),
        out_shape=[jax.ShapeDtypeStruct((share, rows, width), jnp.bfloat16)] * groups,
        in_specs=[pl.BlockSpec(memory_space=place)] * 2,
        out_specs=[vmem] * groups,
        scratch_shapes=scratch if layer == 0 else [],
        compiler_params=pltpu.CompilerParams(vmem_limit_bytes=8 * 2**20),
        name="spread",
    )(
        pltpu.with_memory_space_constraint(x, place) if layer == 0 else x,
        pltpu.with_memory_space_constraint(weight, place),
    )


def meet_kernel(weight, *rest, first, blocks, layer, digits, names):
    given, (total, square) = rest[:-2], rest[-2:]
    inputs, before = given[:blocks], given[blocks:]
    share, _, depth = inputs[0].shape
    inside = lax.axis_index("section") == layer

    @pl.when(inside)
    def _():
        sum_of = before[0][...] if before else jnp.zeros(total.shape, jnp.float32)
        squares = before[1][...] if before else jnp.zeros(square.shape, jnp.float32)
        for j, steps in enumerate(relative(digits)[first : first + share * blocks]):
            x = inputs[j // share][j % share]
            wide = x.astype(jnp.float32)
            squares = squares + jnp.sum(wide * wide, axis=1, keepdims=True)
            start = pl.multiple_of(block_of(steps, digits, names) * depth, depth)
            sum_of = sum_of + jnp.dot(x, weight[0, pl.ds(start, depth), :], preferred_element_type=jnp.float32)
        total[...] = sum_of
        square[...] = squares

    @pl.when(jnp.logical_not(inside))
    def _():
        total[...] = jnp.zeros_like(total)
        square[...] = jnp.zeros_like(square)


def meet(weight, groups, first, before, layer, digits, names):
    rows = groups[0].shape[1]
    vmem = pl.BlockSpec(memory_space=pltpu.VMEM)
    return pl.pallas_call(
        functools.partial(
            meet_kernel, first=first, blocks=len(groups), layer=layer, digits=digits, names=names
        ),
        out_shape=[
            jax.ShapeDtypeStruct((rows, weight.shape[2]), jnp.float32),
            jax.ShapeDtypeStruct((rows, 1), jnp.float32),
        ],
        in_specs=[vmem] * (1 + len(groups) + len(before)),
        out_specs=[vmem, vmem],
        compiler_params=pltpu.CompilerParams(vmem_limit_bytes=8 * 2**20),
        name="meet",
    )(weight, *groups, *before)


def per_device(start_tokens, target_weight, online_weight, head_weight, reward, action_bin, sections, digits, names):
    micro, tokens, width = start_tokens.shape
    tp = 1
    for radix, _ in digits:
        tp *= radix
    everyone = ("section",) + names
    rows = micro * tokens
    features = width * tp
    rounds = len(digits)
    send = functools.partial(exchange, axes=everyone, tp=tp)
    target_weight = pltpu.with_memory_space_constraint(target_weight, pltpu.VMEM)
    hidden = start_tokens.reshape(rows, width)
    for layer in range(sections):
        place = dict(layer=layer, digits=digits, names=names)
        helper = layer - 1 if layer > 0 else min(1, sections - 1)
        own = hidden
        if layer > 0:
            own = send(hidden, route=(helper, layer), radix=1, stride=1, step=0)

        inner = digits[-1][0]
        half = inner // 2
        parts = list(spread(own, online_weight, 0, half, **place)) if half else []
        parts += spread(own, online_weight, half, inner - half, **place)
        stack, mine = (own[None], hidden[None]) if rounds % 2 == 0 else (hidden[None], own[None])
        gathered = [mine]
        for number, (radix, stride) in enumerate(digits):
            route = (helper, layer) if (rounds - number) % 2 == 1 else (layer, helper)
            gathered = []
            for step in order(radix):
                if step == 0 and (number == 0 or helper == layer):
                    gathered.append(mine)
                else:
                    gathered.append(send(stack, route=route, radix=radix, stride=stride, step=step))
            if number < rounds - 1:
                gathered, parts[half:] = lax.optimization_barrier((gathered, parts[half:]))
                stack = mine = jnp.concatenate(gathered, axis=0)
        at = layer
        for number in range(rounds - 1, -1, -1):
            radix, stride = digits[number]
            to = at if (number + 1) % 2 == 1 and at == layer else (helper if at == layer else layer)
            wide = 0.0
            for step, one in zip(order(radix), parts):
                if step > 0 or to != at:
                    one = send(one, route=(at, to), radix=radix, stride=stride, step=step)
                wide = wide + one.astype(jnp.float32)
            at = to
            if number > 0:
                following = digits[number - 1][0]
                part = wide.shape[0] // following
                parts = [wide[i * part : (i + 1) * part].astype(jnp.bfloat16) for i in range(following)]

        before = []
        for begin in range(0, len(gathered), max(1, half)):
            groups = gathered[begin : begin + max(1, half)]
            before = meet(target_weight, groups, begin * groups[0].shape[0], before, **place)
        total, square = before
        update = lax.rsqrt(square / features + 1e-06) * (0.25 * wide[0] + 0.75 * total)
        hidden = (own.astype(jnp.float32) + update).astype(jnp.bfloat16)

    values = jnp.dot(hidden, head_weight, preferred_element_type=jnp.float32)
    values = values.reshape(micro, tokens, values.shape[1])
    last = sections - 1
    share_rows = reward.shape[1]
    mine = values[:, last * share_rows :]
    for other in range(last):
        part = values[:, other * share_rows : (other + 1) * share_rows]
        mine = mine + send(part, route=(last, other), radix=1, stride=1, step=0)
    told = jnp.broadcast_to(mine.astype(jnp.bfloat16)[None], (tp,) + mine.shape)
    told = lax.all_to_all(told, names, split_axis=0, concat_axis=0, tiled=True)
    mine = jnp.sum(told.astype(jnp.float32), axis=0)
    best = jnp.max(mine, axis=2)
    bin_ids = lax.broadcasted_iota(jnp.int32, mine.shape, 2)
    taken = jnp.sum(jnp.where(bin_ids == action_bin[:, :, None], mine, 0.0), axis=2)
    return (reward + 0.98 * best, taken)


def solution(mesh):
    sections, tp = mesh.shape["section"], mesh.shape["tp"]
    digits = digits_of(tp, 4)
    names = tuple(f"tp{number}" for number in range(len(digits)))
    cut = jax.sharding.Mesh(
        mesh.devices.reshape([sections] + [radix for radix, _ in digits]), ("section",) + names
    )
    in_specs = (
        P(None, None, names),
        P("section", None, names),
        P("section", names, None),
        P(names, None),
        P(None, "section"),
        P(None, "section"),
    )
    out_specs = (P(None, "section"), P(None, "section"))
    body = functools.partial(per_device, sections=sections, digits=digits, names=names)
    return jax.shard_map(body, mesh=cut, in_specs=in_specs, out_specs=out_specs, check_vma=False)
```

```python
import functools

import jax
import jax.numpy as jnp
from jax import lax
from jax.experimental import pallas as pl
from jax.experimental.pallas import tpu as pltpu
from jax.sharding import PartitionSpec as P


def digits_of(size, most):
    radices = []
    left = size
    while left > 1:
        radix = next((r for r in range(min(most, left), 1, -1) if left % r == 0), None)
        if radix is None:
            radix = next(r for r in range(2, left + 1) if left % r == 0)
        radices.insert(0, radix)
        left //= radix
    strides = []
    stride = size
    for radix in radices:
        stride //= radix
        strides.append(stride)
    return list(zip(radices, strides))


def peer(digit, step, radix):
    if radix & (radix - 1) == 0:
        return digit ^ step
    return (digit + step) % radix


def exchange(value, axes, tp, route, radix, stride, step):
    pairs = []
    for t in range(tp):
        digit = t // stride % radix
        other = t + (peer(digit, step, radix) - digit) * stride
        pairs.append((route[0] * tp + t, route[1] * tp + other))
    return lax.ppermute(value, axes, pairs)


def block_of(steps, digits, names):
    index = 0
    for step, (radix, stride), name in zip(steps, digits, names):
        index = index + peer(lax.axis_index(name), step, radix) * stride
    return index


def gather_steps(radix, last):
    half = radix // 2 if last else 0
    return [*range(half, radix), *range(half)]


def scatter_steps(radix, last):
    return [*range(radix - 1, -1, -1)] if last else [radix - 1, *range(radix - 1)]


def relative(digits, steps_of):
    found = [()]
    for number, (radix, _) in enumerate(digits):
        found = [one + (step,) for step in steps_of(radix, number == len(digits) - 1) for one in found]
    return found


def spread_kernel(x, weight, *rest, outputs, first, layer, digits, names):
    outs, scratch = rest[:outputs], rest[outputs:]
    share, _, width = outs[0].shape
    wanted = relative(digits, scatter_steps)[first : first + share * outputs]

    @pl.when(lax.axis_index("section") == layer)
    def _():
        here, copies = x, []
        if scratch:
            here, held, x_arrived, arrived = scratch
            copies.append(pltpu.make_async_copy(x, here, x_arrived))
        blocks = []
        for j, steps in enumerate(wanted):
            start = pl.multiple_of(block_of(steps, digits, names) * width, width)
            blocks.append(weight.at[0, :, pl.ds(start, width)])
            if scratch:
                copies.append(pltpu.make_async_copy(blocks[j], held.at[j], arrived.at[j]))
                blocks[j] = held.at[j]
        for copy in copies:
            copy.start()
        if scratch:
            copies[0].wait()
        for j, block in enumerate(blocks):
            if scratch:
                copies[1 + j].wait()
            part = jnp.dot(here[...], block[...], preferred_element_type=jnp.float32)
            outs[j // share][j % share] = part.astype(outs[0].dtype)


def spread(x, weight, first, groups, layer, digits, names):
    rows, depth = x.shape
    count = len(relative(digits, scatter_steps))
    share = count // digits[-1][0]
    width = weight.shape[2] // count
    vmem = pl.BlockSpec(memory_space=pltpu.VMEM)
    place = pltpu.HBM if layer == 0 else pltpu.VMEM
    outs = [jax.ShapeDtypeStruct((share, rows, width), jnp.bfloat16)] * groups
    if layer == 0:
        outs.append(jax.ShapeDtypeStruct(x.shape, x.dtype))
    scratch = [
        pltpu.VMEM((groups * share, depth, width), weight.dtype),
        pltpu.SemaphoreType.DMA,
        pltpu.SemaphoreType.DMA((groups * share,)),
    ]
    return pl.pallas_call(
        functools.partial(
            spread_kernel, outputs=groups, first=first * share, layer=layer, digits=digits, names=names
        ),
        out_shape=outs,
        in_specs=[pl.BlockSpec(memory_space=place)] * 2,
        out_specs=[vmem] * len(outs),
        scratch_shapes=scratch if layer == 0 else [],
        compiler_params=pltpu.CompilerParams(vmem_limit_bytes=16 * 2**20),
        name="spread",
    )(
        pltpu.with_memory_space_constraint(x, place) if layer == 0 else x,
        pltpu.with_memory_space_constraint(weight, place),
    )


def meet_kernel(weight, *rest, first, blocks, given, layer, digits, names):
    inputs, before, (total, square), scratch = (
        rest[:blocks],
        rest[blocks:given],
        rest[given : given + 2],
        rest[given + 2 :],
    )
    share, _, depth = inputs[0].shape
    inside = lax.axis_index("section") == layer

    @pl.when(inside)
    def _():
        rows_of, copies = [], []
        for j, steps in enumerate(relative(digits, gather_steps)[first : first + share * blocks]):
            start = pl.multiple_of(block_of(steps, digits, names) * depth, depth)
            rows_of.append(weight.at[0, pl.ds(start, depth), :])
            if scratch:
                held, arrived = scratch
                copies.append(pltpu.make_async_copy(rows_of[j], held.at[j], arrived.at[j]))
                copies[j].start()
                rows_of[j] = held.at[j]
        sum_of = before[0][...] if before else jnp.zeros(total.shape, jnp.float32)
        squares = before[1][...] if before else jnp.zeros(square.shape, jnp.float32)
        for j in range(share * blocks):
            x = inputs[j // share][j % share]
            wide = x.astype(jnp.float32)
            squares = squares + jnp.sum(wide * wide, axis=1, keepdims=True)
            if copies:
                copies[j].wait()
            sum_of = sum_of + jnp.dot(x, rows_of[j][...], preferred_element_type=jnp.float32)
        total[...] = sum_of
        square[...] = squares

    @pl.when(jnp.logical_not(inside))
    def _():
        total[...] = jnp.zeros_like(total)
        square[...] = jnp.zeros_like(square)


def meet(weight, groups, first, before, layer, digits, names):
    share, rows, depth = groups[0].shape
    count = share * len(groups)
    vmem = pl.BlockSpec(memory_space=pltpu.VMEM)
    place = pltpu.HBM if layer == 0 else pltpu.VMEM
    scratch = [pltpu.VMEM((count, depth, weight.shape[2]), weight.dtype), pltpu.SemaphoreType.DMA((count,))]
    return pl.pallas_call(
        functools.partial(
            meet_kernel,
            first=first,
            blocks=len(groups),
            given=len(groups) + len(before),
            layer=layer,
            digits=digits,
            names=names,
        ),
        out_shape=[
            jax.ShapeDtypeStruct((rows, weight.shape[2]), jnp.float32),
            jax.ShapeDtypeStruct((rows, 1), jnp.float32),
        ],
        in_specs=[pl.BlockSpec(memory_space=place)] + [vmem] * (len(groups) + len(before)),
        out_specs=[vmem, vmem],
        scratch_shapes=scratch if layer == 0 else [],
        compiler_params=pltpu.CompilerParams(vmem_limit_bytes=16 * 2**20),
        name="meet",
    )(pltpu.with_memory_space_constraint(weight, place), *groups, *before)


def per_device(start_tokens, target_weight, online_weight, head_weight, reward, action_bin, sections, digits, names):
    micro, tokens, width = start_tokens.shape
    tp = 1
    for radix, _ in digits:
        tp *= radix
    everyone = ("section",) + names
    rows = micro * tokens
    features = width * tp
    rounds = len(digits)
    send = functools.partial(exchange, axes=everyone, tp=tp)
    hidden = start_tokens.reshape(rows, width)
    for layer in range(sections):
        place = dict(layer=layer, digits=digits, names=names)
        helper = layer - 1 if layer > 0 else min(1, sections - 1)
        own = hidden
        if layer > 0:
            own = send(hidden, route=(helper, layer), radix=1, stride=1, step=0)

        inner = digits[-1][0]
        half = inner // 2
        if layer == 0:
            *parts, first = spread(own, online_weight, 0, inner, **place)
            own = first if rounds % 2 == 0 else own
        else:
            parts = list(spread(own, online_weight, 0, half, **place)) if half else []
            parts += spread(own, online_weight, half, inner - half, **place)
        stack, mine = (own[None], hidden[None]) if rounds % 2 == 0 else (hidden[None], own[None])
        gathered = [mine]
        for number, (radix, stride) in enumerate(digits):
            route = (helper, layer) if (rounds - number) % 2 == 1 else (layer, helper)
            gathered = []
            for step in gather_steps(radix, number == rounds - 1):
                if step == 0 and (number == 0 or helper == layer):
                    gathered.append(mine)
                else:
                    gathered.append(send(stack, route=route, radix=radix, stride=stride, step=step))
            if number < rounds - 1:
                gathered, parts[half:] = lax.optimization_barrier((gathered, parts[half:]))
                stack = mine = jnp.concatenate(gathered, axis=0)
        at = layer
        for number in range(rounds - 1, -1, -1):
            radix, stride = digits[number]
            to = at if (number + 1) % 2 == 1 and at == layer else (helper if at == layer else layer)
            wide = 0.0
            for step, one in zip(scatter_steps(radix, number == rounds - 1), parts):
                if step > 0 or to != at:
                    one = send(one, route=(at, to), radix=radix, stride=stride, step=step)
                wide = wide + one.astype(jnp.float32)
            at = to
            if number > 0:
                following = digits[number - 1][0]
                part = wide.shape[0] // following
                parts = [wide[i * part : (i + 1) * part].astype(jnp.bfloat16) for i in range(following)]

        before = []
        for begin in range(0, len(gathered), max(1, half)):
            groups = gathered[begin : begin + max(1, half)]
            before = meet(target_weight, groups, begin * groups[0].shape[0], before, **place)
        total, square = before
        update = lax.rsqrt(square / features + 1e-06) * (0.25 * wide[0] + 0.75 * total)
        hidden = (own.astype(jnp.float32) + update).astype(jnp.bfloat16)

    values = jnp.dot(hidden, head_weight, preferred_element_type=jnp.float32)
    values = values.reshape(micro, tokens, values.shape[1])
    last = sections - 1
    share_rows = reward.shape[1]
    mine = values[:, last * share_rows :]
    for other in range(last):
        part = values[:, other * share_rows : (other + 1) * share_rows]
        mine = mine + send(part, route=(last, other), radix=1, stride=1, step=0)
    told = jnp.broadcast_to(mine.astype(jnp.bfloat16)[None], (tp,) + mine.shape)
    told = lax.all_to_all(told, names, split_axis=0, concat_axis=0, tiled=True)
    mine = jnp.sum(told.astype(jnp.float32), axis=0)
    best = jnp.max(mine, axis=2)
    bin_ids = lax.broadcasted_iota(jnp.int32, mine.shape, 2)
    taken = jnp.sum(jnp.where(bin_ids == action_bin[:, :, None], mine, 0.0), axis=2)
    return (reward + 0.98 * best, taken)


def solution(mesh):
    sections, tp = mesh.shape["section"], mesh.shape["tp"]
    digits = digits_of(tp, 4)
    names = tuple(f"tp{number}" for number in range(len(digits)))
    cut = jax.sharding.Mesh(
        mesh.devices.reshape([sections] + [radix for radix, _ in digits]), ("section",) + names
    )
    in_specs = (
        P(None, None, names),
        P("section", None, names),
        P("section", names, None),
        P(names, None),
        P(None, "section"),
        P(None, "section"),
    )
    out_specs = (P(None, "section"), P(None, "section"))
    body = functools.partial(per_device, sections=sections, digits=digits, names=names)
    return jax.shard_map(body, mesh=cut, in_specs=in_specs, out_specs=out_specs, check_vma=False)
```

```python
import functools

import jax
import jax.numpy as jnp
from jax import lax
from jax.experimental import pallas as pl
from jax.experimental.pallas import tpu as pltpu
from jax.sharding import PartitionSpec as P


def digits_of(size, most):
    radices = []
    left = size
    while left > 1:
        radix = next((r for r in range(min(most, left), 1, -1) if left % r == 0), None)
        if radix is None:
            radix = next(r for r in range(2, left + 1) if left % r == 0)
        radices.insert(0, radix)
        left //= radix
    strides = []
    stride = size
    for radix in radices:
        stride //= radix
        strides.append(stride)
    return list(zip(radices, strides))


def peer(digit, step, radix):
    if radix & (radix - 1) == 0:
        return digit ^ step
    return (digit + step) % radix


def exchange(value, axes, tp, route, radix, stride, step):
    pairs = []
    for t in range(tp):
        digit = t // stride % radix
        other = t + (peer(digit, step, radix) - digit) * stride
        pairs.append((route[0] * tp + t, route[1] * tp + other))
    return lax.ppermute(value, axes, pairs)


def block_of(steps, digits, names):
    index = 0
    for step, (radix, stride), name in zip(steps, digits, names):
        index = index + peer(lax.axis_index(name), step, radix) * stride
    return index


def gather_steps(radix, last):
    return [*range(radix - 1, -1, -1)]


def scatter_steps(radix, last):
    half = radix // 2 if last else 0
    return [*range(radix - 1, half - 1, -1), *range(half)]


def relative(digits, steps_of):
    found = [()]
    for number, (radix, _) in enumerate(digits):
        found = [one + (step,) for step in steps_of(radix, number == len(digits) - 1) for one in found]
    return found


def spread_kernel(x, weight, *outs, first, layer, digits, names):
    share, _, width = outs[0].shape

    @pl.when(lax.axis_index("section") == layer)
    def _():
        for j, steps in enumerate(relative(digits, scatter_steps)[first : first + share * len(outs)]):
            start = pl.multiple_of(block_of(steps, digits, names) * width, width)
            part = jnp.dot(x[...], weight[0, :, pl.ds(start, width)], preferred_element_type=jnp.float32)
            outs[j // share][j % share] = part.astype(outs[0].dtype)


def first_spread_kernel(x, weight, *rest, outputs, layer, digits, names):
    outs, (here, held, total, x_arrived, arrived) = rest[:outputs], rest[outputs:]
    share, _, width = outs[0].shape
    chunks, pieces = arrived.shape
    depth = weight.shape[1] // chunks
    rows = depth // pieces

    @pl.when(lax.axis_index("section") == layer)
    def _():
        x_copy = pltpu.make_async_copy(x, here, x_arrived)
        x_copy.start()
        copies = []
        for chunk in range(chunks):
            for piece in range(pieces):
                these = pl.ds(chunk * depth + piece * rows, rows)
                copies.append(
                    pltpu.make_async_copy(weight.at[0, these, :], held.at[these, :], arrived.at[chunk, piece])
                )
                copies[-1].start()
        x_copy.wait()
        for chunk in range(chunks):
            for piece in range(pieces):
                copies[chunk * pieces + piece].wait()
            those = slice(chunk * depth, (chunk + 1) * depth)
            for j, steps in enumerate(relative(digits, scatter_steps)):
                start = pl.multiple_of(block_of(steps, digits, names) * width, width)
                part = jnp.dot(here[:, those], held[those, pl.ds(start, width)], preferred_element_type=jnp.float32)
                if chunk > 0:
                    part = part + total[j]
                if chunk < chunks - 1:
                    total[j] = part
                else:
                    outs[j // share][j % share] = part.astype(outs[0].dtype)


def spread(x, weight, first, groups, layer, digits, names):
    rows, depth = x.shape
    count = len(relative(digits, scatter_steps))
    share = count // digits[-1][0]
    width = weight.shape[2] // count
    vmem = pl.BlockSpec(memory_space=pltpu.VMEM)
    outs = [jax.ShapeDtypeStruct((share, rows, width), jnp.bfloat16)] * groups
    if layer > 0:
        return pl.pallas_call(
            functools.partial(spread_kernel, first=first * share, layer=layer, digits=digits, names=names),
            out_shape=outs,
            in_specs=[vmem, vmem],
            out_specs=[vmem] * groups,
            compiler_params=pltpu.CompilerParams(vmem_limit_bytes=8 * 2**20),
            name="spread",
        )(x, pltpu.with_memory_space_constraint(weight, pltpu.VMEM))
    chunks = 2 if depth % 256 == 0 else 1
    return pl.pallas_call(
        functools.partial(first_spread_kernel, outputs=groups, layer=layer, digits=digits, names=names),
        out_shape=outs,
        in_specs=[pl.BlockSpec(memory_space=pltpu.HBM)] * 2,
        out_specs=[vmem] * groups,
        scratch_shapes=[
            pltpu.VMEM(x.shape, x.dtype),
            pltpu.VMEM(weight.shape[1:], weight.dtype),
            pltpu.VMEM((count, rows, width), jnp.float32),
            pltpu.SemaphoreType.DMA,
            pltpu.SemaphoreType.DMA((chunks, 4)),
        ],
        compiler_params=pltpu.CompilerParams(vmem_limit_bytes=20 * 2**20),
        name="first_spread",
    )(
        pltpu.with_memory_space_constraint(x, pltpu.HBM),
        pltpu.with_memory_space_constraint(weight, pltpu.HBM),
    )


def meet_kernel(weight, *rest, first, blocks, given, layer, digits, names):
    inputs, before, (total, square), scratch = (
        rest[:blocks],
        rest[blocks:given],
        rest[given : given + 2],
        rest[given + 2 :],
    )
    share, _, depth = inputs[0].shape
    inside = lax.axis_index("section") == layer

    @pl.when(inside)
    def _():
        rows_of, copies = [], []
        for j, steps in enumerate(relative(digits, gather_steps)[first : first + share * blocks]):
            start = pl.multiple_of(block_of(steps, digits, names) * depth, depth)
            rows_of.append(weight.at[0, pl.ds(start, depth), :])
            if scratch:
                held, arrived = scratch
                copies.append(pltpu.make_async_copy(rows_of[j], held.at[j], arrived.at[j]))
                copies[j].start()
                rows_of[j] = held.at[j]
        sum_of = before[0][...] if before else jnp.zeros(total.shape, jnp.float32)
        squares = before[1][...] if before else jnp.zeros(square.shape, jnp.float32)
        for j in range(share * blocks):
            x = inputs[j // share][j % share]
            wide = x.astype(jnp.float32)
            squares = squares + jnp.sum(wide * wide, axis=1, keepdims=True)
            if copies:
                copies[j].wait()
            sum_of = sum_of + jnp.dot(x, rows_of[j][...], preferred_element_type=jnp.float32)
        total[...] = sum_of
        square[...] = squares

    @pl.when(jnp.logical_not(inside))
    def _():
        total[...] = jnp.zeros_like(total)
        square[...] = jnp.zeros_like(square)


def meet(weight, groups, first, before, layer, digits, names):
    share, rows, depth = groups[0].shape
    count = share * len(groups)
    vmem = pl.BlockSpec(memory_space=pltpu.VMEM)
    place = pltpu.HBM if layer == 0 else pltpu.VMEM
    scratch = [pltpu.VMEM((count, depth, weight.shape[2]), weight.dtype), pltpu.SemaphoreType.DMA((count,))]
    return pl.pallas_call(
        functools.partial(
            meet_kernel,
            first=first,
            blocks=len(groups),
            given=len(groups) + len(before),
            layer=layer,
            digits=digits,
            names=names,
        ),
        out_shape=[
            jax.ShapeDtypeStruct((rows, weight.shape[2]), jnp.float32),
            jax.ShapeDtypeStruct((rows, 1), jnp.float32),
        ],
        in_specs=[pl.BlockSpec(memory_space=place)] + [vmem] * (len(groups) + len(before)),
        out_specs=[vmem, vmem],
        scratch_shapes=scratch if layer == 0 else [],
        compiler_params=pltpu.CompilerParams(vmem_limit_bytes=16 * 2**20),
        name="meet",
    )(pltpu.with_memory_space_constraint(weight, place), *groups, *before)


def per_device(start_tokens, target_weight, online_weight, head_weight, reward, action_bin, sections, digits, names):
    micro, tokens, width = start_tokens.shape
    tp = 1
    for radix, _ in digits:
        tp *= radix
    everyone = ("section",) + names
    rows = micro * tokens
    features = width * tp
    rounds = len(digits)
    send = functools.partial(exchange, axes=everyone, tp=tp)
    hidden = start_tokens.reshape(rows, width)
    for layer in range(sections):
        place = dict(layer=layer, digits=digits, names=names)
        helper = layer - 1 if layer > 0 else min(1, sections - 1)
        own = hidden
        if layer > 0:
            own = send(hidden, route=(helper, layer), radix=1, stride=1, step=0)

        inner = digits[-1][0]
        half = inner // 2
        if layer == 0:
            parts = list(spread(own, online_weight, 0, inner, **place))
        else:
            parts = list(spread(own, online_weight, 0, half, **place)) if half else []
            parts += spread(own, online_weight, half, inner - half, **place)
        stack, mine = (own[None], hidden[None]) if rounds % 2 == 0 else (hidden[None], own[None])
        gathered = [mine]
        for number, (radix, stride) in enumerate(digits):
            route = (helper, layer) if (rounds - number) % 2 == 1 else (layer, helper)
            gathered = []
            for step in gather_steps(radix, number == rounds - 1):
                if step == 0 and (number == 0 or helper == layer):
                    gathered.append(mine)
                else:
                    gathered.append(send(stack, route=route, radix=radix, stride=stride, step=step))
            if number < rounds - 1:
                gathered, parts[half:] = lax.optimization_barrier((gathered, parts[half:]))
                stack = mine = jnp.concatenate(gathered, axis=0)
        at = layer
        for number in range(rounds - 1, -1, -1):
            radix, stride = digits[number]
            to = at if (number + 1) % 2 == 1 and at == layer else (helper if at == layer else layer)
            wide = 0.0
            for step, one in zip(scatter_steps(radix, number == rounds - 1), parts):
                if step > 0 or to != at:
                    one = send(one, route=(at, to), radix=radix, stride=stride, step=step)
                wide = wide + one.astype(jnp.float32)
            at = to
            if number > 0:
                following = digits[number - 1][0]
                part = wide.shape[0] // following
                parts = [wide[i * part : (i + 1) * part].astype(jnp.bfloat16) for i in range(following)]

        before = []
        for begin in range(0, len(gathered), max(1, half)):
            groups = gathered[begin : begin + max(1, half)]
            before = meet(target_weight, groups, begin * groups[0].shape[0], before, **place)
        total, square = before
        update = lax.rsqrt(square / features + 1e-06) * (0.25 * wide[0] + 0.75 * total)
        hidden = (own.astype(jnp.float32) + update).astype(jnp.bfloat16)

    values = jnp.dot(hidden, head_weight, preferred_element_type=jnp.float32)
    values = values.reshape(micro, tokens, values.shape[1])
    last = sections - 1
    share_rows = reward.shape[1]
    mine = values[:, last * share_rows :]
    for other in range(last):
        part = values[:, other * share_rows : (other + 1) * share_rows]
        mine = mine + send(part, route=(last, other), radix=1, stride=1, step=0)
    told = jnp.broadcast_to(mine.astype(jnp.bfloat16)[None], (tp,) + mine.shape)
    told = lax.all_to_all(told, names, split_axis=0, concat_axis=0, tiled=True)
    mine = jnp.sum(told.astype(jnp.float32), axis=0)
    best = jnp.max(mine, axis=2)
    bin_ids = lax.broadcasted_iota(jnp.int32, mine.shape, 2)
    taken = jnp.sum(jnp.where(bin_ids == action_bin[:, :, None], mine, 0.0), axis=2)
    return (reward + 0.98 * best, taken)


def solution(mesh):
    sections, tp = mesh.shape["section"], mesh.shape["tp"]
    digits = digits_of(tp, 4)
    names = tuple(f"tp{number}" for number in range(len(digits)))
    cut = jax.sharding.Mesh(
        mesh.devices.reshape([sections] + [radix for radix, _ in digits]), ("section",) + names
    )
    in_specs = (
        P(None, None, names),
        P("section", None, names),
        P("section", names, None),
        P(names, None),
        P(None, "section"),
        P(None, "section"),
    )
    out_specs = (P(None, "section"), P(None, "section"))
    body = functools.partial(per_device, sections=sections, digits=digits, names=names)
    return jax.shard_map(body, mesh=cut, in_specs=in_specs, out_specs=out_specs, check_vma=False)
```

```python
import functools

import jax
import jax.numpy as jnp
from jax import lax
from jax.experimental import pallas as pl
from jax.experimental.pallas import tpu as pltpu
from jax.sharding import PartitionSpec as P


def digits_of(size, most):
    radices = []
    left = size
    while left > 1:
        radix = next((r for r in range(min(most, left), 1, -1) if left % r == 0), None)
        if radix is None:
            radix = next(r for r in range(2, left + 1) if left % r == 0)
        radices.insert(0, radix)
        left //= radix
    strides = []
    stride = size
    for radix in radices:
        stride //= radix
        strides.append(stride)
    return list(zip(radices, strides))


def peer(digit, step, radix):
    if radix & (radix - 1) == 0:
        return digit ^ step
    return (digit + step) % radix


def exchange(value, axes, tp, route, radix, stride, step):
    pairs = []
    for t in range(tp):
        digit = t // stride % radix
        other = t + (peer(digit, step, radix) - digit) * stride
        pairs.append((route[0] * tp + t, route[1] * tp + other))
    return lax.ppermute(value, axes, pairs)


def block_of(steps, digits, names):
    index = 0
    for step, (radix, stride), name in zip(steps, digits, names):
        index = index + peer(lax.axis_index(name), step, radix) * stride
    return index


def gather_steps(radix, last):
    return [*range(radix - 1, -1, -1)]


def scatter_steps(radix, last):
    half = radix // 2 if last else 0
    return [*range(radix - 1, half - 1, -1), *range(half)]


def relative(digits, steps_of):
    found = [()]
    for number, (radix, _) in enumerate(digits):
        found = [one + (step,) for step in steps_of(radix, number == len(digits) - 1) for one in found]
    return found


def spread_kernel(x, weight, *outs, first, layer, digits, names):
    share, _, width = outs[0].shape

    @pl.when(lax.axis_index("section") == layer)
    def _():
        for j, steps in enumerate(relative(digits, scatter_steps)[first : first + share * len(outs)]):
            start = pl.multiple_of(block_of(steps, digits, names) * width, width)
            part = jnp.dot(x[...], weight[0, :, pl.ds(start, width)], preferred_element_type=jnp.float32)
            outs[j // share][j % share] = part.astype(outs[0].dtype)


def first_spread_kernel(x, weight, *rest, outputs, layer, digits, names):
    outs, (here, held, total, x_arrived, arrived) = rest[:outputs], rest[outputs:]
    share, _, width = outs[0].shape
    chunks, pieces = arrived.shape
    depth = weight.shape[1] // chunks
    rows = depth // pieces

    @pl.when(lax.axis_index("section") == layer)
    def _():
        x_copy = pltpu.make_async_copy(x, here, x_arrived)
        x_copy.start()
        copies = []
        for chunk in range(chunks):
            for piece in range(pieces):
                these = pl.ds(chunk * depth + piece * rows, rows)
                copies.append(
                    pltpu.make_async_copy(weight.at[0, these, :], held.at[these, :], arrived.at[chunk, piece])
                )
                copies[-1].start()
        x_copy.wait()
        for chunk in range(chunks):
            for piece in range(pieces):
                copies[chunk * pieces + piece].wait()
            those = slice(chunk * depth, (chunk + 1) * depth)
            for j, steps in enumerate(relative(digits, scatter_steps)):
                start = pl.multiple_of(block_of(steps, digits, names) * width, width)
                part = jnp.dot(here[:, those], held[those, pl.ds(start, width)], preferred_element_type=jnp.float32)
                if chunk > 0:
                    part = part + total[j]
                if chunk < chunks - 1:
                    total[j] = part
                else:
                    outs[j // share][j % share] = part.astype(outs[0].dtype)


def spread(x, weight, first, groups, layer, digits, names):
    rows, depth = x.shape
    count = len(relative(digits, scatter_steps))
    share = count // digits[-1][0]
    width = weight.shape[2] // count
    vmem = pl.BlockSpec(memory_space=pltpu.VMEM)
    outs = [jax.ShapeDtypeStruct((share, rows, width), jnp.bfloat16)] * groups
    if layer > 0:
        return pl.pallas_call(
            functools.partial(spread_kernel, first=first * share, layer=layer, digits=digits, names=names),
            out_shape=outs,
            in_specs=[vmem, vmem],
            out_specs=[vmem] * groups,
            compiler_params=pltpu.CompilerParams(vmem_limit_bytes=8 * 2**20),
            name="spread",
        )(x, pltpu.with_memory_space_constraint(weight, pltpu.VMEM))
    chunks = 2 if depth % 256 == 0 else 1
    return pl.pallas_call(
        functools.partial(first_spread_kernel, outputs=groups, layer=layer, digits=digits, names=names),
        out_shape=outs,
        in_specs=[pl.BlockSpec(memory_space=pltpu.HBM)] * 2,
        out_specs=[vmem] * groups,
        scratch_shapes=[
            pltpu.VMEM(x.shape, x.dtype),
            pltpu.VMEM(weight.shape[1:], weight.dtype),
            pltpu.VMEM((count, rows, width), jnp.float32),
            pltpu.SemaphoreType.DMA,
            pltpu.SemaphoreType.DMA((chunks, 4)),
        ],
        compiler_params=pltpu.CompilerParams(vmem_limit_bytes=20 * 2**20),
        name="first_spread",
    )(
        pltpu.with_memory_space_constraint(x, pltpu.HBM),
        pltpu.with_memory_space_constraint(weight, pltpu.HBM),
    )


def meet_kernel(weight, *rest, first, blocks, layer, digits, names):
    inputs, before, (total, square) = rest[:blocks], rest[blocks:-2], rest[-2:]
    share, _, depth = inputs[0].shape
    inside = lax.axis_index("section") == layer

    @pl.when(inside)
    def _():
        sum_of = before[0][...] if before else jnp.zeros(total.shape, jnp.float32)
        squares = before[1][...] if before else jnp.zeros(square.shape, jnp.float32)
        for j, steps in enumerate(relative(digits, gather_steps)[first : first + share * blocks]):
            x = inputs[j // share][j % share]
            wide = x.astype(jnp.float32)
            squares = squares + jnp.sum(wide * wide, axis=1, keepdims=True)
            start = pl.multiple_of(block_of(steps, digits, names) * depth, depth)
            sum_of = sum_of + jnp.dot(x, weight[0, pl.ds(start, depth), :], preferred_element_type=jnp.float32)
        total[...] = sum_of
        square[...] = squares

    @pl.when(jnp.logical_not(inside))
    def _():
        total[...] = jnp.zeros_like(total)
        square[...] = jnp.zeros_like(square)


def meet(weight, groups, first, before, layer, digits, names):
    rows = groups[0].shape[1]
    vmem = pl.BlockSpec(memory_space=pltpu.VMEM)
    return pl.pallas_call(
        functools.partial(
            meet_kernel, first=first, blocks=len(groups), layer=layer, digits=digits, names=names
        ),
        out_shape=[
            jax.ShapeDtypeStruct((rows, weight.shape[2]), jnp.float32),
            jax.ShapeDtypeStruct((rows, 1), jnp.float32),
        ],
        in_specs=[vmem] * (1 + len(groups) + len(before)),
        out_specs=[vmem, vmem],
        compiler_params=pltpu.CompilerParams(vmem_limit_bytes=8 * 2**20),
        name="meet",
    )(pltpu.with_memory_space_constraint(weight, pltpu.VMEM), *groups, *before)


def tell_kernel(hidden, head, told, *, micro, sections):
    values = jnp.dot(hidden[...], head[...], preferred_element_type=jnp.float32)
    tokens = values.shape[0] // micro
    share = tokens // sections
    repeats = told.shape[0] // sections
    for section in range(sections):
        starts = [m * tokens + section * share for m in range(micro)]
        mine = jnp.concatenate([values[start : start + share] for start in starts], axis=0)
        for i in range(repeats):
            told[section * repeats + i] = mine.astype(told.dtype)


def tell(hidden, head, micro, sections, repeats):
    shape = (sections * repeats, hidden.shape[0] // sections, head.shape[1])
    vmem = pl.BlockSpec(memory_space=pltpu.VMEM)
    return pl.pallas_call(
        functools.partial(tell_kernel, micro=micro, sections=sections),
        out_shape=jax.ShapeDtypeStruct(shape, jnp.bfloat16),
        in_specs=[vmem, vmem],
        out_specs=vmem,
        compiler_params=pltpu.CompilerParams(vmem_limit_bytes=8 * 2**20),
        name="tell",
    )(hidden, head)


def per_device(start_tokens, target_weight, online_weight, head_weight, reward, action_bin, sections, digits, names):
    micro, tokens, width = start_tokens.shape
    tp = 1
    for radix, _ in digits:
        tp *= radix
    everyone = ("section",) + names
    rows = micro * tokens
    features = width * tp
    rounds = len(digits)
    send = functools.partial(exchange, axes=everyone, tp=tp)
    hidden = start_tokens.reshape(rows, width)
    for layer in range(sections):
        place = dict(layer=layer, digits=digits, names=names)
        helper = layer - 1 if layer > 0 else min(1, sections - 1)
        own = hidden
        if layer > 0:
            own = send(hidden, route=(helper, layer), radix=1, stride=1, step=0)

        inner = digits[-1][0]
        half = inner // 2
        if layer == 0:
            parts = list(spread(own, online_weight, 0, inner, **place))
        else:
            parts = list(spread(own, online_weight, 0, half, **place)) if half else []
            parts += spread(own, online_weight, half, inner - half, **place)
        stack, mine = (own[None], hidden[None]) if rounds % 2 == 0 else (hidden[None], own[None])
        gathered = [mine]
        for number, (radix, stride) in enumerate(digits):
            route = (helper, layer) if (rounds - number) % 2 == 1 else (layer, helper)
            gathered = []
            for step in gather_steps(radix, number == rounds - 1):
                if step == 0 and (number == 0 or helper == layer):
                    gathered.append(mine)
                else:
                    gathered.append(send(stack, route=route, radix=radix, stride=stride, step=step))
            if number < rounds - 1:
                gathered, parts[half:] = lax.optimization_barrier((gathered, parts[half:]))
                stack = mine = jnp.concatenate(gathered, axis=0)
        at = layer
        for number in range(rounds - 1, -1, -1):
            radix, stride = digits[number]
            to = at if (number + 1) % 2 == 1 and at == layer else (helper if at == layer else layer)
            wide = 0.0
            for step, one in zip(scatter_steps(radix, number == rounds - 1), parts):
                if step > 0 or to != at:
                    one = send(one, route=(at, to), radix=radix, stride=stride, step=step)
                wide = wide + one.astype(jnp.float32)
            at = to
            if number > 0:
                following = digits[number - 1][0]
                part = wide.shape[0] // following
                parts = [wide[i * part : (i + 1) * part].astype(jnp.bfloat16) for i in range(following)]

        before = []
        for begin in range(0, len(gathered), max(1, half)):
            groups = gathered[begin : begin + max(1, half)]
            before = meet(target_weight, groups, begin * groups[0].shape[0], before, **place)
        total, square = before
        update = lax.rsqrt(square / features + 1e-06) * (0.25 * wide[0] + 0.75 * total)
        hidden = (own.astype(jnp.float32) + update).astype(jnp.bfloat16)

    share_rows = reward.shape[1]
    bins = head_weight.shape[1]
    told = tell(hidden, head_weight, micro, sections, inner)
    told = lax.all_to_all(told, ("section", names[-1]), split_axis=0, concat_axis=0, tiled=True)
    mine = jnp.sum(told[(sections - 1) * inner :].astype(jnp.float32), axis=0)
    for (radix, _), name in zip(digits[:-1], names):
        told = jnp.broadcast_to(mine.astype(jnp.bfloat16)[None], (radix,) + mine.shape)
        told = lax.all_to_all(told, name, split_axis=0, concat_axis=0, tiled=True)
        mine = jnp.sum(told.astype(jnp.float32), axis=0)
    mine = mine.reshape(micro, share_rows, bins)
    best = jnp.max(mine, axis=2)
    bin_ids = lax.broadcasted_iota(jnp.int32, mine.shape, 2)
    taken = jnp.sum(jnp.where(bin_ids == action_bin[:, :, None], mine, 0.0), axis=2)
    return (reward + 0.98 * best, taken)


def solution(mesh):
    sections, tp = mesh.shape["section"], mesh.shape["tp"]
    digits = digits_of(tp, 4)
    names = tuple(f"tp{number}" for number in range(len(digits)))
    cut = jax.sharding.Mesh(
        mesh.devices.reshape([sections] + [radix for radix, _ in digits]), ("section",) + names
    )
    in_specs = (
        P(None, None, names),
        P("section", None, names),
        P("section", names, None),
        P(names, None),
        P(None, "section"),
        P(None, "section"),
    )
    out_specs = (P(None, "section"), P(None, "section"))
    body = functools.partial(per_device, sections=sections, digits=digits, names=names)
    return jax.shard_map(body, mesh=cut, in_specs=in_specs, out_specs=out_specs, check_vma=False)
```

```python
import functools

import jax
import jax.numpy as jnp
from jax import lax
from jax.experimental import pallas as pl
from jax.experimental.pallas import tpu as pltpu
from jax.sharding import PartitionSpec as P


def digits_of(size, most):
    radices = []
    left = size
    while left > 1:
        radix = next((r for r in range(min(most, left), 1, -1) if left % r == 0), None)
        if radix is None:
            radix = next(r for r in range(2, left + 1) if left % r == 0)
        radices.insert(0, radix)
        left //= radix
    strides = []
    stride = size
    for radix in radices:
        stride //= radix
        strides.append(stride)
    return list(zip(radices, strides))


def peer(digit, step, radix):
    if radix & (radix - 1) == 0:
        return digit ^ step
    return (digit + step) % radix


def exchange(value, axes, tp, route, radix, stride, step):
    pairs = []
    for t in range(tp):
        digit = t // stride % radix
        other = t + (peer(digit, step, radix) - digit) * stride
        pairs.append((route[0] * tp + t, route[1] * tp + other))
    return lax.ppermute(value, axes, pairs)


def block_of(steps, digits, names):
    index = 0
    for step, (radix, stride), name in zip(steps, digits, names):
        index = index + peer(lax.axis_index(name), step, radix) * stride
    return index


def gather_steps(radix, last):
    return [*range(radix)] if last else [*range(radix - 1, -1, -1)]


def scatter_steps(radix, last):
    half = radix // 2 if last else 0
    return [*range(radix - 1, half - 1, -1), *range(half)]


def relative(digits, steps_of):
    found = [()]
    for number, (radix, _) in enumerate(digits):
        found = [one + (step,) for step in steps_of(radix, number == len(digits) - 1) for one in found]
    return found


def spread_kernel(x, weight, *outs, first, layer, digits, names):
    share, _, width = outs[0].shape

    @pl.when(lax.axis_index("section") == layer)
    def _():
        for j, steps in enumerate(relative(digits, scatter_steps)[first : first + share * len(outs)]):
            start = pl.multiple_of(block_of(steps, digits, names) * width, width)
            part = jnp.dot(x[...], weight[0, :, pl.ds(start, width)], preferred_element_type=jnp.float32)
            outs[j // share][j % share] = part.astype(outs[0].dtype)


def first_spread_kernel(x, weight, *rest, outputs, layer, digits, names):
    outs, (here, held, total, x_arrived, arrived) = rest[:outputs], rest[outputs:]
    share, _, width = outs[0].shape
    chunks, pieces = arrived.shape
    depth = weight.shape[1] // chunks
    rows = depth // pieces

    @pl.when(lax.axis_index("section") == layer)
    def _():
        x_copy = pltpu.make_async_copy(x, here, x_arrived)
        x_copy.start()
        copies = []
        for chunk in range(chunks):
            for piece in range(pieces):
                these = pl.ds(chunk * depth + piece * rows, rows)
                copies.append(
                    pltpu.make_async_copy(weight.at[0, these, :], held.at[these, :], arrived.at[chunk, piece])
                )
                copies[-1].start()
        x_copy.wait()
        for chunk in range(chunks):
            for piece in range(pieces):
                copies[chunk * pieces + piece].wait()
            those = slice(chunk * depth, (chunk + 1) * depth)
            for j, steps in enumerate(relative(digits, scatter_steps)):
                start = pl.multiple_of(block_of(steps, digits, names) * width, width)
                part = jnp.dot(here[:, those], held[those, pl.ds(start, width)], preferred_element_type=jnp.float32)
                if chunk > 0:
                    part = part + total[j]
                if chunk < chunks - 1:
                    total[j] = part
                else:
                    outs[j // share][j % share] = part.astype(outs[0].dtype)


def spread(x, weight, first, groups, layer, digits, names):
    rows, depth = x.shape
    count = len(relative(digits, scatter_steps))
    share = count // digits[-1][0]
    width = weight.shape[2] // count
    vmem = pl.BlockSpec(memory_space=pltpu.VMEM)
    outs = [jax.ShapeDtypeStruct((share, rows, width), jnp.bfloat16)] * groups
    if layer > 0:
        return pl.pallas_call(
            functools.partial(spread_kernel, first=first * share, layer=layer, digits=digits, names=names),
            out_shape=outs,
            in_specs=[vmem, vmem],
            out_specs=[vmem] * groups,
            compiler_params=pltpu.CompilerParams(vmem_limit_bytes=8 * 2**20),
            name="spread",
        )(x, pltpu.with_memory_space_constraint(weight, pltpu.VMEM))
    chunks = 2 if depth % 256 == 0 else 1
    return pl.pallas_call(
        functools.partial(first_spread_kernel, outputs=groups, layer=layer, digits=digits, names=names),
        out_shape=outs,
        in_specs=[pl.BlockSpec(memory_space=pltpu.HBM)] * 2,
        out_specs=[vmem] * groups,
        scratch_shapes=[
            pltpu.VMEM(x.shape, x.dtype),
            pltpu.VMEM(weight.shape[1:], weight.dtype),
            pltpu.VMEM((count, rows, width), jnp.float32),
            pltpu.SemaphoreType.DMA,
            pltpu.SemaphoreType.DMA((chunks, 4)),
        ],
        compiler_params=pltpu.CompilerParams(vmem_limit_bytes=20 * 2**20),
        name="first_spread",
    )(
        pltpu.with_memory_space_constraint(x, pltpu.HBM),
        pltpu.with_memory_space_constraint(weight, pltpu.HBM),
    )


def meet_kernel(weight, *rest, first, blocks, layer, digits, names):
    inputs, before, (total, square) = rest[:blocks], rest[blocks:-2], rest[-2:]
    share, _, depth = inputs[0].shape
    inside = lax.axis_index("section") == layer

    @pl.when(inside)
    def _():
        sum_of = before[0][...] if before else jnp.zeros(total.shape, jnp.float32)
        squares = before[1][...] if before else jnp.zeros(square.shape, jnp.float32)
        for j, steps in enumerate(relative(digits, gather_steps)[first : first + share * blocks]):
            x = inputs[j // share][j % share]
            wide = x.astype(jnp.float32)
            squares = squares + jnp.sum(wide * wide, axis=1, keepdims=True)
            start = pl.multiple_of(block_of(steps, digits, names) * depth, depth)
            sum_of = sum_of + jnp.dot(x, weight[0, pl.ds(start, depth), :], preferred_element_type=jnp.float32)
        total[...] = sum_of
        square[...] = squares

    @pl.when(jnp.logical_not(inside))
    def _():
        total[...] = jnp.zeros_like(total)
        square[...] = jnp.zeros_like(square)


def meet(weight, groups, first, before, layer, digits, names):
    rows = groups[0].shape[1]
    vmem = pl.BlockSpec(memory_space=pltpu.VMEM)
    return pl.pallas_call(
        functools.partial(
            meet_kernel, first=first, blocks=len(groups), layer=layer, digits=digits, names=names
        ),
        out_shape=[
            jax.ShapeDtypeStruct((rows, weight.shape[2]), jnp.float32),
            jax.ShapeDtypeStruct((rows, 1), jnp.float32),
        ],
        in_specs=[vmem] * (1 + len(groups) + len(before)),
        out_specs=[vmem, vmem],
        compiler_params=pltpu.CompilerParams(vmem_limit_bytes=8 * 2**20),
        name="meet",
    )(pltpu.with_memory_space_constraint(weight, pltpu.VMEM), *groups, *before)


def tell_kernel(hidden, head, told, *, micro, sections):
    values = jnp.dot(hidden[...], head[...], preferred_element_type=jnp.float32)
    tokens = values.shape[0] // micro
    share = tokens // sections
    repeats = told.shape[0] // sections
    for section in range(sections):
        starts = [m * tokens + section * share for m in range(micro)]
        mine = jnp.concatenate([values[start : start + share] for start in starts], axis=0)
        for i in range(repeats):
            told[section * repeats + i] = mine.astype(told.dtype)


def tell(hidden, head, micro, sections, repeats):
    shape = (sections * repeats, hidden.shape[0] // sections, head.shape[1])
    vmem = pl.BlockSpec(memory_space=pltpu.VMEM)
    return pl.pallas_call(
        functools.partial(tell_kernel, micro=micro, sections=sections),
        out_shape=jax.ShapeDtypeStruct(shape, jnp.bfloat16),
        in_specs=[vmem, vmem],
        out_specs=vmem,
        compiler_params=pltpu.CompilerParams(vmem_limit_bytes=8 * 2**20),
        name="tell",
    )(hidden, head)


def per_device(start_tokens, target_weight, online_weight, head_weight, reward, action_bin, sections, digits, names):
    micro, tokens, width = start_tokens.shape
    tp = 1
    for radix, _ in digits:
        tp *= radix
    everyone = ("section",) + names
    rows = micro * tokens
    features = width * tp
    rounds = len(digits)
    send = functools.partial(exchange, axes=everyone, tp=tp)
    hidden = start_tokens.reshape(rows, width)
    for layer in range(sections):
        place = dict(layer=layer, digits=digits, names=names)
        helper = layer - 1 if layer > 0 else min(1, sections - 1)
        own = hidden
        if layer > 0:
            own = send(hidden, route=(helper, layer), radix=1, stride=1, step=0)

        inner = digits[-1][0]
        half = inner // 2
        if layer == 0:
            parts = list(spread(own, online_weight, 0, inner, **place))
        else:
            parts = list(spread(own, online_weight, 0, half, **place)) if half else []
            parts += spread(own, online_weight, half, inner - half, **place)
        stack, mine = (own[None], hidden[None]) if rounds % 2 == 0 else (hidden[None], own[None])
        gathered = [mine]
        for number, (radix, stride) in enumerate(digits):
            route = (helper, layer) if (rounds - number) % 2 == 1 else (layer, helper)
            gathered = []
            for step in gather_steps(radix, number == rounds - 1):
                if step == 0 and (number == 0 or helper == layer):
                    gathered.append(mine)
                else:
                    gathered.append(send(stack, route=route, radix=radix, stride=stride, step=step))
            if number < rounds - 1:
                gathered, parts[half:] = lax.optimization_barrier((gathered, parts[half:]))
                stack = mine = jnp.concatenate(gathered, axis=0)
        at = layer
        for number in range(rounds - 1, -1, -1):
            radix, stride = digits[number]
            to = at if (number + 1) % 2 == 1 and at == layer else (helper if at == layer else layer)
            wide = 0.0
            for step, one in zip(scatter_steps(radix, number == rounds - 1), parts):
                if step > 0 or to != at:
                    one = send(one, route=(at, to), radix=radix, stride=stride, step=step)
                wide = wide + one.astype(jnp.float32)
            at = to
            if number > 0:
                following = digits[number - 1][0]
                part = wide.shape[0] // following
                parts = [wide[i * part : (i + 1) * part].astype(jnp.bfloat16) for i in range(following)]

        before = []
        for begin in range(0, len(gathered), max(1, half)):
            groups = gathered[begin : begin + max(1, half)]
            before = meet(target_weight, groups, begin * groups[0].shape[0], before, **place)
        total, square = before
        update = lax.rsqrt(square / features + 1e-06) * (0.25 * wide[0] + 0.75 * total)
        hidden = (own.astype(jnp.float32) + update).astype(jnp.bfloat16)

    share_rows = reward.shape[1]
    bins = head_weight.shape[1]
    told = tell(hidden, head_weight, micro, sections, inner)
    told = lax.all_to_all(told, ("section", names[-1]), split_axis=0, concat_axis=0, tiled=True)
    mine = jnp.sum(told[(sections - 1) * inner :].astype(jnp.float32), axis=0)
    for (radix, _), name in zip(digits[:-1], names):
        told = jnp.broadcast_to(mine[None], (radix,) + mine.shape)
        mine = jnp.sum(lax.all_to_all(told, name, split_axis=0, concat_axis=0, tiled=True), axis=0)
    mine = mine.reshape(micro, share_rows, bins)
    best = jnp.max(mine, axis=2)
    bin_ids = lax.broadcasted_iota(jnp.int32, mine.shape, 2)
    taken = jnp.sum(jnp.where(bin_ids == action_bin[:, :, None], mine, 0.0), axis=2)
    return (reward + 0.98 * best, taken)


def solution(mesh):
    sections, tp = mesh.shape["section"], mesh.shape["tp"]
    digits = digits_of(tp, 4)
    names = tuple(f"tp{number}" for number in range(len(digits)))
    cut = jax.sharding.Mesh(
        mesh.devices.reshape([sections] + [radix for radix, _ in digits]), ("section",) + names
    )
    in_specs = (
        P(None, None, names),
        P("section", None, names),
        P("section", names, None),
        P(names, None),
        P(None, "section"),
        P(None, "section"),
    )
    out_specs = (P(None, "section"), P(None, "section"))
    body = functools.partial(per_device, sections=sections, digits=digits, names=names)
    return jax.shard_map(body, mesh=cut, in_specs=in_specs, out_specs=out_specs, check_vma=False)
```

```python
import functools

import jax
import jax.numpy as jnp
from jax import lax
from jax.experimental import pallas as pl
from jax.experimental.pallas import tpu as pltpu
from jax.sharding import PartitionSpec as P


def digits_of(size, most):
    radices = []
    left = size
    while left > 1:
        radix = next((r for r in range(min(most, left), 1, -1) if left % r == 0), None)
        if radix is None:
            radix = next(r for r in range(2, left + 1) if left % r == 0)
        radices.insert(0, radix)
        left //= radix
    strides = []
    stride = size
    for radix in radices:
        stride //= radix
        strides.append(stride)
    return list(zip(radices, strides))


def peer(digit, step, radix):
    if radix & (radix - 1) == 0:
        return digit ^ step
    return (digit + step) % radix


def exchange(value, axes, tp, route, radix, stride, step):
    pairs = []
    for t in range(tp):
        digit = t // stride % radix
        other = t + (peer(digit, step, radix) - digit) * stride
        pairs.append((route[0] * tp + t, route[1] * tp + other))
    return lax.ppermute(value, axes, pairs)


def block_of(steps, digits, names):
    index = 0
    for step, (radix, stride), name in zip(steps, digits, names):
        index = index + peer(lax.axis_index(name), step, radix) * stride
    return index


def gather_steps(radix, last):
    return [*range(radix)] if last else [*range(radix - 1, -1, -1)]


def scatter_steps(radix, last):
    half = radix // 2 if last else 0
    return [*range(radix - 1, half - 1, -1), *range(half)]


def relative(digits, steps_of):
    found = [()]
    for number, (radix, _) in enumerate(digits):
        found = [one + (step,) for step in steps_of(radix, number == len(digits) - 1) for one in found]
    return found


def spread_kernel(x, weight, *outs, first, layer, digits, names):
    share, _, width = outs[0].shape

    @pl.when(lax.axis_index("section") == layer)
    def _():
        for j, steps in enumerate(relative(digits, scatter_steps)[first : first + share * len(outs)]):
            start = pl.multiple_of(block_of(steps, digits, names) * width, width)
            part = jnp.dot(x[...], weight[0, :, pl.ds(start, width)], preferred_element_type=jnp.float32)
            outs[j // share][j % share] = part.astype(outs[0].dtype)


def first_spread_kernel(x, weight, *rest, outputs, layer, digits, names):
    outs, (here, held, total, x_arrived, arrived) = rest[:outputs], rest[outputs:]
    share, _, width = outs[0].shape
    chunks, pieces = arrived.shape
    depth = weight.shape[1] // chunks
    rows = depth // pieces

    @pl.when(lax.axis_index("section") == layer)
    def _():
        x_copy = pltpu.make_async_copy(x, here, x_arrived)
        x_copy.start()
        copies = []
        for chunk in range(chunks):
            for piece in range(pieces):
                these = pl.ds(chunk * depth + piece * rows, rows)
                copies.append(
                    pltpu.make_async_copy(weight.at[0, these, :], held.at[these, :], arrived.at[chunk, piece])
                )
                copies[-1].start()
        x_copy.wait()
        for chunk in range(chunks):
            for piece in range(pieces):
                copies[chunk * pieces + piece].wait()
            those = slice(chunk * depth, (chunk + 1) * depth)
            for j, steps in enumerate(relative(digits, scatter_steps)):
                start = pl.multiple_of(block_of(steps, digits, names) * width, width)
                part = jnp.dot(here[:, those], held[those, pl.ds(start, width)], preferred_element_type=jnp.float32)
                if chunk > 0:
                    part = part + total[j]
                if chunk < chunks - 1:
                    total[j] = part
                else:
                    outs[j // share][j % share] = part.astype(outs[0].dtype)


def spread(x, weight, first, groups, layer, digits, names):
    rows, depth = x.shape
    count = len(relative(digits, scatter_steps))
    share = count // digits[-1][0]
    width = weight.shape[2] // count
    vmem = pl.BlockSpec(memory_space=pltpu.VMEM)
    outs = [jax.ShapeDtypeStruct((share, rows, width), jnp.bfloat16)] * groups
    if layer > 0:
        return pl.pallas_call(
            functools.partial(spread_kernel, first=first * share, layer=layer, digits=digits, names=names),
            out_shape=outs,
            in_specs=[vmem, vmem],
            out_specs=[vmem] * groups,
            compiler_params=pltpu.CompilerParams(vmem_limit_bytes=8 * 2**20),
            name="spread",
        )(x, pltpu.with_memory_space_constraint(weight, pltpu.VMEM))
    chunks = 2 if depth % 256 == 0 else 1
    return pl.pallas_call(
        functools.partial(first_spread_kernel, outputs=groups, layer=layer, digits=digits, names=names),
        out_shape=outs,
        in_specs=[pl.BlockSpec(memory_space=pltpu.HBM)] * 2,
        out_specs=[vmem] * groups,
        scratch_shapes=[
            pltpu.VMEM(x.shape, x.dtype),
            pltpu.VMEM(weight.shape[1:], weight.dtype),
            pltpu.VMEM((count, rows, width), jnp.float32),
            pltpu.SemaphoreType.DMA,
            pltpu.SemaphoreType.DMA((chunks, 4)),
        ],
        compiler_params=pltpu.CompilerParams(vmem_limit_bytes=20 * 2**20),
        name="first_spread",
    )(
        pltpu.with_memory_space_constraint(x, pltpu.HBM),
        pltpu.with_memory_space_constraint(weight, pltpu.HBM),
    )


def meet_kernel(weight, *rest, first, blocks, layer, digits, names):
    inputs, before, (total, square) = rest[:blocks], rest[blocks:-2], rest[-2:]
    share, _, depth = inputs[0].shape
    inside = lax.axis_index("section") == layer

    @pl.when(inside)
    def _():
        sum_of = before[0][...] if before else jnp.zeros(total.shape, jnp.float32)
        squares = before[1][...] if before else jnp.zeros(square.shape, jnp.float32)
        for j, steps in enumerate(relative(digits, gather_steps)[first : first + share * blocks]):
            x = inputs[j // share][j % share]
            wide = x.astype(jnp.float32)
            squares = squares + jnp.sum(wide * wide, axis=1, keepdims=True)
            start = pl.multiple_of(block_of(steps, digits, names) * depth, depth)
            sum_of = sum_of + jnp.dot(x, weight[0, pl.ds(start, depth), :], preferred_element_type=jnp.float32)
        total[...] = sum_of
        square[...] = squares

    @pl.when(jnp.logical_not(inside))
    def _():
        total[...] = jnp.zeros_like(total)
        square[...] = jnp.zeros_like(square)


def meet(weight, groups, first, before, layer, digits, names):
    rows = groups[0].shape[1]
    vmem = pl.BlockSpec(memory_space=pltpu.VMEM)
    return pl.pallas_call(
        functools.partial(
            meet_kernel, first=first, blocks=len(groups), layer=layer, digits=digits, names=names
        ),
        out_shape=[
            jax.ShapeDtypeStruct((rows, weight.shape[2]), jnp.float32),
            jax.ShapeDtypeStruct((rows, 1), jnp.float32),
        ],
        in_specs=[vmem] * (1 + len(groups) + len(before)),
        out_specs=[vmem, vmem],
        compiler_params=pltpu.CompilerParams(vmem_limit_bytes=8 * 2**20),
        name="meet",
    )(pltpu.with_memory_space_constraint(weight, pltpu.VMEM), *groups, *before)


def tell_kernel(hidden, head, told, *, micro, sections):
    values = jnp.dot(hidden[...], head[...], preferred_element_type=jnp.float32)
    tokens = values.shape[0] // micro
    share = tokens // sections
    repeats = told.shape[0] // sections
    for section in range(sections):
        starts = [m * tokens + section * share for m in range(micro)]
        mine = jnp.concatenate([values[start : start + share] for start in starts], axis=0)
        for i in range(repeats):
            told[section * repeats + i] = mine.astype(told.dtype)


def tell(hidden, head, micro, sections, repeats):
    shape = (sections * repeats, hidden.shape[0] // sections, head.shape[1])
    vmem = pl.BlockSpec(memory_space=pltpu.VMEM)
    return pl.pallas_call(
        functools.partial(tell_kernel, micro=micro, sections=sections),
        out_shape=jax.ShapeDtypeStruct(shape, jnp.bfloat16),
        in_specs=[vmem, vmem],
        out_specs=vmem,
        compiler_params=pltpu.CompilerParams(vmem_limit_bytes=8 * 2**20),
        name="tell",
    )(hidden, head)


def per_device(start_tokens, target_weight, online_weight, head_weight, reward, action_bin, sections, digits, names):
    micro, tokens, width = start_tokens.shape
    tp = 1
    for radix, _ in digits:
        tp *= radix
    everyone = ("section",) + names
    rows = micro * tokens
    features = width * tp
    rounds = len(digits)
    send = functools.partial(exchange, axes=everyone, tp=tp)
    hidden = start_tokens.reshape(rows, width)
    for layer in range(sections):
        place = dict(layer=layer, digits=digits, names=names)
        helper = layer - 1 if layer > 0 else min(1, sections - 1)
        own = hidden
        if layer > 0:
            own = send(hidden, route=(helper, layer), radix=1, stride=1, step=0)

        inner = digits[-1][0]
        half = inner // 2
        if layer == 0:
            parts = list(spread(own, online_weight, 0, inner, **place))
        else:
            parts = list(spread(own, online_weight, 0, half, **place)) if half else []
            parts += spread(own, online_weight, half, inner - half, **place)
        stack, mine = (own[None], hidden[None]) if rounds % 2 == 0 else (hidden[None], own[None])
        gathered = [mine]
        for number, (radix, stride) in enumerate(digits):
            route = (helper, layer) if (rounds - number) % 2 == 1 else (layer, helper)
            gathered = []
            for step in gather_steps(radix, number == rounds - 1):
                if step == 0 and (number == 0 or helper == layer):
                    gathered.append(mine)
                else:
                    gathered.append(send(stack, route=route, radix=radix, stride=stride, step=step))
            if number < rounds - 1:
                gathered, parts[half:] = lax.optimization_barrier((gathered, parts[half:]))
                stack = mine = jnp.concatenate(gathered, axis=0)
        at = layer
        for number in range(rounds - 1, -1, -1):
            radix, stride = digits[number]
            to = at if (number + 1) % 2 == 1 and at == layer else (helper if at == layer else layer)
            wide = 0.0
            for step, one in zip(scatter_steps(radix, number == rounds - 1), parts):
                if step > 0 or to != at:
                    one = send(one, route=(at, to), radix=radix, stride=stride, step=step)
                wide = wide + one.astype(jnp.float32)
            at = to
            if number > 0:
                following = digits[number - 1][0]
                part = wide.shape[0] // following
                parts = [wide[i * part : (i + 1) * part].astype(jnp.bfloat16) for i in range(following)]

        before = []
        for begin in range(0, len(gathered), max(1, half)):
            groups = gathered[begin : begin + max(1, half)]
            before = meet(target_weight, groups, begin * groups[0].shape[0], before, **place)
        total, square = before
        update = lax.rsqrt(square / features + 1e-06) * (0.25 * wide[0] + 0.75 * total)
        hidden = (own.astype(jnp.float32) + update).astype(jnp.bfloat16)

    share_rows = reward.shape[1]
    bins = head_weight.shape[1]
    told = tell(hidden, head_weight, micro, sections, inner)
    told = lax.all_to_all(told, ("section", names[-1]), split_axis=0, concat_axis=0, tiled=True)
    mine = jnp.sum(told[(sections - 1) * inner :].astype(jnp.float32), axis=0)
    mine = mine.reshape(micro, share_rows, bins)
    for (radix, _), name in zip(digits[:-1], names):
        told = jnp.broadcast_to(mine[None], (radix,) + mine.shape)
        mine = jnp.sum(lax.all_to_all(told, name, split_axis=0, concat_axis=0, tiled=True), axis=0)
    best = jnp.max(mine, axis=2)
    bin_ids = lax.broadcasted_iota(jnp.int32, mine.shape, 2)
    taken = jnp.sum(jnp.where(bin_ids == action_bin[:, :, None], mine, 0.0), axis=2)
    return (reward + 0.98 * best, taken)


def solution(mesh):
    sections, tp = mesh.shape["section"], mesh.shape["tp"]
    digits = digits_of(tp, 4)
    names = tuple(f"tp{number}" for number in range(len(digits)))
    cut = jax.sharding.Mesh(
        mesh.devices.reshape([sections] + [radix for radix, _ in digits]), ("section",) + names
    )
    in_specs = (
        P(None, None, names),
        P("section", None, names),
        P("section", names, None),
        P(names, None),
        P(None, "section"),
        P(None, "section"),
    )
    out_specs = (P(None, "section"), P(None, "section"))
    body = functools.partial(per_device, sections=sections, digits=digits, names=names)
    return jax.shard_map(body, mesh=cut, in_specs=in_specs, out_specs=out_specs, check_vma=False)
```

```python
import functools

import jax
import jax.numpy as jnp
from jax import lax
from jax.experimental import pallas as pl
from jax.experimental.pallas import tpu as pltpu
from jax.sharding import PartitionSpec as P


def digits_of(size, most):
    radices = []
    left = size
    while left > 1:
        radix = next((r for r in range(min(most, left), 1, -1) if left % r == 0), None)
        if radix is None:
            radix = next(r for r in range(2, left + 1) if left % r == 0)
        radices.insert(0, radix)
        left //= radix
    strides = []
    stride = size
    for radix in radices:
        stride //= radix
        strides.append(stride)
    return list(zip(radices, strides))


def peer(digit, step, radix):
    if radix & (radix - 1) == 0:
        return digit ^ step
    return (digit + step) % radix


def exchange(value, axes, tp, routes, radix, stride, step):
    pairs = []
    for start, end in routes:
        for t in range(tp):
            digit = t // stride % radix
            other = t + (peer(digit, step, radix) - digit) * stride
            pairs.append((start * tp + t, end * tp + other))
    return lax.ppermute(value, axes, pairs)


def block_of(steps, digits, names):
    index = 0
    for step, (radix, stride), name in zip(steps, digits, names):
        index = index + peer(lax.axis_index(name), step, radix) * stride
    return index


def gather_steps(radix, last):
    return [*range(radix)] if last else [*range(radix - 1, -1, -1)]


def scatter_steps(radix, last):
    half = radix // 2 if last else 0
    return [*range(radix - 1, half - 1, -1), *range(half)]


def relative(digits, steps_of):
    found = [()]
    for number, (radix, _) in enumerate(digits):
        found = [one + (step,) for step in steps_of(radix, number == len(digits) - 1) for one in found]
    return found


def spread_kernel(x, weight, *outs, first, layer, digits, names):
    share, _, width = outs[0].shape

    @pl.when(lax.axis_index("section") == layer)
    def _():
        for j, steps in enumerate(relative(digits, scatter_steps)[first : first + share * len(outs)]):
            start = pl.multiple_of(block_of(steps, digits, names) * width, width)
            part = jnp.dot(x[...], weight[0, :, pl.ds(start, width)], preferred_element_type=jnp.float32)
            outs[j // share][j % share] = part.astype(outs[0].dtype)


def first_spread_kernel(x, weight, *rest, outputs, layer, digits, names):
    outs, (here, held, total, x_arrived, arrived) = rest[:outputs], rest[outputs:]
    share, _, width = outs[0].shape
    chunks, pieces = arrived.shape
    depth = weight.shape[1] // chunks
    rows = depth // pieces

    @pl.when(lax.axis_index("section") == layer)
    def _():
        x_copy = pltpu.make_async_copy(x, here, x_arrived)
        x_copy.start()
        copies = []
        for chunk in range(chunks):
            for piece in range(pieces):
                these = pl.ds(chunk * depth + piece * rows, rows)
                copies.append(
                    pltpu.make_async_copy(weight.at[0, these, :], held.at[these, :], arrived.at[chunk, piece])
                )
                copies[-1].start()
        x_copy.wait()
        for chunk in range(chunks):
            for piece in range(pieces):
                copies[chunk * pieces + piece].wait()
            those = slice(chunk * depth, (chunk + 1) * depth)
            for j, steps in enumerate(relative(digits, scatter_steps)):
                start = pl.multiple_of(block_of(steps, digits, names) * width, width)
                part = jnp.dot(here[:, those], held[those, pl.ds(start, width)], preferred_element_type=jnp.float32)
                if chunk > 0:
                    part = part + total[j]
                if chunk < chunks - 1:
                    total[j] = part
                else:
                    outs[j // share][j % share] = part.astype(outs[0].dtype)


def spread(x, weight, first, groups, layer, digits, names):
    rows, depth = x.shape
    count = len(relative(digits, scatter_steps))
    share = count // digits[-1][0]
    width = weight.shape[2] // count
    vmem = pl.BlockSpec(memory_space=pltpu.VMEM)
    outs = [jax.ShapeDtypeStruct((share, rows, width), jnp.bfloat16)] * groups
    if layer > 0:
        return pl.pallas_call(
            functools.partial(spread_kernel, first=first * share, layer=layer, digits=digits, names=names),
            out_shape=outs,
            in_specs=[vmem, vmem],
            out_specs=[vmem] * groups,
            compiler_params=pltpu.CompilerParams(vmem_limit_bytes=8 * 2**20),
            name="spread",
        )(x, pltpu.with_memory_space_constraint(weight, pltpu.VMEM))
    chunks = 2 if depth % 256 == 0 else 1
    return pl.pallas_call(
        functools.partial(first_spread_kernel, outputs=groups, layer=layer, digits=digits, names=names),
        out_shape=outs,
        in_specs=[pl.BlockSpec(memory_space=pltpu.HBM)] * 2,
        out_specs=[vmem] * groups,
        scratch_shapes=[
            pltpu.VMEM(x.shape, x.dtype),
            pltpu.VMEM(weight.shape[1:], weight.dtype),
            pltpu.VMEM((count, rows, width), jnp.float32),
            pltpu.SemaphoreType.DMA,
            pltpu.SemaphoreType.DMA((chunks, 4)),
        ],
        compiler_params=pltpu.CompilerParams(vmem_limit_bytes=20 * 2**20),
        name="first_spread",
    )(
        pltpu.with_memory_space_constraint(x, pltpu.HBM),
        pltpu.with_memory_space_constraint(weight, pltpu.HBM),
    )


def meet_kernel(weight, *rest, first, blocks, layer, digits, names):
    inputs, before, (total, square) = rest[:blocks], rest[blocks:-2], rest[-2:]
    share, _, depth = inputs[0].shape
    inside = lax.axis_index("section") == layer

    @pl.when(inside)
    def _():
        sum_of = before[0][...] if before else jnp.zeros(total.shape, jnp.float32)
        squares = before[1][...] if before else jnp.zeros(square.shape, jnp.float32)
        for j, steps in enumerate(relative(digits, gather_steps)[first : first + share * blocks]):
            x = inputs[j // share][j % share]
            wide = x.astype(jnp.float32)
            squares = squares + jnp.sum(wide * wide, axis=1, keepdims=True)
            start = pl.multiple_of(block_of(steps, digits, names) * depth, depth)
            sum_of = sum_of + jnp.dot(x, weight[0, pl.ds(start, depth), :], preferred_element_type=jnp.float32)
        total[...] = sum_of
        square[...] = squares

    @pl.when(jnp.logical_not(inside))
    def _():
        total[...] = jnp.zeros_like(total)
        square[...] = jnp.zeros_like(square)


def meet(weight, groups, first, before, layer, digits, names):
    rows = groups[0].shape[1]
    vmem = pl.BlockSpec(memory_space=pltpu.VMEM)
    return pl.pallas_call(
        functools.partial(
            meet_kernel, first=first, blocks=len(groups), layer=layer, digits=digits, names=names
        ),
        out_shape=[
            jax.ShapeDtypeStruct((rows, weight.shape[2]), jnp.float32),
            jax.ShapeDtypeStruct((rows, 1), jnp.float32),
        ],
        in_specs=[vmem] * (1 + len(groups) + len(before)),
        out_specs=[vmem, vmem],
        compiler_params=pltpu.CompilerParams(vmem_limit_bytes=8 * 2**20),
        name="meet",
    )(pltpu.with_memory_space_constraint(weight, pltpu.VMEM), *groups, *before)


def tell_kernel(hidden, head, told, *, micro, sections):
    values = jnp.dot(hidden[...], head[...], preferred_element_type=jnp.float32)
    tokens = values.shape[0] // micro
    share = tokens // sections
    repeats = told.shape[0] // sections
    for section in range(sections):
        starts = [m * tokens + section * share for m in range(micro)]
        mine = jnp.concatenate([values[start : start + share] for start in starts], axis=0)
        for i in range(repeats):
            told[section * repeats + i] = mine.astype(told.dtype)


def tell(hidden, head, micro, sections, repeats):
    shape = (sections * repeats, hidden.shape[0] // sections, head.shape[1])
    vmem = pl.BlockSpec(memory_space=pltpu.VMEM)
    return pl.pallas_call(
        functools.partial(tell_kernel, micro=micro, sections=sections),
        out_shape=jax.ShapeDtypeStruct(shape, jnp.bfloat16),
        in_specs=[vmem, vmem],
        out_specs=vmem,
        compiler_params=pltpu.CompilerParams(vmem_limit_bytes=8 * 2**20),
        name="tell",
    )(hidden, head)


def per_device(start_tokens, target_weight, online_weight, head_weight, reward, action_bin, sections, digits, names):
    micro, tokens, width = start_tokens.shape
    tp = 1
    for radix, _ in digits:
        tp *= radix
    everyone = ("section",) + names
    rows = micro * tokens
    features = width * tp
    rounds = len(digits)
    send = functools.partial(exchange, axes=everyone, tp=tp)
    hidden = start_tokens.reshape(rows, width)
    for layer in range(sections):
        place = dict(layer=layer, digits=digits, names=names)
        helper = layer - 1 if layer > 0 else min(1, sections - 1)
        own = hidden
        if layer > 0:
            own = send(hidden, routes=[(helper, layer)], radix=1, stride=1, step=0)

        inner = digits[-1][0]
        half = inner // 2
        if layer == 0:
            parts = list(spread(own, online_weight, 0, inner, **place))
        else:
            parts = list(spread(own, online_weight, 0, half, **place)) if half else []
            parts += spread(own, online_weight, half, inner - half, **place)
        stack, mine = (own[None], hidden[None]) if rounds % 2 == 0 else (hidden[None], own[None])
        gathered = [mine]
        for number, (radix, stride) in enumerate(digits):
            routes = [(helper, layer) if (rounds - number) % 2 == 1 else (layer, helper)]
            if layer == 0 < helper and number < rounds - 1:
                routes = [(layer, helper), (helper, layer)]
            gathered = []
            for step in gather_steps(radix, number == rounds - 1):
                if step == 0 and (layer == 0 or number == 0):
                    gathered.append(mine)
                else:
                    gathered.append(send(stack, routes=routes, radix=radix, stride=stride, step=step))
            if number < rounds - 1:
                gathered, parts[half:] = lax.optimization_barrier((gathered, parts[half:]))
                stack = mine = jnp.concatenate(gathered, axis=0)
        at = layer
        for number in range(rounds - 1, -1, -1):
            radix, stride = digits[number]
            to = at if (number + 1) % 2 == 1 and at == layer else (helper if at == layer else layer)
            wide = 0.0
            for step, one in zip(scatter_steps(radix, number == rounds - 1), parts):
                if step > 0 or to != at:
                    one = send(one, routes=[(at, to)], radix=radix, stride=stride, step=step)
                wide = wide + one.astype(jnp.float32)
            at = to
            if number > 0:
                following = digits[number - 1][0]
                part = wide.shape[0] // following
                parts = [wide[i * part : (i + 1) * part].astype(jnp.bfloat16) for i in range(following)]

        before = []
        for begin in range(0, len(gathered), max(1, half)):
            groups = gathered[begin : begin + max(1, half)]
            before = meet(target_weight, groups, begin * groups[0].shape[0], before, **place)
        total, square = before
        update = lax.rsqrt(square / features + 1e-06) * (0.25 * wide[0] + 0.75 * total)
        hidden = (own.astype(jnp.float32) + update).astype(jnp.bfloat16)

    share_rows = reward.shape[1]
    bins = head_weight.shape[1]
    told = tell(hidden, head_weight, micro, sections, inner)
    told = lax.all_to_all(told, ("section", names[-1]), split_axis=0, concat_axis=0, tiled=True)
    mine = jnp.sum(told[(sections - 1) * inner :].astype(jnp.float32), axis=0)
    mine = mine.reshape(micro, share_rows, bins)
    for (radix, _), name in zip(digits[:-1], names):
        told = jnp.broadcast_to(mine[None], (radix,) + mine.shape)
        mine = jnp.sum(lax.all_to_all(told, name, split_axis=0, concat_axis=0, tiled=True), axis=0)
    best = jnp.max(mine, axis=2)
    bin_ids = lax.broadcasted_iota(jnp.int32, mine.shape, 2)
    taken = jnp.sum(jnp.where(bin_ids == action_bin[:, :, None], mine, 0.0), axis=2)
    return (reward + 0.98 * best, taken)


def solution(mesh):
    sections, tp = mesh.shape["section"], mesh.shape["tp"]
    digits = digits_of(tp, 4)
    names = tuple(f"tp{number}" for number in range(len(digits)))
    cut = jax.sharding.Mesh(
        mesh.devices.reshape([sections] + [radix for radix, _ in digits]), ("section",) + names
    )
    in_specs = (
        P(None, None, names),
        P("section", None, names),
        P("section", names, None),
        P(names, None),
        P(None, "section"),
        P(None, "section"),
    )
    out_specs = (P(None, "section"), P(None, "section"))
    body = functools.partial(per_device, sections=sections, digits=digits, names=names)
    return jax.shard_map(body, mesh=cut, in_specs=in_specs, out_specs=out_specs, check_vma=False)
```

```python
import functools

import jax
import jax.numpy as jnp
from jax import lax
from jax.experimental import pallas as pl
from jax.experimental.pallas import tpu as pltpu
from jax.sharding import PartitionSpec as P


def digits_of(size, most):
    radices = []
    left = size
    while left > 1:
        radix = next((r for r in range(min(most, left), 1, -1) if left % r == 0), None)
        if radix is None:
            radix = next(r for r in range(2, left + 1) if left % r == 0)
        radices.insert(0, radix)
        left //= radix
    strides = []
    stride = size
    for radix in radices:
        stride //= radix
        strides.append(stride)
    return list(zip(radices, strides))


def peer(digit, step, radix):
    if radix & (radix - 1) == 0:
        return digit ^ step
    return (digit + step) % radix


def exchange(value, axes, tp, routes, radix, stride, step):
    pairs = []
    for start, end in routes:
        for t in range(tp):
            digit = t // stride % radix
            other = t + (peer(digit, step, radix) - digit) * stride
            pairs.append((start * tp + t, end * tp + other))
    return lax.ppermute(value, axes, pairs)


def block_of(steps, digits, names):
    index = 0
    for step, (radix, stride), name in zip(steps, digits, names):
        index = index + peer(lax.axis_index(name), step, radix) * stride
    return index


def steps_of(radix):
    return [*range(radix - 1, -1, -1)]


def relative(digits):
    found = [()]
    for radix, _ in digits:
        found = [one + (step,) for step in steps_of(radix) for one in found]
    return found


def spread_kernel(x, weight, *outs, layer, digits, names):
    share, _, width = outs[0].shape

    @pl.when(lax.axis_index("section") == layer)
    def _():
        for j, steps in enumerate(relative(digits)):
            start = pl.multiple_of(block_of(steps, digits, names) * width, width)
            part = jnp.dot(x[...], weight[0, :, pl.ds(start, width)], preferred_element_type=jnp.float32)
            outs[j // share][j % share] = part.astype(outs[0].dtype)


def first_spread_kernel(x, weight, *rest, outputs, layer, digits, names):
    outs, (here, held, total, x_arrived, arrived) = rest[:outputs], rest[outputs:]
    share, _, width = outs[0].shape
    chunks, pieces = arrived.shape
    depth = weight.shape[1] // chunks
    rows = depth // pieces

    @pl.when(lax.axis_index("section") == layer)
    def _():
        x_copy = pltpu.make_async_copy(x, here, x_arrived)
        x_copy.start()
        copies = []
        for chunk in range(chunks):
            for piece in range(pieces):
                these = pl.ds(chunk * depth + piece * rows, rows)
                copies.append(
                    pltpu.make_async_copy(weight.at[0, these, :], held.at[these, :], arrived.at[chunk, piece])
                )
                copies[-1].start()
        x_copy.wait()
        for chunk in range(chunks):
            for piece in range(pieces):
                copies[chunk * pieces + piece].wait()
            those = slice(chunk * depth, (chunk + 1) * depth)
            for j, steps in enumerate(relative(digits)):
                start = pl.multiple_of(block_of(steps, digits, names) * width, width)
                part = jnp.dot(here[:, those], held[those, pl.ds(start, width)], preferred_element_type=jnp.float32)
                if chunk > 0:
                    part = part + total[j]
                if chunk < chunks - 1:
                    total[j] = part
                else:
                    outs[j // share][j % share] = part.astype(outs[0].dtype)


def spread(x, weight, layer, digits, names):
    rows, depth = x.shape
    groups = digits[-1][0]
    count = len(relative(digits))
    share = count // groups
    width = weight.shape[2] // count
    vmem = pl.BlockSpec(memory_space=pltpu.VMEM)
    outs = [jax.ShapeDtypeStruct((share, rows, width), jnp.bfloat16)] * groups
    if layer > 0:
        return pl.pallas_call(
            functools.partial(spread_kernel, layer=layer, digits=digits, names=names),
            out_shape=outs,
            in_specs=[vmem, vmem],
            out_specs=[vmem] * groups,
            compiler_params=pltpu.CompilerParams(vmem_limit_bytes=8 * 2**20),
            name="spread",
        )(x, pltpu.with_memory_space_constraint(weight, pltpu.VMEM))
    chunks = 2 if depth % 256 == 0 else 1
    return pl.pallas_call(
        functools.partial(first_spread_kernel, outputs=groups, layer=layer, digits=digits, names=names),
        out_shape=outs,
        in_specs=[pl.BlockSpec(memory_space=pltpu.HBM)] * 2,
        out_specs=[vmem] * groups,
        scratch_shapes=[
            pltpu.VMEM(x.shape, x.dtype),
            pltpu.VMEM(weight.shape[1:], weight.dtype),
            pltpu.VMEM((count, rows, width), jnp.float32),
            pltpu.SemaphoreType.DMA,
            pltpu.SemaphoreType.DMA((chunks, 4)),
        ],
        compiler_params=pltpu.CompilerParams(vmem_limit_bytes=20 * 2**20),
        name="first_spread",
    )(
        pltpu.with_memory_space_constraint(x, pltpu.HBM),
        pltpu.with_memory_space_constraint(weight, pltpu.HBM),
    )


def mix_kernel(*rest, groups, layer):
    parts, blocks, outs = rest[:groups], rest[groups:-groups], rest[-groups:]
    inside = lax.axis_index("section") == layer

    @pl.when(inside)
    def _():
        for part, out in zip(parts, outs):
            out[...] = part[...]

    @pl.when(jnp.logical_not(inside))
    def _():
        start = 0
        for block in blocks:
            for out in outs:
                out[start : start + block.shape[0]] = block[...]
            start += block.shape[0]


def mix(parts, blocks, layer):
    vmem = pl.BlockSpec(memory_space=pltpu.VMEM)
    return pl.pallas_call(
        functools.partial(mix_kernel, groups=len(parts), layer=layer),
        out_shape=[jax.ShapeDtypeStruct(part.shape, part.dtype) for part in parts],
        in_specs=[vmem] * (len(parts) + len(blocks)),
        out_specs=[vmem] * len(parts),
        compiler_params=pltpu.CompilerParams(vmem_limit_bytes=8 * 2**20),
        name="mix",
    )(*parts, *blocks)


def meet_kernel(weight, *rest, first, blocks, layer, digits, names):
    inputs, before, (total, square) = rest[:blocks], rest[blocks:-2], rest[-2:]
    share, _, depth = inputs[0].shape
    inside = lax.axis_index("section") == layer

    @pl.when(inside)
    def _():
        sum_of = before[0][...] if before else jnp.zeros(total.shape, jnp.float32)
        squares = before[1][...] if before else jnp.zeros(square.shape, jnp.float32)
        for j, steps in enumerate(relative(digits)[first : first + share * blocks]):
            x = inputs[j // share][j % share]
            wide = x.astype(jnp.float32)
            squares = squares + jnp.sum(wide * wide, axis=1, keepdims=True)
            start = pl.multiple_of(block_of(steps, digits, names) * depth, depth)
            sum_of = sum_of + jnp.dot(x, weight[0, pl.ds(start, depth), :], preferred_element_type=jnp.float32)
        total[...] = sum_of
        square[...] = squares

    @pl.when(jnp.logical_not(inside))
    def _():
        total[...] = jnp.zeros_like(total)
        square[...] = jnp.full_like(square, -1.0)


def meet(weight, groups, first, before, layer, digits, names):
    rows = groups[0].shape[1]
    vmem = pl.BlockSpec(memory_space=pltpu.VMEM)
    return pl.pallas_call(
        functools.partial(
            meet_kernel, first=first, blocks=len(groups), layer=layer, digits=digits, names=names
        ),
        out_shape=[
            jax.ShapeDtypeStruct((rows, weight.shape[2]), jnp.float32),
            jax.ShapeDtypeStruct((rows, 1), jnp.float32),
        ],
        in_specs=[vmem] * (1 + len(groups) + len(before)),
        out_specs=[vmem, vmem],
        compiler_params=pltpu.CompilerParams(vmem_limit_bytes=8 * 2**20),
        name="meet",
    )(pltpu.with_memory_space_constraint(weight, pltpu.VMEM), *groups, *before)


def tell_kernel(hidden, head, told, *, micro, sections):
    values = jnp.dot(hidden[...], head[...], preferred_element_type=jnp.float32)
    tokens = values.shape[0] // micro
    share = tokens // sections
    repeats = told.shape[0] // sections
    for section in range(sections):
        starts = [m * tokens + section * share for m in range(micro)]
        mine = jnp.concatenate([values[start : start + share] for start in starts], axis=0)
        for i in range(repeats):
            told[section * repeats + i] = mine.astype(told.dtype)


def tell(hidden, head, micro, sections, repeats):
    shape = (sections * repeats, hidden.shape[0] // sections, head.shape[1])
    vmem = pl.BlockSpec(memory_space=pltpu.VMEM)
    return pl.pallas_call(
        functools.partial(tell_kernel, micro=micro, sections=sections),
        out_shape=jax.ShapeDtypeStruct(shape, jnp.bfloat16),
        in_specs=[vmem, vmem],
        out_specs=vmem,
        compiler_params=pltpu.CompilerParams(vmem_limit_bytes=8 * 2**20),
        name="tell",
    )(hidden, head)


def per_device(start_tokens, target_weight, online_weight, head_weight, reward, action_bin, sections, digits, names):
    micro, tokens, width = start_tokens.shape
    tp = 1
    for radix, _ in digits:
        tp *= radix
    everyone = ("section",) + names
    rows = micro * tokens
    features = width * tp
    rounds = len(digits)
    send = functools.partial(exchange, axes=everyone, tp=tp)
    own = start_tokens.reshape(rows, width)
    for layer in range(sections):
        place = dict(layer=layer, digits=digits, names=names)
        helper = layer - 1 if layer > 0 else min(1, sections - 1)
        both = [(layer, helper), (helper, layer)] if helper != layer else [(layer, layer)]
        if layer > 0:
            own = own + send(own, routes=both, radix=1, stride=1, step=0)
        parts = spread(own, online_weight, **place)
        blocks = [own[None]]
        for radix, stride in digits[:-1]:
            stack = jnp.concatenate(blocks, axis=0) if len(blocks) > 1 else blocks[0]
            blocks = []
            for step in steps_of(radix):
                blocks.append(stack if step == 0 else send(stack, routes=both, radix=radix, stride=stride, step=step))
        stack = jnp.concatenate(blocks, axis=0) if len(blocks) > 1 else blocks[0]
        radix, stride = digits[-1]
        if helper != layer and rounds > 1:
            at = helper
            sent = [
                send(one, routes=both, radix=radix, stride=stride, step=step)
                for step, one in zip(steps_of(radix), mix(parts, blocks, layer))
            ]
            gathered = sent[:-1] + [stack]
        else:
            at = layer
            here = functools.partial(send, routes=[(layer, layer)], radix=radix, stride=stride)
            gathered = [stack if step == 0 else here(stack, step=step) for step in steps_of(radix)]
            sent = [one if step == 0 else here(one, step=step) for step, one in zip(steps_of(radix), parts)]
        wide = functools.reduce(jnp.add, [one.astype(jnp.float32) for one in sent])
        for number in range(rounds - 2, -1, -1):
            radix, stride = digits[number]
            part = wide.shape[0] // radix
            sums = wide
            cross = number == 0 and at != layer
            routes = both if cross else [(at, at)]
            sent = []
            for i, step in enumerate(steps_of(radix)):
                one = sums[i * part : (i + 1) * part].astype(jnp.bfloat16)
                if cross or step > 0:
                    one = send(one, routes=routes, radix=radix, stride=stride, step=step)
                sent.append(one)
            wide = functools.reduce(jnp.add, [one.astype(jnp.float32) for one in sent])

        before = []
        half = max(1, len(gathered) // 2)
        for begin in range(0, len(gathered), half):
            groups = gathered[begin : begin + half]
            before = meet(target_weight, groups, begin * groups[0].shape[0], before, **place)
        total, square = before
        update = lax.rsqrt(square / features + 1e-06) * (0.25 * wide[0] + 0.75 * total)
        own = jnp.where(square >= 0.0, own.astype(jnp.float32) + update, 0.0).astype(jnp.bfloat16)

    share_rows = reward.shape[1]
    bins = head_weight.shape[1]
    inner = digits[-1][0]
    told = tell(own, head_weight, micro, sections, inner)
    told = lax.all_to_all(told, ("section", names[-1]), split_axis=0, concat_axis=0, tiled=True)
    mine = jnp.sum(told[(sections - 1) * inner :].astype(jnp.float32), axis=0)
    mine = mine.reshape(micro, share_rows, bins)
    for (radix, _), name in zip(digits[:-1], names):
        told = jnp.broadcast_to(mine[None], (radix,) + mine.shape)
        mine = jnp.sum(lax.all_to_all(told, name, split_axis=0, concat_axis=0, tiled=True), axis=0)
    best = jnp.max(mine, axis=2)
    bin_ids = lax.broadcasted_iota(jnp.int32, mine.shape, 2)
    taken = jnp.sum(jnp.where(bin_ids == action_bin[:, :, None], mine, 0.0), axis=2)
    return (reward + 0.98 * best, taken)


def solution(mesh):
    sections, tp = mesh.shape["section"], mesh.shape["tp"]
    digits = digits_of(tp, 4)
    names = tuple(f"tp{number}" for number in range(len(digits)))
    cut = jax.sharding.Mesh(
        mesh.devices.reshape([sections] + [radix for radix, _ in digits]), ("section",) + names
    )
    in_specs = (
        P(None, None, names),
        P("section", None, names),
        P("section", names, None),
        P(names, None),
        P(None, "section"),
        P(None, "section"),
    )
    out_specs = (P(None, "section"), P(None, "section"))
    body = functools.partial(per_device, sections=sections, digits=digits, names=names)
    return jax.shard_map(body, mesh=cut, in_specs=in_specs, out_specs=out_specs, check_vma=False)
```

```python
import functools

import jax
import jax.numpy as jnp
from jax import lax
from jax.experimental import pallas as pl
from jax.experimental.pallas import tpu as pltpu
from jax.sharding import PartitionSpec as P


def digits_of(size, most):
    radices = []
    left = size
    while left > 1:
        radix = next((r for r in range(min(most, left), 1, -1) if left % r == 0), None)
        if radix is None:
            radix = next(r for r in range(2, left + 1) if left % r == 0)
        radices.insert(0, radix)
        left //= radix
    strides = []
    stride = size
    for radix in radices:
        stride //= radix
        strides.append(stride)
    return list(zip(radices, strides))


def peer(digit, step, radix):
    if radix & (radix - 1) == 0:
        return digit ^ step
    return (digit + step) % radix


def exchange(value, axes, tp, routes, radix, stride, step):
    pairs = []
    for start, end in routes:
        for t in range(tp):
            digit = t // stride % radix
            other = t + (peer(digit, step, radix) - digit) * stride
            pairs.append((start * tp + t, end * tp + other))
    return lax.ppermute(value, axes, pairs)


def block_of(steps, digits, names):
    index = 0
    for step, (radix, stride), name in zip(steps, digits, names):
        index = index + peer(lax.axis_index(name), step, radix) * stride
    return index


def gather_steps(radix, last):
    return [*range(radix)] if last else [*range(radix - 1, -1, -1)]


def scatter_steps(radix, last):
    half = radix // 2 if last else 0
    return [*range(radix - 1, half - 1, -1), *range(half)]


def relative(digits, steps_of):
    found = [()]
    for number, (radix, _) in enumerate(digits):
        found = [one + (step,) for step in steps_of(radix, number == len(digits) - 1) for one in found]
    return found


def spread_kernel(x, weight, *outs, first, layer, digits, names):
    share, _, width = outs[0].shape

    @pl.when(lax.axis_index("section") == layer)
    def _():
        for j, steps in enumerate(relative(digits, scatter_steps)[first : first + share * len(outs)]):
            start = pl.multiple_of(block_of(steps, digits, names) * width, width)
            part = jnp.dot(x[...], weight[0, :, pl.ds(start, width)], preferred_element_type=jnp.float32)
            outs[j // share][j % share] = part.astype(outs[0].dtype)


def first_spread_kernel(x, weight, *rest, outputs, layer, digits, names):
    outs, (here, held, total, x_arrived, arrived) = rest[:outputs], rest[outputs:]
    share, _, width = outs[0].shape
    chunks, pieces = arrived.shape
    depth = weight.shape[1] // chunks
    rows = depth // pieces

    @pl.when(lax.axis_index("section") == layer)
    def _():
        x_copy = pltpu.make_async_copy(x, here, x_arrived)
        x_copy.start()
        copies = []
        for chunk in range(chunks):
            for piece in range(pieces):
                these = pl.ds(chunk * depth + piece * rows, rows)
                copies.append(
                    pltpu.make_async_copy(weight.at[0, these, :], held.at[these, :], arrived.at[chunk, piece])
                )
                copies[-1].start()
        x_copy.wait()
        for chunk in range(chunks):
            for piece in range(pieces):
                copies[chunk * pieces + piece].wait()
            those = slice(chunk * depth, (chunk + 1) * depth)
            for j, steps in enumerate(relative(digits, scatter_steps)):
                start = pl.multiple_of(block_of(steps, digits, names) * width, width)
                part = jnp.dot(here[:, those], held[those, pl.ds(start, width)], preferred_element_type=jnp.float32)
                if chunk > 0:
                    part = part + total[j]
                if chunk < chunks - 1:
                    total[j] = part
                else:
                    outs[j // share][j % share] = part.astype(outs[0].dtype)


def spread(x, weight, first, groups, layer, digits, names):
    rows, depth = x.shape
    count = len(relative(digits, scatter_steps))
    share = count // digits[-1][0]
    width = weight.shape[2] // count
    vmem = pl.BlockSpec(memory_space=pltpu.VMEM)
    outs = [jax.ShapeDtypeStruct((share, rows, width), jnp.bfloat16)] * groups
    if layer > 0:
        return pl.pallas_call(
            functools.partial(spread_kernel, first=first * share, layer=layer, digits=digits, names=names),
            out_shape=outs,
            in_specs=[vmem, vmem],
            out_specs=[vmem] * groups,
            compiler_params=pltpu.CompilerParams(vmem_limit_bytes=8 * 2**20),
            name="spread",
        )(x, pltpu.with_memory_space_constraint(weight, pltpu.VMEM))
    chunks = 2 if depth % 256 == 0 else 1
    return pl.pallas_call(
        functools.partial(first_spread_kernel, outputs=groups, layer=layer, digits=digits, names=names),
        out_shape=outs,
        in_specs=[pl.BlockSpec(memory_space=pltpu.HBM)] * 2,
        out_specs=[vmem] * groups,
        scratch_shapes=[
            pltpu.VMEM(x.shape, x.dtype),
            pltpu.VMEM(weight.shape[1:], weight.dtype),
            pltpu.VMEM((count, rows, width), jnp.float32),
            pltpu.SemaphoreType.DMA,
            pltpu.SemaphoreType.DMA((chunks, 4)),
        ],
        compiler_params=pltpu.CompilerParams(vmem_limit_bytes=20 * 2**20),
        name="first_spread",
    )(
        pltpu.with_memory_space_constraint(x, pltpu.HBM),
        pltpu.with_memory_space_constraint(weight, pltpu.HBM),
    )


def meet_kernel(weight, *rest, first, blocks, layer, digits, names):
    inputs, before, (total, square) = rest[:blocks], rest[blocks:-2], rest[-2:]
    share, _, depth = inputs[0].shape
    inside = lax.axis_index("section") == layer

    @pl.when(inside)
    def _():
        sum_of = before[0][...] if before else jnp.zeros(total.shape, jnp.float32)
        squares = before[1][...] if before else jnp.zeros(square.shape, jnp.float32)
        for j, steps in enumerate(relative(digits, gather_steps)[first : first + share * blocks]):
            x = inputs[j // share][j % share]
            wide = x.astype(jnp.float32)
            squares = squares + jnp.sum(wide * wide, axis=1, keepdims=True)
            start = pl.multiple_of(block_of(steps, digits, names) * depth, depth)
            sum_of = sum_of + jnp.dot(x, weight[0, pl.ds(start, depth), :], preferred_element_type=jnp.float32)
        total[...] = sum_of
        square[...] = squares

    @pl.when(jnp.logical_not(inside))
    def _():
        total[...] = jnp.zeros_like(total)
        square[...] = jnp.full_like(square, -1.0)


def meet(weight, groups, first, before, layer, digits, names):
    rows = groups[0].shape[1]
    vmem = pl.BlockSpec(memory_space=pltpu.VMEM)
    return pl.pallas_call(
        functools.partial(
            meet_kernel, first=first, blocks=len(groups), layer=layer, digits=digits, names=names
        ),
        out_shape=[
            jax.ShapeDtypeStruct((rows, weight.shape[2]), jnp.float32),
            jax.ShapeDtypeStruct((rows, 1), jnp.float32),
        ],
        in_specs=[vmem] * (1 + len(groups) + len(before)),
        out_specs=[vmem, vmem],
        compiler_params=pltpu.CompilerParams(vmem_limit_bytes=8 * 2**20),
        name="meet",
    )(pltpu.with_memory_space_constraint(weight, pltpu.VMEM), *groups, *before)


def tell_kernel(hidden, head, told, *, micro, sections):
    values = jnp.dot(hidden[...], head[...], preferred_element_type=jnp.float32)
    tokens = values.shape[0] // micro
    share = tokens // sections
    repeats = told.shape[0] // sections
    for section in range(sections):
        starts = [m * tokens + section * share for m in range(micro)]
        mine = jnp.concatenate([values[start : start + share] for start in starts], axis=0)
        for i in range(repeats):
            told[section * repeats + i] = mine.astype(told.dtype)


def tell(hidden, head, micro, sections, repeats):
    shape = (sections * repeats, hidden.shape[0] // sections, head.shape[1])
    vmem = pl.BlockSpec(memory_space=pltpu.VMEM)
    return pl.pallas_call(
        functools.partial(tell_kernel, micro=micro, sections=sections),
        out_shape=jax.ShapeDtypeStruct(shape, jnp.bfloat16),
        in_specs=[vmem, vmem],
        out_specs=vmem,
        compiler_params=pltpu.CompilerParams(vmem_limit_bytes=8 * 2**20),
        name="tell",
    )(hidden, head)


def per_device(start_tokens, target_weight, online_weight, head_weight, reward, action_bin, sections, digits, names):
    micro, tokens, width = start_tokens.shape
    tp = 1
    for radix, _ in digits:
        tp *= radix
    everyone = ("section",) + names
    rows = micro * tokens
    features = width * tp
    rounds = len(digits)
    send = functools.partial(exchange, axes=everyone, tp=tp)
    own = start_tokens.reshape(rows, width)
    inner = digits[-1][0]
    half = inner // 2
    for layer in range(sections):
        place = dict(layer=layer, digits=digits, names=names)
        helper = layer - 1 if layer > 0 else min(1, sections - 1)
        both = [(layer, helper), (helper, layer)] if helper != layer else [(layer, layer)]
        if layer > 0:
            own = own + send(own, routes=both, radix=1, stride=1, step=0)

        if layer == 0:
            parts = list(spread(own, online_weight, 0, inner, **place))
        else:
            parts = list(spread(own, online_weight, 0, half, **place)) if half else []
            parts += spread(own, online_weight, half, inner - half, **place)
        stack = own[None]
        for number, (radix, stride) in enumerate(digits):
            final = number == rounds - 1
            routes = both
            if final:
                routes = [(helper, layer)]
                at = layer if number % 2 == 0 else helper
                sent = []
                for step, one in zip(scatter_steps(radix, True), parts):
                    if step > 0 or at != layer:
                        one = send(one, routes=[(layer, at)], radix=radix, stride=stride, step=step)
                    sent.append(one)
                if layer == 0 and rounds > 1:
                    stack, sent[:half] = lax.optimization_barrier((stack, sent[:half]))
            gathered = [
                stack if step == 0 else send(stack, routes=routes, radix=radix, stride=stride, step=step)
                for step in gather_steps(radix, final)
            ]
            if not final:
                gathered, parts[half:] = lax.optimization_barrier((gathered, parts[half:]))
                stack = jnp.concatenate(gathered, axis=0)
        wide = functools.reduce(jnp.add, [one.astype(jnp.float32) for one in sent])
        for number in range(rounds - 2, -1, -1):
            radix, stride = digits[number]
            to = layer if at != layer or number % 2 == 0 else helper
            part = wide.shape[0] // radix
            sent = []
            for i, step in enumerate(scatter_steps(radix, False)):
                one = wide[i * part : (i + 1) * part].astype(jnp.bfloat16)
                if step > 0 or to != at:
                    one = send(one, routes=[(at, to)], radix=radix, stride=stride, step=step)
                sent.append(one)
            at = to
            wide = functools.reduce(jnp.add, [one.astype(jnp.float32) for one in sent])

        before = []
        for begin in range(0, len(gathered), max(1, half)):
            groups = gathered[begin : begin + max(1, half)]
            before = meet(target_weight, groups, begin * groups[0].shape[0], before, **place)
        total, square = before
        update = lax.rsqrt(square / features + 1e-06) * (0.25 * wide[0] + 0.75 * total)
        own = jnp.where(square >= 0.0, own.astype(jnp.float32) + update, 0.0).astype(jnp.bfloat16)

    share_rows = reward.shape[1]
    bins = head_weight.shape[1]
    told = tell(own, head_weight, micro, sections, inner)
    told = lax.all_to_all(told, ("section", names[-1]), split_axis=0, concat_axis=0, tiled=True)
    mine = jnp.sum(told[(sections - 1) * inner :].astype(jnp.float32), axis=0)
    mine = mine.reshape(micro, share_rows, bins)
    for (radix, _), name in zip(digits[:-1], names):
        told = jnp.broadcast_to(mine[None], (radix,) + mine.shape)
        mine = jnp.sum(lax.all_to_all(told, name, split_axis=0, concat_axis=0, tiled=True), axis=0)
    best = jnp.max(mine, axis=2)
    bin_ids = lax.broadcasted_iota(jnp.int32, mine.shape, 2)
    taken = jnp.sum(jnp.where(bin_ids == action_bin[:, :, None], mine, 0.0), axis=2)
    return (reward + 0.98 * best, taken)


def solution(mesh):
    sections, tp = mesh.shape["section"], mesh.shape["tp"]
    digits = digits_of(tp, 4)
    names = tuple(f"tp{number}" for number in range(len(digits)))
    cut = jax.sharding.Mesh(
        mesh.devices.reshape([sections] + [radix for radix, _ in digits]), ("section",) + names
    )
    in_specs = (
        P(None, None, names),
        P("section", None, names),
        P("section", names, None),
        P(names, None),
        P(None, "section"),
        P(None, "section"),
    )
    out_specs = (P(None, "section"), P(None, "section"))
    body = functools.partial(per_device, sections=sections, digits=digits, names=names)
    return jax.shard_map(body, mesh=cut, in_specs=in_specs, out_specs=out_specs, check_vma=False)
```

```python
import functools

import jax
import jax.numpy as jnp
from jax import lax
from jax.experimental import pallas as pl
from jax.experimental.pallas import tpu as pltpu
from jax.sharding import PartitionSpec as P


def digits_of(size, most):
    radices = []
    left = size
    while left > 1:
        radix = next((r for r in range(min(most, left), 1, -1) if left % r == 0), None)
        if radix is None:
            radix = next(r for r in range(2, left + 1) if left % r == 0)
        radices.insert(0, radix)
        left //= radix
    strides = []
    stride = size
    for radix in radices:
        stride //= radix
        strides.append(stride)
    return list(zip(radices, strides))


def peer(digit, step, radix):
    if radix & (radix - 1) == 0:
        return digit ^ step
    return (digit + step) % radix


def exchange(value, axes, tp, routes, radix, stride, step):
    pairs = []
    for start, end in routes:
        for t in range(tp):
            digit = t // stride % radix
            other = t + (peer(digit, step, radix) - digit) * stride
            pairs.append((start * tp + t, end * tp + other))
    return lax.ppermute(value, axes, pairs)


def block_of(steps, digits, names):
    index = 0
    for step, (radix, stride), name in zip(steps, digits, names):
        index = index + peer(lax.axis_index(name), step, radix) * stride
    return index


def gather_steps(radix, last):
    return [*range(radix)] if last else [*range(radix - 1, -1, -1)]


def scatter_steps(radix, last):
    half = radix // 2 if last else 0
    return [*range(radix - 1, half - 1, -1), *range(half)]


def relative(digits, steps_of):
    found = [()]
    for number, (radix, _) in enumerate(digits):
        found = [one + (step,) for step in steps_of(radix, number == len(digits) - 1) for one in found]
    return found


def spread_kernel(x, weight, *outs, first, layer, digits, names):
    share, _, width = outs[0].shape

    @pl.when(lax.axis_index("section") == layer)
    def _():
        for j, steps in enumerate(relative(digits, scatter_steps)[first : first + share * len(outs)]):
            start = pl.multiple_of(block_of(steps, digits, names) * width, width)
            part = jnp.dot(x[...], weight[0, :, pl.ds(start, width)], preferred_element_type=jnp.float32)
            outs[j // share][j % share] = part.astype(outs[0].dtype)


def first_spread_kernel(x, weight, *rest, outputs, layer, digits, names):
    outs, (here, held, total, x_arrived, arrived) = rest[:outputs], rest[outputs:]
    share, _, width = outs[0].shape
    chunks, pieces = arrived.shape
    depth = weight.shape[1] // chunks
    rows = depth // pieces

    @pl.when(lax.axis_index("section") == layer)
    def _():
        x_copy = pltpu.make_async_copy(x, here, x_arrived)
        x_copy.start()
        copies = []
        for chunk in range(chunks):
            for piece in range(pieces):
                these = pl.ds(chunk * depth + piece * rows, rows)
                copies.append(
                    pltpu.make_async_copy(weight.at[0, these, :], held.at[these, :], arrived.at[chunk, piece])
                )
                copies[-1].start()
        x_copy.wait()
        for chunk in range(chunks):
            for piece in range(pieces):
                copies[chunk * pieces + piece].wait()
            those = slice(chunk * depth, (chunk + 1) * depth)
            for j, steps in enumerate(relative(digits, scatter_steps)):
                start = pl.multiple_of(block_of(steps, digits, names) * width, width)
                part = jnp.dot(here[:, those], held[those, pl.ds(start, width)], preferred_element_type=jnp.float32)
                if chunk > 0:
                    part = part + total[j]
                if chunk < chunks - 1:
                    total[j] = part
                else:
                    outs[j // share][j % share] = part.astype(outs[0].dtype)


def spread(x, weight, first, groups, layer, digits, names):
    rows, depth = x.shape
    count = len(relative(digits, scatter_steps))
    share = count // digits[-1][0]
    width = weight.shape[2] // count
    vmem = pl.BlockSpec(memory_space=pltpu.VMEM)
    outs = [jax.ShapeDtypeStruct((share, rows, width), jnp.bfloat16)] * groups
    if layer > 0:
        return pl.pallas_call(
            functools.partial(spread_kernel, first=first * share, layer=layer, digits=digits, names=names),
            out_shape=outs,
            in_specs=[vmem, vmem],
            out_specs=[vmem] * groups,
            compiler_params=pltpu.CompilerParams(vmem_limit_bytes=8 * 2**20),
            name="spread",
        )(x, pltpu.with_memory_space_constraint(weight, pltpu.VMEM))
    chunks = 2 if depth % 256 == 0 else 1
    return pl.pallas_call(
        functools.partial(first_spread_kernel, outputs=groups, layer=layer, digits=digits, names=names),
        out_shape=outs,
        in_specs=[pl.BlockSpec(memory_space=pltpu.HBM)] * 2,
        out_specs=[vmem] * groups,
        scratch_shapes=[
            pltpu.VMEM(x.shape, x.dtype),
            pltpu.VMEM(weight.shape[1:], weight.dtype),
            pltpu.VMEM((count, rows, width), jnp.float32),
            pltpu.SemaphoreType.DMA,
            pltpu.SemaphoreType.DMA((chunks, 4)),
        ],
        compiler_params=pltpu.CompilerParams(vmem_limit_bytes=20 * 2**20),
        name="first_spread",
    )(
        pltpu.with_memory_space_constraint(x, pltpu.HBM),
        pltpu.with_memory_space_constraint(weight, pltpu.HBM),
    )


def meet_kernel(weight, *rest, first, blocks, layer, digits, names):
    inputs, before, (total, square) = rest[:blocks], rest[blocks:-2], rest[-2:]
    share, _, depth = inputs[0].shape
    inside = lax.axis_index("section") == layer

    @pl.when(inside)
    def _():
        sum_of = before[0][...] if before else jnp.zeros(total.shape, jnp.float32)
        squares = before[1][...] if before else jnp.zeros(square.shape, jnp.float32)
        for j, steps in enumerate(relative(digits, gather_steps)[first : first + share * blocks]):
            x = inputs[j // share][j % share]
            wide = x.astype(jnp.float32)
            squares = squares + jnp.sum(wide * wide, axis=1, keepdims=True)
            start = pl.multiple_of(block_of(steps, digits, names) * depth, depth)
            sum_of = sum_of + jnp.dot(x, weight[0, pl.ds(start, depth), :], preferred_element_type=jnp.float32)
        total[...] = sum_of
        square[...] = squares

    @pl.when(jnp.logical_not(inside))
    def _():
        total[...] = jnp.zeros_like(total)
        square[...] = jnp.full_like(square, -1.0)


def meet(weight, groups, first, before, layer, digits, names):
    rows = groups[0].shape[1]
    vmem = pl.BlockSpec(memory_space=pltpu.VMEM)
    return pl.pallas_call(
        functools.partial(
            meet_kernel, first=first, blocks=len(groups), layer=layer, digits=digits, names=names
        ),
        out_shape=[
            jax.ShapeDtypeStruct((rows, weight.shape[2]), jnp.float32),
            jax.ShapeDtypeStruct((rows, 1), jnp.float32),
        ],
        in_specs=[vmem] * (1 + len(groups) + len(before)),
        out_specs=[vmem, vmem],
        compiler_params=pltpu.CompilerParams(vmem_limit_bytes=8 * 2**20),
        name="meet",
    )(pltpu.with_memory_space_constraint(weight, pltpu.VMEM), *groups, *before)


def tell_kernel(hidden, head, *outs, micro):
    values = jnp.dot(hidden[...], head[...], preferred_element_type=jnp.float32)
    tokens = values.shape[0] // micro
    share = tokens // len(outs)
    for section, out in enumerate(outs):
        starts = [m * tokens + section * share for m in range(micro)]
        out[...] = jnp.concatenate([values[start : start + share] for start in starts], axis=0)


def tell(hidden, head, micro, sections):
    shape = (hidden.shape[0] // sections, head.shape[1])
    vmem = pl.BlockSpec(memory_space=pltpu.VMEM)
    return pl.pallas_call(
        functools.partial(tell_kernel, micro=micro),
        out_shape=[jax.ShapeDtypeStruct(shape, jnp.float32)] * sections,
        in_specs=[vmem, vmem],
        out_specs=[vmem] * sections,
        compiler_params=pltpu.CompilerParams(vmem_limit_bytes=8 * 2**20),
        name="tell",
    )(hidden, head)


def paired_sum(terms):
    while len(terms) > 1:
        terms = [a + b for a, b in zip(terms[::2], terms[1::2])] + terms[len(terms) // 2 * 2 :]
    return terms[0]


def per_device(start_tokens, target_weight, online_weight, head_weight, reward, action_bin, sections, digits, names):
    micro, tokens, width = start_tokens.shape
    tp = 1
    for radix, _ in digits:
        tp *= radix
    everyone = ("section",) + names
    rows = micro * tokens
    features = width * tp
    rounds = len(digits)
    send = functools.partial(exchange, axes=everyone, tp=tp)
    own = start_tokens.reshape(rows, width)
    inner = digits[-1][0]
    half = inner // 2
    for layer in range(sections):
        place = dict(layer=layer, digits=digits, names=names)
        helper = layer - 1 if layer > 0 else min(1, sections - 1)
        both = [(layer, helper), (helper, layer)] if helper != layer else [(layer, layer)]
        if layer > 0:
            own = own + send(own, routes=both, radix=1, stride=1, step=0)

        if layer == 0:
            parts = list(spread(own, online_weight, 0, inner, **place))
        else:
            parts = list(spread(own, online_weight, 0, half, **place)) if half else []
            parts += spread(own, online_weight, half, inner - half, **place)
        stack = own[None]
        for number, (radix, stride) in enumerate(digits):
            final = number == rounds - 1
            routes = both
            if final:
                routes = [(helper, layer)]
                at = layer if number % 2 == 0 else helper
                sent = []
                for step, one in zip(scatter_steps(radix, True), parts):
                    if step > 0 or at != layer:
                        one = send(one, routes=[(layer, at)], radix=radix, stride=stride, step=step)
                    sent.append(one)
                if layer == 0 and rounds > 1:
                    stack, sent[:1] = lax.optimization_barrier((stack, sent[:1]))
            gathered = [
                stack if step == 0 else send(stack, routes=routes, radix=radix, stride=stride, step=step)
                for step in gather_steps(radix, final)
            ]
            if not final:
                gathered, parts[half:] = lax.optimization_barrier((gathered, parts[half:]))
                stack = jnp.concatenate(gathered, axis=0)
        wide = functools.reduce(jnp.add, [one.astype(jnp.float32) for one in sent])
        for number in range(rounds - 2, -1, -1):
            radix, stride = digits[number]
            to = layer if at != layer or number % 2 == 0 else helper
            part = wide.shape[0] // radix
            sent = []
            for i, step in enumerate(scatter_steps(radix, False)):
                one = wide[i * part : (i + 1) * part].astype(jnp.bfloat16)
                if step > 0 or to != at:
                    one = send(one, routes=[(at, to)], radix=radix, stride=stride, step=step)
                sent.append(one)
            at = to
            wide = functools.reduce(jnp.add, [one.astype(jnp.float32) for one in sent])

        before = []
        for begin in range(0, len(gathered), max(1, half)):
            groups = gathered[begin : begin + max(1, half)]
            before = meet(target_weight, groups, begin * groups[0].shape[0], before, **place)
        total, square = before
        update = lax.rsqrt(square / features + 1e-06) * (0.25 * wide[0] + 0.75 * total)
        own = jnp.where(square >= 0.0, own.astype(jnp.float32) + update, 0.0).astype(jnp.bfloat16)

    share_rows = reward.shape[1]
    end = sections - 1
    values = tell(own, head_weight, micro, sections)
    mine = values[end]
    for other in range(end):
        mine = mine + send(values[other], routes=[(end, other), (other, end)], radix=1, stride=1, step=0)
    everywhere = [(section, section) for section in range(sections)]
    for radix, stride in digits[::-1]:
        told = mine.astype(jnp.bfloat16)
        far = [send(told, routes=everywhere, radix=radix, stride=stride, step=step) for step in range(radix - 1, 0, -1)]
        mine = paired_sum([term.astype(jnp.float32) for term in [*far, told]])
    mine = mine.reshape(micro, share_rows, head_weight.shape[1])
    best = jnp.max(mine, axis=2)
    bin_ids = lax.broadcasted_iota(jnp.int32, mine.shape, 2)
    taken = jnp.sum(jnp.where(bin_ids == action_bin[:, :, None], mine, 0.0), axis=2)
    return (reward + 0.98 * best, taken)


def solution(mesh):
    sections, tp = mesh.shape["section"], mesh.shape["tp"]
    digits = digits_of(tp, 4)
    names = tuple(f"tp{number}" for number in range(len(digits)))
    cut = jax.sharding.Mesh(
        mesh.devices.reshape([sections] + [radix for radix, _ in digits]), ("section",) + names
    )
    in_specs = (
        P(None, None, names),
        P("section", None, names),
        P("section", names, None),
        P(names, None),
        P(None, "section"),
        P(None, "section"),
    )
    out_specs = (P(None, "section"), P(None, "section"))
    body = functools.partial(per_device, sections=sections, digits=digits, names=names)
    return jax.shard_map(body, mesh=cut, in_specs=in_specs, out_specs=out_specs, check_vma=False)
```

```python
import functools

import jax
import jax.numpy as jnp
from jax import lax
from jax.experimental import pallas as pl
from jax.experimental.pallas import tpu as pltpu
from jax.sharding import PartitionSpec as P


def digits_of(size, most):
    radices = []
    left = size
    while left > 1:
        radix = next((r for r in range(min(most, left), 1, -1) if left % r == 0), None)
        if radix is None:
            radix = next(r for r in range(2, left + 1) if left % r == 0)
        radices.insert(0, radix)
        left //= radix
    strides = []
    stride = size
    for radix in radices:
        stride //= radix
        strides.append(stride)
    return list(zip(radices, strides))


def peer(digit, step, radix):
    if radix & (radix - 1) == 0:
        return digit ^ step
    return (digit + step) % radix


def exchange(value, axes, tp, routes, radix, stride, step):
    pairs = []
    for start, end in routes:
        for t in range(tp):
            digit = t // stride % radix
            other = t + (peer(digit, step, radix) - digit) * stride
            pairs.append((start * tp + t, end * tp + other))
    return lax.ppermute(value, axes, pairs)


def block_of(steps, digits, names):
    index = 0
    for step, (radix, stride), name in zip(steps, digits, names):
        index = index + peer(lax.axis_index(name), step, radix) * stride
    return index


def gather_steps(radix, last):
    return [*range(radix)] if last else [*range(radix - 1, -1, -1)]


def scatter_steps(radix, last):
    return [*range(radix - 1, -1, -1)]


def relative(digits, steps_of):
    found = [()]
    for number, (radix, _) in enumerate(digits):
        found = [one + (step,) for step in steps_of(radix, number == len(digits) - 1) for one in found]
    return found


def spread_kernel(x, weight, *outs, first, layer, digits, names):
    share, _, width = outs[0].shape

    @pl.when(lax.axis_index("section") == layer)
    def _():
        for j, steps in enumerate(relative(digits, scatter_steps)[first : first + share * len(outs)]):
            start = pl.multiple_of(block_of(steps, digits, names) * width, width)
            part = jnp.dot(x[...], weight[0, :, pl.ds(start, width)], preferred_element_type=jnp.float32)
            outs[j // share][j % share] = part.astype(outs[0].dtype)


def first_spread_kernel(x, weight, *rest, outputs, layer, digits, names):
    outs, (here, held, total, x_arrived, arrived) = rest[:outputs], rest[outputs:]
    share, _, width = outs[0].shape
    chunks, pieces = arrived.shape
    depth = weight.shape[1] // chunks
    rows = depth // pieces

    @pl.when(lax.axis_index("section") == layer)
    def _():
        x_copy = pltpu.make_async_copy(x, here, x_arrived)
        x_copy.start()
        copies = []
        for chunk in range(chunks):
            for piece in range(pieces):
                these = pl.ds(chunk * depth + piece * rows, rows)
                copies.append(
                    pltpu.make_async_copy(weight.at[0, these, :], held.at[these, :], arrived.at[chunk, piece])
                )
                copies[-1].start()
        x_copy.wait()
        for chunk in range(chunks):
            for piece in range(pieces):
                copies[chunk * pieces + piece].wait()
            those = slice(chunk * depth, (chunk + 1) * depth)
            for j, steps in enumerate(relative(digits, scatter_steps)):
                start = pl.multiple_of(block_of(steps, digits, names) * width, width)
                part = jnp.dot(here[:, those], held[those, pl.ds(start, width)], preferred_element_type=jnp.float32)
                if chunk > 0:
                    part = part + total[j]
                if chunk < chunks - 1:
                    total[j] = part
                else:
                    outs[j // share][j % share] = part.astype(outs[0].dtype)


def spread(x, weight, first, groups, layer, digits, names):
    rows, depth = x.shape
    count = len(relative(digits, scatter_steps))
    share = count // digits[-1][0]
    width = weight.shape[2] // count
    vmem = pl.BlockSpec(memory_space=pltpu.VMEM)
    outs = [jax.ShapeDtypeStruct((share, rows, width), jnp.bfloat16)] * groups
    if layer > 0:
        return pl.pallas_call(
            functools.partial(spread_kernel, first=first * share, layer=layer, digits=digits, names=names),
            out_shape=outs,
            in_specs=[vmem, vmem],
            out_specs=[vmem] * groups,
            compiler_params=pltpu.CompilerParams(vmem_limit_bytes=8 * 2**20),
            name="spread",
        )(x, pltpu.with_memory_space_constraint(weight, pltpu.VMEM))
    chunks = 2 if depth % 256 == 0 else 1
    return pl.pallas_call(
        functools.partial(first_spread_kernel, outputs=groups, layer=layer, digits=digits, names=names),
        out_shape=outs,
        in_specs=[pl.BlockSpec(memory_space=pltpu.HBM)] * 2,
        out_specs=[vmem] * groups,
        scratch_shapes=[
            pltpu.VMEM(x.shape, x.dtype),
            pltpu.VMEM(weight.shape[1:], weight.dtype),
            pltpu.VMEM((count, rows, width), jnp.float32),
            pltpu.SemaphoreType.DMA,
            pltpu.SemaphoreType.DMA((chunks, 4)),
        ],
        compiler_params=pltpu.CompilerParams(vmem_limit_bytes=20 * 2**20),
        name="first_spread",
    )(
        pltpu.with_memory_space_constraint(x, pltpu.HBM),
        pltpu.with_memory_space_constraint(weight, pltpu.HBM),
    )


def meet_kernel(weight, *rest, first, blocks, layer, digits, names):
    inputs, before, (total, square) = rest[:blocks], rest[blocks:-2], rest[-2:]
    share, _, depth = inputs[0].shape
    inside = lax.axis_index("section") == layer

    @pl.when(inside)
    def _():
        sum_of = before[0][...] if before else jnp.zeros(total.shape, jnp.float32)
        squares = before[1][...] if before else jnp.zeros(square.shape, jnp.float32)
        for j, steps in enumerate(relative(digits, gather_steps)[first : first + share * blocks]):
            x = inputs[j // share][j % share]
            wide = x.astype(jnp.float32)
            squares = squares + jnp.sum(wide * wide, axis=1, keepdims=True)
            start = pl.multiple_of(block_of(steps, digits, names) * depth, depth)
            sum_of = sum_of + jnp.dot(x, weight[0, pl.ds(start, depth), :], preferred_element_type=jnp.float32)
        total[...] = sum_of
        square[...] = squares

    @pl.when(jnp.logical_not(inside))
    def _():
        total[...] = jnp.zeros_like(total)
        square[...] = jnp.full_like(square, -1.0)


def meet(weight, groups, first, before, layer, digits, names):
    rows = groups[0].shape[1]
    vmem = pl.BlockSpec(memory_space=pltpu.VMEM)
    return pl.pallas_call(
        functools.partial(
            meet_kernel, first=first, blocks=len(groups), layer=layer, digits=digits, names=names
        ),
        out_shape=[
            jax.ShapeDtypeStruct((rows, weight.shape[2]), jnp.float32),
            jax.ShapeDtypeStruct((rows, 1), jnp.float32),
        ],
        in_specs=[vmem] * (1 + len(groups) + len(before)),
        out_specs=[vmem, vmem],
        compiler_params=pltpu.CompilerParams(vmem_limit_bytes=8 * 2**20),
        name="meet",
    )(pltpu.with_memory_space_constraint(weight, pltpu.VMEM), *groups, *before)


def tell_kernel(hidden, head, *outs, micro):
    values = jnp.dot(hidden[...], head[...], preferred_element_type=jnp.float32)
    tokens = values.shape[0] // micro
    share = tokens // len(outs)
    for section, out in enumerate(outs):
        starts = [m * tokens + section * share for m in range(micro)]
        out[...] = jnp.concatenate([values[start : start + share] for start in starts], axis=0)


def tell(hidden, head, micro, sections):
    shape = (hidden.shape[0] // sections, head.shape[1])
    vmem = pl.BlockSpec(memory_space=pltpu.VMEM)
    return pl.pallas_call(
        functools.partial(tell_kernel, micro=micro),
        out_shape=[jax.ShapeDtypeStruct(shape, jnp.float32)] * sections,
        in_specs=[vmem, vmem],
        out_specs=[vmem] * sections,
        compiler_params=pltpu.CompilerParams(vmem_limit_bytes=8 * 2**20),
        name="tell",
    )(hidden, head)


def finish_kernel(*refs, terms):
    values = paired_sum([ref[...].astype(jnp.float32) for ref in refs[:terms]])
    reward, action, best, taken = refs[terms:]
    values = values.reshape(*reward.shape, values.shape[1])
    bins = lax.broadcasted_iota(jnp.int32, values.shape, 2)
    picked = jnp.where(bins == action[...][:, :, None], values, 0.0)
    best[...] = reward[...] + 0.98 * jnp.max(values, axis=2)
    taken[...] = jnp.sum(picked, axis=2)


def finish(terms, reward, action):
    vmem = pl.BlockSpec(memory_space=pltpu.VMEM)
    return pl.pallas_call(
        functools.partial(finish_kernel, terms=len(terms)),
        out_shape=[jax.ShapeDtypeStruct(reward.shape, jnp.float32)] * 2,
        in_specs=[vmem] * (len(terms) + 2),
        out_specs=[vmem] * 2,
        compiler_params=pltpu.CompilerParams(vmem_limit_bytes=8 * 2**20),
        name="finish",
    )(*terms, reward, action)


def paired_sum(terms):
    while len(terms) > 1:
        terms = [a + b for a, b in zip(terms[::2], terms[1::2])] + terms[len(terms) // 2 * 2 :]
    return terms[0]


def per_device(start_tokens, target_weight, online_weight, head_weight, reward, action_bin, sections, digits, names):
    micro, tokens, width = start_tokens.shape
    tp = 1
    for radix, _ in digits:
        tp *= radix
    everyone = ("section",) + names
    rows = micro * tokens
    features = width * tp
    rounds = len(digits)
    send = functools.partial(exchange, axes=everyone, tp=tp)
    own = start_tokens.reshape(rows, width)
    inner = digits[-1][0]
    half = inner // 2
    for layer in range(sections):
        place = dict(layer=layer, digits=digits, names=names)
        helper = layer - 1 if layer > 0 else min(1, sections - 1)
        both = [(layer, helper), (helper, layer)] if helper != layer else [(layer, layer)]
        if layer > 0:
            own = own + send(own, routes=both, radix=1, stride=1, step=0)

        if layer == 0:
            parts = list(spread(own, online_weight, 0, inner, **place))
        else:
            parts = list(spread(own, online_weight, 0, half, **place)) if half else []
            parts += spread(own, online_weight, half, inner - half, **place)
        stack = own[None]
        for number, (radix, stride) in enumerate(digits):
            final = number == rounds - 1
            routes = both
            if final:
                routes = [(helper, layer)]
                at = layer if number % 2 == 0 else helper
                sent = []
                for step, one in zip(scatter_steps(radix, True), parts):
                    if step > 0 or at != layer:
                        one = send(one, routes=[(layer, at)], radix=radix, stride=stride, step=step)
                    sent.append(one)
                if layer == 0 and rounds > 1:
                    stack, sent[:1] = lax.optimization_barrier((stack, sent[:1]))
            gathered = [
                stack if step == 0 else send(stack, routes=routes, radix=radix, stride=stride, step=step)
                for step in gather_steps(radix, final)
            ]
            if not final:
                gathered, parts[-1:] = lax.optimization_barrier((gathered, parts[-1:]))
                stack = jnp.concatenate(gathered, axis=0)
        wide = functools.reduce(jnp.add, [one.astype(jnp.float32) for one in sent])
        for number in range(rounds - 2, -1, -1):
            radix, stride = digits[number]
            to = layer if at != layer or number % 2 == 0 else helper
            part = wide.shape[0] // radix
            sent = []
            for i, step in enumerate(scatter_steps(radix, False)):
                one = wide[i * part : (i + 1) * part].astype(jnp.bfloat16)
                if step > 0 or to != at:
                    one = send(one, routes=[(at, to)], radix=radix, stride=stride, step=step)
                sent.append(one)
            at = to
            wide = functools.reduce(jnp.add, [one.astype(jnp.float32) for one in sent])

        before = []
        for begin in range(0, len(gathered), max(1, half)):
            groups = gathered[begin : begin + max(1, half)]
            before = meet(target_weight, groups, begin * groups[0].shape[0], before, **place)
        total, square = before
        update = lax.rsqrt(square / features + 1e-06) * (0.25 * wide[0] + 0.75 * total)
        own = jnp.where(square >= 0.0, own.astype(jnp.float32) + update, 0.0).astype(jnp.bfloat16)

    end = sections - 1
    values = tell(own, head_weight, micro, sections)
    mine = values[end]
    for other in range(end):
        mine = mine + send(values[other], routes=[(end, other), (other, end)], radix=1, stride=1, step=0)
    everywhere = [(section, section) for section in range(sections)]
    terms = [mine]
    for radix, stride in digits[::-1]:
        told = paired_sum([term.astype(jnp.float32) for term in terms]).astype(jnp.bfloat16)
        terms = [send(told, routes=everywhere, radix=radix, stride=stride, step=step) for step in range(radix - 1, 0, -1)]
        terms.append(told)
    return tuple(finish(terms, reward, action_bin))


def solution(mesh):
    sections, tp = mesh.shape["section"], mesh.shape["tp"]
    digits = digits_of(tp, 4)
    names = tuple(f"tp{number}" for number in range(len(digits)))
    cut = jax.sharding.Mesh(
        mesh.devices.reshape([sections] + [radix for radix, _ in digits]), ("section",) + names
    )
    in_specs = (
        P(None, None, names),
        P("section", None, names),
        P("section", names, None),
        P(names, None),
        P(None, "section"),
        P(None, "section"),
    )
    out_specs = (P(None, "section"), P(None, "section"))
    body = functools.partial(per_device, sections=sections, digits=digits, names=names)
    return jax.shard_map(body, mesh=cut, in_specs=in_specs, out_specs=out_specs, check_vma=False)
```

```python
import functools

import jax
import jax.numpy as jnp
from jax import lax
from jax.experimental import pallas as pl
from jax.experimental.pallas import tpu as pltpu
from jax.sharding import PartitionSpec as P


def digits_of(size, most):
    radices = []
    left = size
    while left > 1:
        radix = next((r for r in range(min(most, left), 1, -1) if left % r == 0), None)
        if radix is None:
            radix = next(r for r in range(2, left + 1) if left % r == 0)
        radices.insert(0, radix)
        left //= radix
    strides = []
    stride = size
    for radix in radices:
        stride //= radix
        strides.append(stride)
    return list(zip(radices, strides))


def peer(digit, step, radix):
    if radix & (radix - 1) == 0:
        return digit ^ step
    return (digit + step) % radix


def exchange(value, axes, tp, routes, radix, stride, step):
    pairs = []
    for start, end in routes:
        for t in range(tp):
            digit = t // stride % radix
            other = t + (peer(digit, step, radix) - digit) * stride
            pairs.append((start * tp + t, end * tp + other))
    return lax.ppermute(value, axes, pairs)


def block_of(steps, digits, names):
    index = 0
    for step, (radix, stride), name in zip(steps, digits, names):
        index = index + peer(lax.axis_index(name), step, radix) * stride
    return index


def gather_steps(radix, last):
    return [*range(radix)] if last else [*range(radix - 1, -1, -1)]


def scatter_steps(radix, last):
    return [*range(radix - 1, -1, -1)]


def relative(digits, steps_of):
    found = [()]
    for number, (radix, _) in enumerate(digits):
        found = [one + (step,) for step in steps_of(radix, number == len(digits) - 1) for one in found]
    return found


def spread_kernel(x, weight, *outs, first, layer, digits, names):
    share, _, width = outs[0].shape

    @pl.when(lax.axis_index("section") == layer)
    def _():
        for j, steps in enumerate(relative(digits, scatter_steps)[first : first + share * len(outs)]):
            start = pl.multiple_of(block_of(steps, digits, names) * width, width)
            part = jnp.dot(x[...], weight[0, :, pl.ds(start, width)], preferred_element_type=jnp.float32)
            outs[j // share][j % share] = part.astype(outs[0].dtype)


def first_spread_kernel(x, weight, *rest, outputs, layer, digits, names):
    outs, (here, held, total, x_arrived, arrived) = rest[:outputs], rest[outputs:]
    share, _, width = outs[0].shape
    chunks, pieces = arrived.shape
    depth = weight.shape[1] // chunks
    rows = depth // pieces

    @pl.when(lax.axis_index("section") == layer)
    def _():
        x_copy = pltpu.make_async_copy(x, here, x_arrived)
        x_copy.start()
        copies = []
        for chunk in range(chunks):
            for piece in range(pieces):
                these = pl.ds(chunk * depth + piece * rows, rows)
                copies.append(
                    pltpu.make_async_copy(weight.at[0, these, :], held.at[these, :], arrived.at[chunk, piece])
                )
                copies[-1].start()
        x_copy.wait()
        for chunk in range(chunks):
            for piece in range(pieces):
                copies[chunk * pieces + piece].wait()
            those = slice(chunk * depth, (chunk + 1) * depth)
            for j, steps in enumerate(relative(digits, scatter_steps)):
                start = pl.multiple_of(block_of(steps, digits, names) * width, width)
                part = jnp.dot(here[:, those], held[those, pl.ds(start, width)], preferred_element_type=jnp.float32)
                if chunk > 0:
                    part = part + total[j]
                if chunk < chunks - 1:
                    total[j] = part
                else:
                    outs[j // share][j % share] = part.astype(outs[0].dtype)


def spread(x, weight, first, groups, layer, digits, names):
    rows, depth = x.shape
    count = len(relative(digits, scatter_steps))
    share = count // digits[-1][0]
    width = weight.shape[2] // count
    vmem = pl.BlockSpec(memory_space=pltpu.VMEM)
    outs = [jax.ShapeDtypeStruct((share, rows, width), jnp.bfloat16)] * groups
    if layer > 0:
        return pl.pallas_call(
            functools.partial(spread_kernel, first=first * share, layer=layer, digits=digits, names=names),
            out_shape=outs,
            in_specs=[vmem, vmem],
            out_specs=[vmem] * groups,
            compiler_params=pltpu.CompilerParams(vmem_limit_bytes=8 * 2**20),
            name="spread",
        )(x, pltpu.with_memory_space_constraint(weight, pltpu.VMEM))
    chunks = 2 if depth % 256 == 0 else 1
    return pl.pallas_call(
        functools.partial(first_spread_kernel, outputs=groups, layer=layer, digits=digits, names=names),
        out_shape=outs,
        in_specs=[pl.BlockSpec(memory_space=pltpu.HBM)] * 2,
        out_specs=[vmem] * groups,
        scratch_shapes=[
            pltpu.VMEM(x.shape, x.dtype),
            pltpu.VMEM(weight.shape[1:], weight.dtype),
            pltpu.VMEM((count, rows, width), jnp.float32),
            pltpu.SemaphoreType.DMA,
            pltpu.SemaphoreType.DMA((chunks, 4)),
        ],
        compiler_params=pltpu.CompilerParams(vmem_limit_bytes=20 * 2**20),
        name="first_spread",
    )(
        pltpu.with_memory_space_constraint(x, pltpu.HBM),
        pltpu.with_memory_space_constraint(weight, pltpu.HBM),
    )


def meet_kernel(weight, *rest, first, blocks, layer, digits, names):
    inputs, before, (total, square) = rest[:blocks], rest[blocks:-2], rest[-2:]
    share, _, depth = inputs[0].shape
    inside = lax.axis_index("section") == layer

    @pl.when(inside)
    def _():
        sum_of = before[0][...] if before else jnp.zeros(total.shape, jnp.float32)
        squares = before[1][...] if before else jnp.zeros(square.shape, jnp.float32)
        for j, steps in enumerate(relative(digits, gather_steps)[first : first + share * blocks]):
            x = inputs[j // share][j % share]
            wide = x.astype(jnp.float32)
            squares = squares + jnp.sum(wide * wide, axis=1, keepdims=True)
            start = pl.multiple_of(block_of(steps, digits, names) * depth, depth)
            sum_of = sum_of + jnp.dot(x, weight[0, pl.ds(start, depth), :], preferred_element_type=jnp.float32)
        total[...] = sum_of
        square[...] = squares

    @pl.when(jnp.logical_not(inside))
    def _():
        total[...] = jnp.zeros_like(total)
        square[...] = jnp.full_like(square, -1.0)


def meet(weight, groups, first, before, layer, digits, names):
    rows = groups[0].shape[1]
    vmem = pl.BlockSpec(memory_space=pltpu.VMEM)
    return pl.pallas_call(
        functools.partial(
            meet_kernel, first=first, blocks=len(groups), layer=layer, digits=digits, names=names
        ),
        out_shape=[
            jax.ShapeDtypeStruct((rows, weight.shape[2]), jnp.float32),
            jax.ShapeDtypeStruct((rows, 1), jnp.float32),
        ],
        in_specs=[vmem] * (1 + len(groups) + len(before)),
        out_specs=[vmem, vmem],
        compiler_params=pltpu.CompilerParams(vmem_limit_bytes=8 * 2**20),
        name="meet",
    )(pltpu.with_memory_space_constraint(weight, pltpu.VMEM), *groups, *before)


def tell_kernel(hidden, head, *outs, micro):
    values = jnp.dot(hidden[...], head[...], preferred_element_type=jnp.float32)
    tokens = values.shape[0] // micro
    share = tokens // len(outs)
    for section, out in enumerate(outs):
        starts = [m * tokens + section * share for m in range(micro)]
        out[...] = jnp.concatenate([values[start : start + share] for start in starts], axis=0)


def tell(hidden, head, micro, sections):
    shape = (hidden.shape[0] // sections, head.shape[1])
    vmem = pl.BlockSpec(memory_space=pltpu.VMEM)
    return pl.pallas_call(
        functools.partial(tell_kernel, micro=micro),
        out_shape=[jax.ShapeDtypeStruct(shape, jnp.float32)] * sections,
        in_specs=[vmem, vmem],
        out_specs=[vmem] * sections,
        compiler_params=pltpu.CompilerParams(vmem_limit_bytes=8 * 2**20),
        name="tell",
    )(hidden, head)


def finish_kernel(*refs, terms):
    values = paired_sum([ref[...] for ref in refs[:terms]])
    reward, action, best, taken = refs[terms:]
    values = values.reshape(*reward.shape, values.shape[1])
    bins = lax.broadcasted_iota(jnp.int32, values.shape, 2)
    picked = jnp.where(bins == action[...][:, :, None], values, 0.0)
    best[...] = reward[...] + 0.98 * jnp.max(values, axis=2)
    taken[...] = jnp.sum(picked, axis=2)


def finish(terms, reward, action):
    vmem = pl.BlockSpec(memory_space=pltpu.VMEM)
    return pl.pallas_call(
        functools.partial(finish_kernel, terms=len(terms)),
        out_shape=[jax.ShapeDtypeStruct(reward.shape, jnp.float32)] * 2,
        in_specs=[vmem] * (len(terms) + 2),
        out_specs=[vmem] * 2,
        compiler_params=pltpu.CompilerParams(vmem_limit_bytes=8 * 2**20),
        name="finish",
    )(*terms, reward, action)


def paired_sum(terms):
    while len(terms) > 1:
        terms = [a + b for a, b in zip(terms[::2], terms[1::2])] + terms[len(terms) // 2 * 2 :]
    return terms[0]


def per_device(start_tokens, target_weight, online_weight, head_weight, reward, action_bin, sections, digits, names):
    micro, tokens, width = start_tokens.shape
    tp = 1
    for radix, _ in digits:
        tp *= radix
    everyone = ("section",) + names
    rows = micro * tokens
    features = width * tp
    rounds = len(digits)
    send = functools.partial(exchange, axes=everyone, tp=tp)
    own = start_tokens.reshape(rows, width)
    inner = digits[-1][0]
    half = inner // 2
    for layer in range(sections):
        place = dict(layer=layer, digits=digits, names=names)
        helper = layer - 1 if layer > 0 else min(1, sections - 1)
        both = [(layer, helper), (helper, layer)] if helper != layer else [(layer, layer)]
        if layer > 0:
            own = own + send(own, routes=both, radix=1, stride=1, step=0)

        if layer == 0:
            parts = list(spread(own, online_weight, 0, inner, **place))
        else:
            parts = list(spread(own, online_weight, 0, half, **place)) if half else []
            parts += spread(own, online_weight, half, inner - half, **place)
        stack = own[None]
        for number, (radix, stride) in enumerate(digits):
            final = number == rounds - 1
            routes = both
            if final:
                routes = [(helper, layer)]
                at = layer if number % 2 == 0 else helper
                sent = []
                for step, one in zip(scatter_steps(radix, True), parts):
                    if step > 0 or at != layer:
                        one = send(one, routes=[(layer, at)], radix=radix, stride=stride, step=step)
                    sent.append(one)
                if layer == 0 and rounds > 1:
                    stack, sent[:1] = lax.optimization_barrier((stack, sent[:1]))
            gathered = [
                stack if step == 0 else send(stack, routes=routes, radix=radix, stride=stride, step=step)
                for step in gather_steps(radix, final)
            ]
            if not final:
                gathered, parts[-1:] = lax.optimization_barrier((gathered, parts[-1:]))
                stack = jnp.concatenate(gathered, axis=0)
        wide = functools.reduce(jnp.add, [one.astype(jnp.float32) for one in sent])
        for number in range(rounds - 2, -1, -1):
            radix, stride = digits[number]
            to = layer if at != layer or number % 2 == 0 else helper
            part = wide.shape[0] // radix
            sent = []
            for i, step in enumerate(scatter_steps(radix, False)):
                one = wide[i * part : (i + 1) * part].astype(jnp.bfloat16)
                if step > 0 or to != at:
                    one = send(one, routes=[(at, to)], radix=radix, stride=stride, step=step)
                sent.append(one)
            at = to
            wide = functools.reduce(jnp.add, [one.astype(jnp.float32) for one in sent])

        before = []
        for begin in range(0, len(gathered), max(1, half)):
            groups = gathered[begin : begin + max(1, half)]
            before = meet(target_weight, groups, begin * groups[0].shape[0], before, **place)
        total, square = before
        update = lax.rsqrt(square / features + 1e-06) * (0.25 * wide[0] + 0.75 * total)
        own = jnp.where(square >= 0.0, own.astype(jnp.float32) + update, 0.0).astype(jnp.bfloat16)

    end = sections - 1
    values = tell(own, head_weight, micro, sections)
    mine = values[end]
    for other in range(end):
        mine = mine + send(values[other], routes=[(end, other), (other, end)], radix=1, stride=1, step=0)
    everywhere = [(section, section) for section in range(sections)]
    terms = [mine]
    for radix, stride in digits_of(tp, 2)[::-1]:
        told = paired_sum(terms)
        terms = [send(told, routes=everywhere, radix=radix, stride=stride, step=step) for step in range(radix - 1, 0, -1)]
        terms.append(told)
    return tuple(finish(terms, reward, action_bin))


def solution(mesh):
    sections, tp = mesh.shape["section"], mesh.shape["tp"]
    digits = digits_of(tp, 4)
    names = tuple(f"tp{number}" for number in range(len(digits)))
    cut = jax.sharding.Mesh(
        mesh.devices.reshape([sections] + [radix for radix, _ in digits]), ("section",) + names
    )
    in_specs = (
        P(None, None, names),
        P("section", None, names),
        P("section", names, None),
        P(names, None),
        P(None, "section"),
        P(None, "section"),
    )
    out_specs = (P(None, "section"), P(None, "section"))
    body = functools.partial(per_device, sections=sections, digits=digits, names=names)
    return jax.shard_map(body, mesh=cut, in_specs=in_specs, out_specs=out_specs, check_vma=False)
```

```python
import functools

import jax
import jax.numpy as jnp
from jax import lax
from jax.experimental import pallas as pl
from jax.experimental.pallas import tpu as pltpu
from jax.sharding import PartitionSpec as P


def digits_of(size, most):
    radices = []
    left = size
    while left > 1:
        radix = next((r for r in range(min(most, left), 1, -1) if left % r == 0), None)
        if radix is None:
            radix = next(r for r in range(2, left + 1) if left % r == 0)
        radices.insert(0, radix)
        left //= radix
    strides = []
    stride = size
    for radix in radices:
        stride //= radix
        strides.append(stride)
    return list(zip(radices, strides))


def peer(digit, step, radix):
    if radix & (radix - 1) == 0:
        return digit ^ step
    return (digit + step) % radix


def exchange(value, axes, tp, routes, radix, stride, step):
    pairs = []
    for start, end in routes:
        for t in range(tp):
            digit = t // stride % radix
            other = t + (peer(digit, step, radix) - digit) * stride
            pairs.append((start * tp + t, end * tp + other))
    return lax.ppermute(value, axes, pairs)


def block_of(steps, digits, names):
    index = 0
    for step, (radix, stride), name in zip(steps, digits, names):
        index = index + peer(lax.axis_index(name), step, radix) * stride
    return index


def gather_steps(radix, last):
    if not last:
        return [*range(radix - 1, -1, -1)]
    return [0, *range(2, radix), 1][:radix]


def scatter_steps(radix, last):
    return [*range(radix - 1, -1, -1)]


def relative(digits, steps_of):
    found = [()]
    for number, (radix, _) in enumerate(digits):
        found = [one + (step,) for step in steps_of(radix, number == len(digits) - 1) for one in found]
    return found


def spread_kernel(x, weight, *outs, first, layer, digits, names):
    share, _, width = outs[0].shape

    @pl.when(lax.axis_index("section") == layer)
    def _():
        for j, steps in enumerate(relative(digits, scatter_steps)[first : first + share * len(outs)]):
            start = pl.multiple_of(block_of(steps, digits, names) * width, width)
            part = jnp.dot(x[...], weight[0, :, pl.ds(start, width)], preferred_element_type=jnp.float32)
            outs[j // share][j % share] = part.astype(outs[0].dtype)


def first_spread_kernel(x, weight, *rest, outputs, layer, digits, names):
    outs, (here, held, total, x_arrived, arrived) = rest[:outputs], rest[outputs:]
    share, _, width = outs[0].shape
    chunks, pieces = arrived.shape
    depth = weight.shape[1] // chunks
    rows = depth // pieces

    @pl.when(lax.axis_index("section") == layer)
    def _():
        x_copy = pltpu.make_async_copy(x, here, x_arrived)
        x_copy.start()
        copies = []
        for chunk in range(chunks):
            for piece in range(pieces):
                these = pl.ds(chunk * depth + piece * rows, rows)
                copies.append(
                    pltpu.make_async_copy(weight.at[0, these, :], held.at[these, :], arrived.at[chunk, piece])
                )
                copies[-1].start()
        x_copy.wait()
        for chunk in range(chunks):
            for piece in range(pieces):
                copies[chunk * pieces + piece].wait()
            those = slice(chunk * depth, (chunk + 1) * depth)
            for j, steps in enumerate(relative(digits, scatter_steps)):
                start = pl.multiple_of(block_of(steps, digits, names) * width, width)
                part = jnp.dot(here[:, those], held[those, pl.ds(start, width)], preferred_element_type=jnp.float32)
                if chunk > 0:
                    part = part + total[j]
                if chunk < chunks - 1:
                    total[j] = part
                else:
                    outs[j // share][j % share] = part.astype(outs[0].dtype)


def spread(x, weight, first, groups, layer, digits, names):
    rows, depth = x.shape
    count = len(relative(digits, scatter_steps))
    share = count // digits[-1][0]
    width = weight.shape[2] // count
    vmem = pl.BlockSpec(memory_space=pltpu.VMEM)
    outs = [jax.ShapeDtypeStruct((share, rows, width), jnp.bfloat16)] * groups
    if layer > 0:
        return pl.pallas_call(
            functools.partial(spread_kernel, first=first * share, layer=layer, digits=digits, names=names),
            out_shape=outs,
            in_specs=[vmem, vmem],
            out_specs=[vmem] * groups,
            compiler_params=pltpu.CompilerParams(vmem_limit_bytes=8 * 2**20),
            name="spread",
        )(x, pltpu.with_memory_space_constraint(weight, pltpu.VMEM))
    chunks = 2 if depth % 256 == 0 else 1
    return pl.pallas_call(
        functools.partial(first_spread_kernel, outputs=groups, layer=layer, digits=digits, names=names),
        out_shape=outs,
        in_specs=[pl.BlockSpec(memory_space=pltpu.HBM)] * 2,
        out_specs=[vmem] * groups,
        scratch_shapes=[
            pltpu.VMEM(x.shape, x.dtype),
            pltpu.VMEM(weight.shape[1:], weight.dtype),
            pltpu.VMEM((count, rows, width), jnp.float32),
            pltpu.SemaphoreType.DMA,
            pltpu.SemaphoreType.DMA((chunks, 4)),
        ],
        compiler_params=pltpu.CompilerParams(vmem_limit_bytes=20 * 2**20),
        name="first_spread",
    )(
        pltpu.with_memory_space_constraint(x, pltpu.HBM),
        pltpu.with_memory_space_constraint(weight, pltpu.HBM),
    )


def meet_kernel(weight, *rest, first, blocks, layer, digits, names):
    inputs, before, (total, square) = rest[:blocks], rest[blocks:-2], rest[-2:]
    share, _, depth = inputs[0].shape
    inside = lax.axis_index("section") == layer

    @pl.when(inside)
    def _():
        sum_of = before[0][...] if before else jnp.zeros(total.shape, jnp.float32)
        squares = before[1][...] if before else jnp.zeros(square.shape, jnp.float32)
        for j, steps in enumerate(relative(digits, gather_steps)[first : first + share * blocks]):
            x = inputs[j // share][j % share]
            wide = x.astype(jnp.float32)
            squares = squares + jnp.sum(wide * wide, axis=1, keepdims=True)
            start = pl.multiple_of(block_of(steps, digits, names) * depth, depth)
            sum_of = sum_of + jnp.dot(x, weight[0, pl.ds(start, depth), :], preferred_element_type=jnp.float32)
        total[...] = sum_of
        square[...] = squares

    @pl.when(jnp.logical_not(inside))
    def _():
        total[...] = jnp.zeros_like(total)
        square[...] = jnp.full_like(square, -1.0)


def meet(weight, groups, first, before, layer, digits, names):
    rows = groups[0].shape[1]
    vmem = pl.BlockSpec(memory_space=pltpu.VMEM)
    return pl.pallas_call(
        functools.partial(
            meet_kernel, first=first, blocks=len(groups), layer=layer, digits=digits, names=names
        ),
        out_shape=[
            jax.ShapeDtypeStruct((rows, weight.shape[2]), jnp.float32),
            jax.ShapeDtypeStruct((rows, 1), jnp.float32),
        ],
        in_specs=[vmem] * (1 + len(groups) + len(before)),
        out_specs=[vmem, vmem],
        compiler_params=pltpu.CompilerParams(vmem_limit_bytes=8 * 2**20),
        name="meet",
    )(pltpu.with_memory_space_constraint(weight, pltpu.VMEM), *groups, *before)


def tell_kernel(hidden, head, *outs, micro):
    values = jnp.dot(hidden[...], head[...], preferred_element_type=jnp.float32)
    tokens = values.shape[0] // micro
    share = tokens // len(outs)
    for section, out in enumerate(outs):
        starts = [m * tokens + section * share for m in range(micro)]
        out[...] = jnp.concatenate([values[start : start + share] for start in starts], axis=0)


def tell(hidden, head, micro, sections):
    shape = (hidden.shape[0] // sections, head.shape[1])
    vmem = pl.BlockSpec(memory_space=pltpu.VMEM)
    return pl.pallas_call(
        functools.partial(tell_kernel, micro=micro),
        out_shape=[jax.ShapeDtypeStruct(shape, jnp.float32)] * sections,
        in_specs=[vmem, vmem],
        out_specs=[vmem] * sections,
        compiler_params=pltpu.CompilerParams(vmem_limit_bytes=8 * 2**20),
        name="tell",
    )(hidden, head)


def finish_kernel(*refs, terms):
    values = paired_sum([ref[...].astype(jnp.float32) for ref in refs[:terms]])
    reward, action, best, taken = refs[terms:]
    values = values.reshape(*reward.shape, values.shape[1])
    bins = lax.broadcasted_iota(jnp.int32, values.shape, 2)
    picked = jnp.where(bins == action[...][:, :, None], values, 0.0)
    best[...] = reward[...] + 0.98 * jnp.max(values, axis=2)
    taken[...] = jnp.sum(picked, axis=2)


def finish(terms, reward, action):
    vmem = pl.BlockSpec(memory_space=pltpu.VMEM)
    return pl.pallas_call(
        functools.partial(finish_kernel, terms=len(terms)),
        out_shape=[jax.ShapeDtypeStruct(reward.shape, jnp.float32)] * 2,
        in_specs=[vmem] * (len(terms) + 2),
        out_specs=[vmem] * 2,
        compiler_params=pltpu.CompilerParams(vmem_limit_bytes=8 * 2**20),
        name="finish",
    )(*terms, reward, action)


def paired_sum(terms):
    while len(terms) > 1:
        terms = [a + b for a, b in zip(terms[::2], terms[1::2])] + terms[len(terms) // 2 * 2 :]
    return terms[0]


def per_device(start_tokens, target_weight, online_weight, head_weight, reward, action_bin, sections, digits, names):
    micro, tokens, width = start_tokens.shape
    tp = 1
    for radix, _ in digits:
        tp *= radix
    everyone = ("section",) + names
    rows = micro * tokens
    features = width * tp
    rounds = len(digits)
    send = functools.partial(exchange, axes=everyone, tp=tp)
    own = start_tokens.reshape(rows, width)
    inner = digits[-1][0]
    half = inner // 2
    for layer in range(sections):
        place = dict(layer=layer, digits=digits, names=names)
        helper = layer - 1 if layer > 0 else min(1, sections - 1)
        both = [(layer, helper), (helper, layer)] if helper != layer else [(layer, layer)]
        if layer > 0:
            own = own + send(own, routes=both, radix=1, stride=1, step=0)

        if layer == 0:
            parts = list(spread(own, online_weight, 0, inner, **place))
        else:
            parts = list(spread(own, online_weight, 0, half, **place)) if half else []
            parts += spread(own, online_weight, half, inner - half, **place)
        stack = own[None]
        for number, (radix, stride) in enumerate(digits):
            final = number == rounds - 1
            routes = both
            if final:
                routes = [(helper, layer)]
                at = layer if number % 2 == 0 else helper
                sent = []
                for step, one in zip(scatter_steps(radix, True), parts):
                    if step > 0 or at != layer:
                        one = send(one, routes=[(layer, at)], radix=radix, stride=stride, step=step)
                    sent.append(one)
                if layer == 0 and rounds > 1:
                    stack, sent[:1] = lax.optimization_barrier((stack, sent[:1]))
            gathered = [
                stack if step == 0 else send(stack, routes=routes, radix=radix, stride=stride, step=step)
                for step in gather_steps(radix, final)
            ]
            if not final:
                gathered, parts[-1:] = lax.optimization_barrier((gathered, parts[-1:]))
                stack = jnp.concatenate(gathered, axis=0)
        wide = functools.reduce(jnp.add, [one.astype(jnp.float32) for one in sent])
        for number in range(rounds - 2, -1, -1):
            radix, stride = digits[number]
            to = layer if at != layer or number % 2 == 0 else helper
            part = wide.shape[0] // radix
            sent = []
            for i, step in enumerate(scatter_steps(radix, False)):
                one = wide[i * part : (i + 1) * part].astype(jnp.bfloat16)
                if step > 0 or to != at:
                    one = send(one, routes=[(at, to)], radix=radix, stride=stride, step=step)
                sent.append(one)
            at = to
            wide = functools.reduce(jnp.add, [one.astype(jnp.float32) for one in sent])

        before = []
        for begin in range(0, len(gathered), max(1, half)):
            groups = gathered[begin : begin + max(1, half)]
            before = meet(target_weight, groups, begin * groups[0].shape[0], before, **place)
        total, square = before
        update = lax.rsqrt(square / features + 1e-06) * (0.25 * wide[0] + 0.75 * total)
        own = jnp.where(square >= 0.0, own.astype(jnp.float32) + update, 0.0).astype(jnp.bfloat16)

    end = sections - 1
    values = tell(own, head_weight, micro, sections)
    mine = values[end]
    for other in range(end):
        mine = mine + send(values[other], routes=[(end, other), (other, end)], radix=1, stride=1, step=0)
    everywhere = [(section, section) for section in range(sections)]
    terms = [mine]
    for radix, stride in digits[::-1]:
        told = paired_sum([term.astype(jnp.float32) for term in terms]).astype(jnp.bfloat16)
        terms = [send(told, routes=everywhere, radix=radix, stride=stride, step=step) for step in range(radix - 1, 0, -1)]
        terms.append(told)
    return tuple(finish(terms, reward, action_bin))


def solution(mesh):
    sections, tp = mesh.shape["section"], mesh.shape["tp"]
    digits = digits_of(tp, 4)
    names = tuple(f"tp{number}" for number in range(len(digits)))
    cut = jax.sharding.Mesh(
        mesh.devices.reshape([sections] + [radix for radix, _ in digits]), ("section",) + names
    )
    in_specs = (
        P(None, None, names),
        P("section", None, names),
        P("section", names, None),
        P(names, None),
        P(None, "section"),
        P(None, "section"),
    )
    out_specs = (P(None, "section"), P(None, "section"))
    body = functools.partial(per_device, sections=sections, digits=digits, names=names)
    return jax.shard_map(body, mesh=cut, in_specs=in_specs, out_specs=out_specs, check_vma=False)
```

```python
import functools

import jax
import jax.numpy as jnp
from jax import lax
from jax.experimental import pallas as pl
from jax.experimental.pallas import tpu as pltpu
from jax.sharding import PartitionSpec as P


def digits_of(size, most):
    radices = []
    left = size
    while left > 1:
        radix = next((r for r in range(min(most, left), 1, -1) if left % r == 0), None)
        if radix is None:
            radix = next(r for r in range(2, left + 1) if left % r == 0)
        radices.insert(0, radix)
        left //= radix
    strides = []
    stride = size
    for radix in radices:
        stride //= radix
        strides.append(stride)
    return list(zip(radices, strides))


def peer(digit, step, radix):
    if radix & (radix - 1) == 0:
        return digit ^ step
    return (digit + step) % radix


def exchange(value, axes, tp, routes, radix, stride, step):
    pairs = []
    for start, end in routes:
        for t in range(tp):
            digit = t // stride % radix
            other = t + (peer(digit, step, radix) - digit) * stride
            pairs.append((start * tp + t, end * tp + other))
    return lax.ppermute(value, axes, pairs)


def block_of(steps, digits, names):
    index = 0
    for step, (radix, stride), name in zip(steps, digits, names):
        index = index + peer(lax.axis_index(name), step, radix) * stride
    return index


def gather_steps(radix, last):
    return [*range(radix)] if last else [*range(radix - 1, -1, -1)]


def scatter_steps(radix, last):
    return [*range(radix - 1, -1, -1)]


def relative(digits, steps_of):
    found = [()]
    for number, (radix, _) in enumerate(digits):
        found = [one + (step,) for step in steps_of(radix, number == len(digits) - 1) for one in found]
    return found


def spread_kernel(x, weight, *outs, first, layer, digits, names):
    share, _, width = outs[0].shape

    @pl.when(lax.axis_index("section") == layer)
    def _():
        for j, steps in enumerate(relative(digits, scatter_steps)[first : first + share * len(outs)]):
            start = pl.multiple_of(block_of(steps, digits, names) * width, width)
            part = jnp.dot(x[...], weight[0, :, pl.ds(start, width)], preferred_element_type=jnp.float32)
            outs[j // share][j % share] = part.astype(outs[0].dtype)


def first_spread_kernel(x, weight, *rest, outputs, layer, digits, names):
    outs, (here, held, total, x_arrived, arrived) = rest[:outputs], rest[outputs:]
    share, _, width = outs[0].shape
    chunks, pieces = arrived.shape
    depth = weight.shape[1] // chunks
    rows = depth // pieces

    @pl.when(lax.axis_index("section") == layer)
    def _():
        x_copy = pltpu.make_async_copy(x, here, x_arrived)
        x_copy.start()
        copies = []
        for chunk in range(chunks):
            for piece in range(pieces):
                these = pl.ds(chunk * depth + piece * rows, rows)
                copies.append(
                    pltpu.make_async_copy(weight.at[0, these, :], held.at[these, :], arrived.at[chunk, piece])
                )
                copies[-1].start()
        x_copy.wait()
        for chunk in range(chunks):
            for piece in range(pieces):
                copies[chunk * pieces + piece].wait()
            those = slice(chunk * depth, (chunk + 1) * depth)
            for j, steps in enumerate(relative(digits, scatter_steps)):
                start = pl.multiple_of(block_of(steps, digits, names) * width, width)
                part = jnp.dot(here[:, those], held[those, pl.ds(start, width)], preferred_element_type=jnp.float32)
                if chunk > 0:
                    part = part + total[j]
                if chunk < chunks - 1:
                    total[j] = part
                else:
                    outs[j // share][j % share] = part.astype(outs[0].dtype)


def spread(x, weight, first, groups, layer, digits, names):
    rows, depth = x.shape
    count = len(relative(digits, scatter_steps))
    share = count // digits[-1][0]
    width = weight.shape[2] // count
    vmem = pl.BlockSpec(memory_space=pltpu.VMEM)
    outs = [jax.ShapeDtypeStruct((share, rows, width), jnp.bfloat16)] * groups
    if layer > 0:
        return pl.pallas_call(
            functools.partial(spread_kernel, first=first * share, layer=layer, digits=digits, names=names),
            out_shape=outs,
            in_specs=[vmem, vmem],
            out_specs=[vmem] * groups,
            compiler_params=pltpu.CompilerParams(vmem_limit_bytes=8 * 2**20),
            name="spread",
        )(x, pltpu.with_memory_space_constraint(weight, pltpu.VMEM))
    chunks = 2 if depth % 256 == 0 else 1
    return pl.pallas_call(
        functools.partial(first_spread_kernel, outputs=groups, layer=layer, digits=digits, names=names),
        out_shape=outs,
        in_specs=[pl.BlockSpec(memory_space=pltpu.HBM)] * 2,
        out_specs=[vmem] * groups,
        scratch_shapes=[
            pltpu.VMEM(x.shape, x.dtype),
            pltpu.VMEM(weight.shape[1:], weight.dtype),
            pltpu.VMEM((count, rows, width), jnp.float32),
            pltpu.SemaphoreType.DMA,
            pltpu.SemaphoreType.DMA((chunks, 4)),
        ],
        compiler_params=pltpu.CompilerParams(vmem_limit_bytes=20 * 2**20),
        name="first_spread",
    )(
        pltpu.with_memory_space_constraint(x, pltpu.HBM),
        pltpu.with_memory_space_constraint(weight, pltpu.HBM),
    )


def meet_kernel(weight, *rest, first, blocks, layer, digits, names):
    inputs, before, (total, square) = rest[:blocks], rest[blocks:-2], rest[-2:]
    share, _, depth = inputs[0].shape
    inside = lax.axis_index("section") == layer

    @pl.when(inside)
    def _():
        sum_of = before[0][...] if before else jnp.zeros(total.shape, jnp.float32)
        squares = before[1][...] if before else jnp.zeros(square.shape, jnp.float32)
        for j, steps in enumerate(relative(digits, gather_steps)[first : first + share * blocks]):
            x = inputs[j // share][j % share]
            wide = x.astype(jnp.float32)
            squares = squares + jnp.sum(wide * wide, axis=1, keepdims=True)
            start = pl.multiple_of(block_of(steps, digits, names) * depth, depth)
            sum_of = sum_of + jnp.dot(x, weight[0, pl.ds(start, depth), :], preferred_element_type=jnp.float32)
        total[...] = sum_of
        square[...] = squares

    @pl.when(jnp.logical_not(inside))
    def _():
        total[...] = jnp.zeros_like(total)
        square[...] = jnp.full_like(square, -1.0)


def meet(weight, groups, first, before, layer, digits, names):
    rows = groups[0].shape[1]
    vmem = pl.BlockSpec(memory_space=pltpu.VMEM)
    return pl.pallas_call(
        functools.partial(
            meet_kernel, first=first, blocks=len(groups), layer=layer, digits=digits, names=names
        ),
        out_shape=[
            jax.ShapeDtypeStruct((rows, weight.shape[2]), jnp.float32),
            jax.ShapeDtypeStruct((rows, 1), jnp.float32),
        ],
        in_specs=[vmem] * (1 + len(groups) + len(before)),
        out_specs=[vmem, vmem],
        compiler_params=pltpu.CompilerParams(vmem_limit_bytes=8 * 2**20),
        name="meet",
    )(pltpu.with_memory_space_constraint(weight, pltpu.VMEM), *groups, *before)


def tell_kernel(hidden, head, *outs, micro):
    values = jnp.dot(hidden[...], head[...], preferred_element_type=jnp.float32)
    tokens = values.shape[0] // micro
    share = tokens // len(outs)
    for section, out in enumerate(outs):
        starts = [m * tokens + section * share for m in range(micro)]
        out[...] = jnp.concatenate([values[start : start + share] for start in starts], axis=0)


def tell(hidden, head, micro, sections):
    shape = (hidden.shape[0] // sections, head.shape[1])
    vmem = pl.BlockSpec(memory_space=pltpu.VMEM)
    return pl.pallas_call(
        functools.partial(tell_kernel, micro=micro),
        out_shape=[jax.ShapeDtypeStruct(shape, jnp.float32)] * sections,
        in_specs=[vmem, vmem],
        out_specs=[vmem] * sections,
        compiler_params=pltpu.CompilerParams(vmem_limit_bytes=8 * 2**20),
        name="tell",
    )(hidden, head)


def finish_kernel(*refs, terms):
    values = paired_sum([ref[...].astype(jnp.float32) for ref in refs[:terms]])
    reward, action, best, taken = refs[terms:]
    values = values.reshape(*reward.shape, values.shape[1])
    bins = lax.broadcasted_iota(jnp.int32, values.shape, 2)
    picked = jnp.where(bins == action[...][:, :, None], values, 0.0)
    best[...] = reward[...] + 0.98 * jnp.max(values, axis=2)
    taken[...] = jnp.sum(picked, axis=2)


def finish(terms, reward, action):
    vmem = pl.BlockSpec(memory_space=pltpu.VMEM)
    return pl.pallas_call(
        functools.partial(finish_kernel, terms=len(terms)),
        out_shape=[jax.ShapeDtypeStruct(reward.shape, jnp.float32)] * 2,
        in_specs=[vmem] * (len(terms) + 2),
        out_specs=[vmem] * 2,
        compiler_params=pltpu.CompilerParams(vmem_limit_bytes=8 * 2**20),
        name="finish",
    )(*terms, reward, action)


def paired_sum(terms):
    while len(terms) > 1:
        terms = [a + b for a, b in zip(terms[::2], terms[1::2])] + terms[len(terms) // 2 * 2 :]
    return terms[0]


def per_device(start_tokens, target_weight, online_weight, head_weight, reward, action_bin, sections, digits, names):
    micro, tokens, width = start_tokens.shape
    tp = 1
    for radix, _ in digits:
        tp *= radix
    everyone = ("section",) + names
    rows = micro * tokens
    features = width * tp
    rounds = len(digits)
    send = functools.partial(exchange, axes=everyone, tp=tp)
    own = start_tokens.reshape(rows, width)
    inner = digits[-1][0]
    half = inner // 2
    for layer in range(sections):
        place = dict(layer=layer, digits=digits, names=names)
        helper = layer - 1 if layer > 0 else min(1, sections - 1)
        both = [(layer, helper), (helper, layer)] if helper != layer else [(layer, layer)]
        if layer > 0:
            own = own + send(own, routes=both, radix=1, stride=1, step=0)

        if layer == 0:
            parts = list(spread(own, online_weight, 0, inner, **place))
        else:
            parts = list(spread(own, online_weight, 0, half, **place)) if half else []
            parts += spread(own, online_weight, half, inner - half, **place)
        stack = own[None]
        for number, (radix, stride) in enumerate(digits):
            final = number == rounds - 1
            if final:
                at = layer if number % 2 == 0 else helper
                sent = []
                for step, one in zip(scatter_steps(radix, True), parts):
                    if step > 0 or at != layer:
                        routes = both if step == 0 else [(layer, at)]
                        one = send(one, routes=routes, radix=radix, stride=stride, step=step)
                    sent.append(one)
                if layer == 0 and rounds > 1:
                    stack, sent[:1] = lax.optimization_barrier((stack, sent[:1]))
            routes = [(helper, layer)] if final else both
            gathered = [
                stack if step == 0 else send(stack, routes=routes, radix=radix, stride=stride, step=step)
                for step in gather_steps(radix, final)
            ]
            if not final:
                gathered, parts[-1:] = lax.optimization_barrier((gathered, parts[-1:]))
                stack = jnp.concatenate(gathered, axis=0)
        wide = functools.reduce(jnp.add, [one.astype(jnp.float32) for one in sent])
        for number in range(rounds - 2, -1, -1):
            radix, stride = digits[number]
            to = layer if at != layer or number % 2 == 0 else helper
            part = wide.shape[0] // radix
            sent = []
            for i, step in enumerate(scatter_steps(radix, False)):
                one = wide[i * part : (i + 1) * part].astype(jnp.bfloat16)
                if step > 0 or to != at:
                    routes = both if step == 0 else [(at, to)]
                    one = send(one, routes=routes, radix=radix, stride=stride, step=step)
                sent.append(one)
            at = to
            wide = functools.reduce(jnp.add, [one.astype(jnp.float32) for one in sent])

        before = []
        for begin in range(0, len(gathered), max(1, half)):
            groups = gathered[begin : begin + max(1, half)]
            before = meet(target_weight, groups, begin * groups[0].shape[0], before, **place)
        total, square = before
        update = lax.rsqrt(square / features + 1e-06) * (0.25 * wide[0] + 0.75 * total)
        own = jnp.where(square >= 0.0, own.astype(jnp.float32) + update, 0.0).astype(jnp.bfloat16)

    end = sections - 1
    values = tell(own, head_weight, micro, sections)
    mine = values[end]
    for other in range(end):
        mine = mine + send(values[other], routes=[(end, other), (other, end)], radix=1, stride=1, step=0)
    everywhere = [(section, section) for section in range(sections)]
    terms = [mine]
    for radix, stride in digits[::-1]:
        told = paired_sum([term.astype(jnp.float32) for term in terms]).astype(jnp.bfloat16)
        terms = [send(told, routes=everywhere, radix=radix, stride=stride, step=step) for step in range(radix - 1, 0, -1)]
        terms.append(told)
    return tuple(finish(terms, reward, action_bin))


def solution(mesh):
    sections, tp = mesh.shape["section"], mesh.shape["tp"]
    digits = digits_of(tp, 4)
    names = tuple(f"tp{number}" for number in range(len(digits)))
    cut = jax.sharding.Mesh(
        mesh.devices.reshape([sections] + [radix for radix, _ in digits]), ("section",) + names
    )
    in_specs = (
        P(None, None, names),
        P("section", None, names),
        P("section", names, None),
        P(names, None),
        P(None, "section"),
        P(None, "section"),
    )
    out_specs = (P(None, "section"), P(None, "section"))
    body = functools.partial(per_device, sections=sections, digits=digits, names=names)
    return jax.shard_map(body, mesh=cut, in_specs=in_specs, out_specs=out_specs, check_vma=False)
```

```python
import functools

import jax
import jax.numpy as jnp
from jax import lax
from jax.experimental import pallas as pl
from jax.experimental.pallas import tpu as pltpu
from jax.sharding import PartitionSpec as P


def digits_of(size, most):
    radices = []
    left = size
    while left > 1:
        radix = next((r for r in range(min(most, left), 1, -1) if left % r == 0), None)
        if radix is None:
            radix = next(r for r in range(2, left + 1) if left % r == 0)
        radices.insert(0, radix)
        left //= radix
    strides = []
    stride = size
    for radix in radices:
        stride //= radix
        strides.append(stride)
    return list(zip(radices, strides))


def peer(digit, step, radix):
    if radix & (radix - 1) == 0:
        return digit ^ step
    return (digit + step) % radix


def exchange(value, axes, tp, routes, radix, stride, step):
    pairs = []
    for start, end in routes:
        for t in range(tp):
            digit = t // stride % radix
            other = t + (peer(digit, step, radix) - digit) * stride
            pairs.append((start * tp + t, end * tp + other))
    return lax.ppermute(value, axes, pairs)


def block_of(steps, digits, names):
    index = 0
    for step, (radix, stride), name in zip(steps, digits, names):
        index = index + peer(lax.axis_index(name), step, radix) * stride
    return index


def gather_steps(radix, last):
    return [*range(radix)] if last else [*range(radix - 1, -1, -1)]


def scatter_steps(radix, last):
    return [*range(radix - 1, -1, -1)]


def relative(digits, steps_of):
    found = [()]
    for number, (radix, _) in enumerate(digits):
        found = [one + (step,) for step in steps_of(radix, number == len(digits) - 1) for one in found]
    return found


def spread_kernel(x, weight, *outs, first, layer, digits, names):
    share, _, width = outs[0].shape

    @pl.when(lax.axis_index("section") == layer)
    def _():
        for j, steps in enumerate(relative(digits, scatter_steps)[first : first + share * len(outs)]):
            start = pl.multiple_of(block_of(steps, digits, names) * width, width)
            part = jnp.dot(x[...], weight[0, :, pl.ds(start, width)], preferred_element_type=jnp.float32)
            outs[j // share][j % share] = part.astype(outs[0].dtype)


def first_spread_kernel(x, weight, *rest, outputs, layer, digits, names):
    outs, (here, held, total, x_arrived, arrived) = rest[:outputs], rest[outputs:]
    share, _, width = outs[0].shape
    chunks, pieces = arrived.shape
    depth = weight.shape[1] // chunks
    rows = depth // pieces

    @pl.when(lax.axis_index("section") == layer)
    def _():
        x_copy = pltpu.make_async_copy(x, here, x_arrived)
        x_copy.start()
        copies = []
        for chunk in range(chunks):
            for piece in range(pieces):
                these = pl.ds(chunk * depth + piece * rows, rows)
                copies.append(
                    pltpu.make_async_copy(weight.at[0, these, :], held.at[these, :], arrived.at[chunk, piece])
                )
                copies[-1].start()
        x_copy.wait()
        for chunk in range(chunks):
            for piece in range(pieces):
                copies[chunk * pieces + piece].wait()
            those = slice(chunk * depth, (chunk + 1) * depth)
            for j, steps in enumerate(relative(digits, scatter_steps)):
                start = pl.multiple_of(block_of(steps, digits, names) * width, width)
                part = jnp.dot(here[:, those], held[those, pl.ds(start, width)], preferred_element_type=jnp.float32)
                if chunk > 0:
                    part = part + total[j]
                if chunk < chunks - 1:
                    total[j] = part
                else:
                    outs[j // share][j % share] = part.astype(outs[0].dtype)


def spread(x, weight, first, groups, layer, digits, names):
    rows, depth = x.shape
    count = len(relative(digits, scatter_steps))
    share = count // digits[-1][0]
    width = weight.shape[2] // count
    vmem = pl.BlockSpec(memory_space=pltpu.VMEM)
    outs = [jax.ShapeDtypeStruct((share, rows, width), jnp.bfloat16)] * groups
    if layer > 0:
        return pl.pallas_call(
            functools.partial(spread_kernel, first=first * share, layer=layer, digits=digits, names=names),
            out_shape=outs,
            in_specs=[vmem, vmem],
            out_specs=[vmem] * groups,
            compiler_params=pltpu.CompilerParams(vmem_limit_bytes=8 * 2**20),
            name="spread",
        )(x, pltpu.with_memory_space_constraint(weight, pltpu.VMEM))
    chunks = 2 if depth % 256 == 0 else 1
    return pl.pallas_call(
        functools.partial(first_spread_kernel, outputs=groups, layer=layer, digits=digits, names=names),
        out_shape=outs,
        in_specs=[pl.BlockSpec(memory_space=pltpu.HBM)] * 2,
        out_specs=[vmem] * groups,
        scratch_shapes=[
            pltpu.VMEM(x.shape, x.dtype),
            pltpu.VMEM(weight.shape[1:], weight.dtype),
            pltpu.VMEM((count, rows, width), jnp.float32),
            pltpu.SemaphoreType.DMA,
            pltpu.SemaphoreType.DMA((chunks, 4)),
        ],
        compiler_params=pltpu.CompilerParams(vmem_limit_bytes=20 * 2**20),
        name="first_spread",
    )(
        pltpu.with_memory_space_constraint(x, pltpu.HBM),
        pltpu.with_memory_space_constraint(weight, pltpu.HBM),
    )


def mix_kernel(*rest, groups, layer):
    parts, blocks, outs = rest[:groups], rest[groups:-groups], rest[-groups:]
    inside = lax.axis_index("section") == layer

    @pl.when(inside)
    def _():
        for part, out in zip(parts, outs):
            out[...] = part[...]

    @pl.when(jnp.logical_not(inside))
    def _():
        start = 0
        for block in blocks:
            for out in outs:
                out[start : start + block.shape[0]] = block[...]
            start += block.shape[0]


def mix(parts, blocks, layer):
    vmem = pl.BlockSpec(memory_space=pltpu.VMEM)
    return pl.pallas_call(
        functools.partial(mix_kernel, groups=len(parts), layer=layer),
        out_shape=[jax.ShapeDtypeStruct(part.shape, part.dtype) for part in parts],
        in_specs=[vmem] * (len(parts) + len(blocks)),
        out_specs=[vmem] * len(parts),
        compiler_params=pltpu.CompilerParams(vmem_limit_bytes=8 * 2**20),
        name="mix",
    )(*parts, *blocks)


def meet_kernel(weight, *rest, first, blocks, layer, digits, names):
    inputs, before, (total, square) = rest[:blocks], rest[blocks:-2], rest[-2:]
    share, _, depth = inputs[0].shape
    inside = lax.axis_index("section") == layer

    @pl.when(inside)
    def _():
        sum_of = before[0][...] if before else jnp.zeros(total.shape, jnp.float32)
        squares = before[1][...] if before else jnp.zeros(square.shape, jnp.float32)
        for j, steps in enumerate(relative(digits, gather_steps)[first : first + share * blocks]):
            x = inputs[j // share][j % share]
            wide = x.astype(jnp.float32)
            squares = squares + jnp.sum(wide * wide, axis=1, keepdims=True)
            start = pl.multiple_of(block_of(steps, digits, names) * depth, depth)
            sum_of = sum_of + jnp.dot(x, weight[0, pl.ds(start, depth), :], preferred_element_type=jnp.float32)
        total[...] = sum_of
        square[...] = squares

    @pl.when(jnp.logical_not(inside))
    def _():
        total[...] = jnp.zeros_like(total)
        square[...] = jnp.full_like(square, -1.0)


def meet(weight, groups, first, before, layer, digits, names):
    rows = groups[0].shape[1]
    vmem = pl.BlockSpec(memory_space=pltpu.VMEM)
    return pl.pallas_call(
        functools.partial(
            meet_kernel, first=first, blocks=len(groups), layer=layer, digits=digits, names=names
        ),
        out_shape=[
            jax.ShapeDtypeStruct((rows, weight.shape[2]), jnp.float32),
            jax.ShapeDtypeStruct((rows, 1), jnp.float32),
        ],
        in_specs=[vmem] * (1 + len(groups) + len(before)),
        out_specs=[vmem, vmem],
        compiler_params=pltpu.CompilerParams(vmem_limit_bytes=8 * 2**20),
        name="meet",
    )(pltpu.with_memory_space_constraint(weight, pltpu.VMEM), *groups, *before)


def tell_kernel(hidden, head, *outs, micro):
    values = jnp.dot(hidden[...], head[...], preferred_element_type=jnp.float32)
    tokens = values.shape[0] // micro
    share = tokens // len(outs)
    for section, out in enumerate(outs):
        starts = [m * tokens + section * share for m in range(micro)]
        out[...] = jnp.concatenate([values[start : start + share] for start in starts], axis=0)


def tell(hidden, head, micro, sections):
    shape = (hidden.shape[0] // sections, head.shape[1])
    vmem = pl.BlockSpec(memory_space=pltpu.VMEM)
    return pl.pallas_call(
        functools.partial(tell_kernel, micro=micro),
        out_shape=[jax.ShapeDtypeStruct(shape, jnp.float32)] * sections,
        in_specs=[vmem, vmem],
        out_specs=[vmem] * sections,
        compiler_params=pltpu.CompilerParams(vmem_limit_bytes=8 * 2**20),
        name="tell",
    )(hidden, head)


def finish_kernel(*refs, terms):
    values = paired_sum([ref[...].astype(jnp.float32) for ref in refs[:terms]])
    reward, action, best, taken = refs[terms:]
    values = values.reshape(*reward.shape, values.shape[1])
    bins = lax.broadcasted_iota(jnp.int32, values.shape, 2)
    picked = jnp.where(bins == action[...][:, :, None], values, 0.0)
    best[...] = reward[...] + 0.98 * jnp.max(values, axis=2)
    taken[...] = jnp.sum(picked, axis=2)


def finish(terms, reward, action):
    vmem = pl.BlockSpec(memory_space=pltpu.VMEM)
    return pl.pallas_call(
        functools.partial(finish_kernel, terms=len(terms)),
        out_shape=[jax.ShapeDtypeStruct(reward.shape, jnp.float32)] * 2,
        in_specs=[vmem] * (len(terms) + 2),
        out_specs=[vmem] * 2,
        compiler_params=pltpu.CompilerParams(vmem_limit_bytes=8 * 2**20),
        name="finish",
    )(*terms, reward, action)


def paired_sum(terms):
    while len(terms) > 1:
        terms = [a + b for a, b in zip(terms[::2], terms[1::2])] + terms[len(terms) // 2 * 2 :]
    return terms[0]


def per_device(start_tokens, target_weight, online_weight, head_weight, reward, action_bin, sections, digits, names):
    micro, tokens, width = start_tokens.shape
    tp = 1
    for radix, _ in digits:
        tp *= radix
    everyone = ("section",) + names
    rows = micro * tokens
    features = width * tp
    rounds = len(digits)
    send = functools.partial(exchange, axes=everyone, tp=tp)
    own = start_tokens.reshape(rows, width)
    inner = digits[-1][0]
    half = inner // 2
    for layer in range(sections):
        place = dict(layer=layer, digits=digits, names=names)
        helper = layer - 1 if layer > 0 else min(1, sections - 1)
        both = [(layer, helper), (helper, layer)] if helper != layer else [(layer, layer)]
        if layer > 0:
            own = own + send(own, routes=both, radix=1, stride=1, step=0)

        if layer == 0:
            parts = list(spread(own, online_weight, 0, inner, **place))
        else:
            parts = list(spread(own, online_weight, 0, half, **place)) if half else []
            parts += spread(own, online_weight, half, inner - half, **place)
        stack = own[None]
        for number, (radix, stride) in enumerate(digits):
            final = number == rounds - 1
            if final:
                at = layer if number % 2 == 0 else helper
                sent, shared = [], None
                for step, one in zip(scatter_steps(radix, True), parts):
                    if step == 1 and at != layer:
                        (one,) = mix([one], [stack], layer)
                        one = shared = send(one, routes=both, radix=radix, stride=stride, step=step)
                    elif step > 0 or at != layer:
                        routes = both if step == 0 else [(layer, at)]
                        one = send(one, routes=routes, radix=radix, stride=stride, step=step)
                    sent.append(one)
                if layer == 0 and rounds > 1:
                    stack, sent[:1] = lax.optimization_barrier((stack, sent[:1]))
            routes = [(helper, layer)] if final else both
            gathered = []
            for step in gather_steps(radix, final):
                if step == 0:
                    gathered.append(stack)
                elif final and step == 1 and shared is not None:
                    gathered.append(shared)
                else:
                    gathered.append(send(stack, routes=routes, radix=radix, stride=stride, step=step))
            if not final:
                gathered, parts[-1:] = lax.optimization_barrier((gathered, parts[-1:]))
                stack = jnp.concatenate(gathered, axis=0)
        wide = functools.reduce(jnp.add, [one.astype(jnp.float32) for one in sent])
        for number in range(rounds - 2, -1, -1):
            radix, stride = digits[number]
            to = layer if at != layer or number % 2 == 0 else helper
            part = wide.shape[0] // radix
            sent = []
            for i, step in enumerate(scatter_steps(radix, False)):
                one = wide[i * part : (i + 1) * part].astype(jnp.bfloat16)
                if step > 0 or to != at:
                    routes = both if step <= 1 and to != at else [(at, to)]
                    one = send(one, routes=routes, radix=radix, stride=stride, step=step)
                sent.append(one)
            at = to
            if layer == 0:
                sent = sent[-1:] + sent[:-1]
            wide = functools.reduce(jnp.add, [one.astype(jnp.float32) for one in sent])

        before = []
        for begin in range(0, len(gathered), max(1, half)):
            groups = gathered[begin : begin + max(1, half)]
            before = meet(target_weight, groups, begin * groups[0].shape[0], before, **place)
        total, square = before
        update = lax.rsqrt(square / features + 1e-06) * (0.25 * wide[0] + 0.75 * total)
        own = jnp.where(square >= 0.0, own.astype(jnp.float32) + update, 0.0).astype(jnp.bfloat16)

    end = sections - 1
    values = tell(own, head_weight, micro, sections)
    mine = values[end]
    for other in range(end):
        mine = mine + send(values[other], routes=[(end, other), (other, end)], radix=1, stride=1, step=0)
    everywhere = [(section, section) for section in range(sections)]
    terms = [mine]
    for radix, stride in digits[::-1]:
        told = paired_sum([term.astype(jnp.float32) for term in terms]).astype(jnp.bfloat16)
        terms = [send(told, routes=everywhere, radix=radix, stride=stride, step=step) for step in range(radix - 1, 0, -1)]
        terms.append(told)
    return tuple(finish(terms, reward, action_bin))


def solution(mesh):
    sections, tp = mesh.shape["section"], mesh.shape["tp"]
    digits = digits_of(tp, 4)
    names = tuple(f"tp{number}" for number in range(len(digits)))
    cut = jax.sharding.Mesh(
        mesh.devices.reshape([sections] + [radix for radix, _ in digits]), ("section",) + names
    )
    in_specs = (
        P(None, None, names),
        P("section", None, names),
        P("section", names, None),
        P(names, None),
        P(None, "section"),
        P(None, "section"),
    )
    out_specs = (P(None, "section"), P(None, "section"))
    body = functools.partial(per_device, sections=sections, digits=digits, names=names)
    return jax.shard_map(body, mesh=cut, in_specs=in_specs, out_specs=out_specs, check_vma=False)
```

```python
import functools

import jax
import jax.numpy as jnp
from jax import lax
from jax.experimental import pallas as pl
from jax.experimental.pallas import tpu as pltpu
from jax.sharding import PartitionSpec as P


def digits_of(size, most):
    radices = []
    left = size
    while left > 1:
        radix = next((r for r in range(min(most, left), 1, -1) if left % r == 0), None)
        if radix is None:
            radix = next(r for r in range(2, left + 1) if left % r == 0)
        radices.insert(0, radix)
        left //= radix
    strides = []
    stride = size
    for radix in radices:
        stride //= radix
        strides.append(stride)
    return list(zip(radices, strides))


def peer(digit, step, radix):
    if radix & (radix - 1) == 0:
        return digit ^ step
    return (digit + step) % radix


def exchange(value, axes, tp, routes, radix, stride, step):
    pairs = []
    for start, end in routes:
        for t in range(tp):
            digit = t // stride % radix
            other = t + (peer(digit, step, radix) - digit) * stride
            pairs.append((start * tp + t, end * tp + other))
    if len(routes) == 1 and routes[0][0] != routes[0][1]:
        start, end = routes[0]
        pairs += [(end * tp + t, start * tp + t) for t in range(tp)]
    return lax.ppermute(value, axes, pairs)


def block_of(steps, digits, names):
    index = 0
    for step, (radix, stride), name in zip(steps, digits, names):
        index = index + peer(lax.axis_index(name), step, radix) * stride
    return index


def gather_steps(radix, last):
    return [*range(radix)] if last else [*range(radix - 1, -1, -1)]


def scatter_steps(radix, last):
    return [*range(radix - 1, -1, -1)]


def relative(digits, steps_of):
    found = [()]
    for number, (radix, _) in enumerate(digits):
        found = [one + (step,) for step in steps_of(radix, number == len(digits) - 1) for one in found]
    return found


def spread_kernel(x, weight, *outs, first, layer, digits, names):
    share, _, width = outs[0].shape

    @pl.when(lax.axis_index("section") == layer)
    def _():
        for j, steps in enumerate(relative(digits, scatter_steps)[first : first + share * len(outs)]):
            start = pl.multiple_of(block_of(steps, digits, names) * width, width)
            part = jnp.dot(x[...], weight[0, :, pl.ds(start, width)], preferred_element_type=jnp.float32)
            outs[j // share][j % share] = part.astype(outs[0].dtype)


def first_spread_kernel(x, weight, *rest, outputs, layer, digits, names):
    outs, (here, held, total, x_arrived, arrived) = rest[:outputs], rest[outputs:]
    share, _, width = outs[0].shape
    chunks, pieces = arrived.shape
    depth = weight.shape[1] // chunks
    rows = depth // pieces

    @pl.when(lax.axis_index("section") == layer)
    def _():
        x_copy = pltpu.make_async_copy(x, here, x_arrived)
        x_copy.start()
        copies = []
        for chunk in range(chunks):
            for piece in range(pieces):
                these = pl.ds(chunk * depth + piece * rows, rows)
                copies.append(
                    pltpu.make_async_copy(weight.at[0, these, :], held.at[these, :], arrived.at[chunk, piece])
                )
                copies[-1].start()
        x_copy.wait()
        for chunk in range(chunks):
            for piece in range(pieces):
                copies[chunk * pieces + piece].wait()
            those = slice(chunk * depth, (chunk + 1) * depth)
            for j, steps in enumerate(relative(digits, scatter_steps)):
                start = pl.multiple_of(block_of(steps, digits, names) * width, width)
                part = jnp.dot(here[:, those], held[those, pl.ds(start, width)], preferred_element_type=jnp.float32)
                if chunk > 0:
                    part = part + total[j]
                if chunk < chunks - 1:
                    total[j] = part
                else:
                    outs[j // share][j % share] = part.astype(outs[0].dtype)


def spread(x, weight, first, groups, layer, digits, names):
    rows, depth = x.shape
    count = len(relative(digits, scatter_steps))
    share = count // digits[-1][0]
    width = weight.shape[2] // count
    vmem = pl.BlockSpec(memory_space=pltpu.VMEM)
    outs = [jax.ShapeDtypeStruct((share, rows, width), jnp.bfloat16)] * groups
    if layer > 0:
        return pl.pallas_call(
            functools.partial(spread_kernel, first=first * share, layer=layer, digits=digits, names=names),
            out_shape=outs,
            in_specs=[vmem, vmem],
            out_specs=[vmem] * groups,
            compiler_params=pltpu.CompilerParams(vmem_limit_bytes=8 * 2**20),
            name="spread",
        )(x, pltpu.with_memory_space_constraint(weight, pltpu.VMEM))
    chunks = 2 if depth % 256 == 0 else 1
    return pl.pallas_call(
        functools.partial(first_spread_kernel, outputs=groups, layer=layer, digits=digits, names=names),
        out_shape=outs,
        in_specs=[pl.BlockSpec(memory_space=pltpu.HBM)] * 2,
        out_specs=[vmem] * groups,
        scratch_shapes=[
            pltpu.VMEM(x.shape, x.dtype),
            pltpu.VMEM(weight.shape[1:], weight.dtype),
            pltpu.VMEM((count, rows, width), jnp.float32),
            pltpu.SemaphoreType.DMA,
            pltpu.SemaphoreType.DMA((chunks, 4)),
        ],
        compiler_params=pltpu.CompilerParams(vmem_limit_bytes=20 * 2**20),
        name="first_spread",
    )(
        pltpu.with_memory_space_constraint(x, pltpu.HBM),
        pltpu.with_memory_space_constraint(weight, pltpu.HBM),
    )


def meet_kernel(weight, *rest, first, blocks, layer, digits, names):
    inputs, before, (total, square) = rest[:blocks], rest[blocks:-2], rest[-2:]
    share, _, depth = inputs[0].shape
    inside = lax.axis_index("section") == layer

    @pl.when(inside)
    def _():
        sum_of = before[0][...] if before else jnp.zeros(total.shape, jnp.float32)
        squares = before[1][...] if before else jnp.zeros(square.shape, jnp.float32)
        for j, steps in enumerate(relative(digits, gather_steps)[first : first + share * blocks]):
            x = inputs[j // share][j % share]
            wide = x.astype(jnp.float32)
            squares = squares + jnp.sum(wide * wide, axis=1, keepdims=True)
            start = pl.multiple_of(block_of(steps, digits, names) * depth, depth)
            sum_of = sum_of + jnp.dot(x, weight[0, pl.ds(start, depth), :], preferred_element_type=jnp.float32)
        total[...] = sum_of
        square[...] = squares

    @pl.when(jnp.logical_not(inside))
    def _():
        total[...] = jnp.zeros_like(total)
        square[...] = jnp.full_like(square, -1.0)


def meet(weight, groups, first, before, layer, digits, names):
    rows = groups[0].shape[1]
    vmem = pl.BlockSpec(memory_space=pltpu.VMEM)
    return pl.pallas_call(
        functools.partial(
            meet_kernel, first=first, blocks=len(groups), layer=layer, digits=digits, names=names
        ),
        out_shape=[
            jax.ShapeDtypeStruct((rows, weight.shape[2]), jnp.float32),
            jax.ShapeDtypeStruct((rows, 1), jnp.float32),
        ],
        in_specs=[vmem] * (1 + len(groups) + len(before)),
        out_specs=[vmem, vmem],
        compiler_params=pltpu.CompilerParams(vmem_limit_bytes=8 * 2**20),
        name="meet",
    )(pltpu.with_memory_space_constraint(weight, pltpu.VMEM), *groups, *before)


def tell_kernel(hidden, head, *outs, micro):
    values = jnp.dot(hidden[...], head[...], preferred_element_type=jnp.float32)
    tokens = values.shape[0] // micro
    share = tokens // len(outs)
    for section, out in enumerate(outs):
        starts = [m * tokens + section * share for m in range(micro)]
        out[...] = jnp.concatenate([values[start : start + share] for start in starts], axis=0)


def tell(hidden, head, micro, sections):
    shape = (hidden.shape[0] // sections, head.shape[1])
    vmem = pl.BlockSpec(memory_space=pltpu.VMEM)
    return pl.pallas_call(
        functools.partial(tell_kernel, micro=micro),
        out_shape=[jax.ShapeDtypeStruct(shape, jnp.float32)] * sections,
        in_specs=[vmem, vmem],
        out_specs=[vmem] * sections,
        compiler_params=pltpu.CompilerParams(vmem_limit_bytes=8 * 2**20),
        name="tell",
    )(hidden, head)


def finish_kernel(*refs, terms):
    values = paired_sum([ref[...].astype(jnp.float32) for ref in refs[:terms]])
    reward, action, best, taken = refs[terms:]
    values = values.reshape(*reward.shape, values.shape[1])
    bins = lax.broadcasted_iota(jnp.int32, values.shape, 2)
    picked = jnp.where(bins == action[...][:, :, None], values, 0.0)
    best[...] = reward[...] + 0.98 * jnp.max(values, axis=2)
    taken[...] = jnp.sum(picked, axis=2)


def finish(terms, reward, action):
    vmem = pl.BlockSpec(memory_space=pltpu.VMEM)
    return pl.pallas_call(
        functools.partial(finish_kernel, terms=len(terms)),
        out_shape=[jax.ShapeDtypeStruct(reward.shape, jnp.float32)] * 2,
        in_specs=[vmem] * (len(terms) + 2),
        out_specs=[vmem] * 2,
        compiler_params=pltpu.CompilerParams(vmem_limit_bytes=8 * 2**20),
        name="finish",
    )(*terms, reward, action)


def paired_sum(terms):
    while len(terms) > 1:
        terms = [a + b for a, b in zip(terms[::2], terms[1::2])] + terms[len(terms) // 2 * 2 :]
    return terms[0]


def per_device(start_tokens, target_weight, online_weight, head_weight, reward, action_bin, sections, digits, names):
    micro, tokens, width = start_tokens.shape
    tp = 1
    for radix, _ in digits:
        tp *= radix
    everyone = ("section",) + names
    rows = micro * tokens
    features = width * tp
    rounds = len(digits)
    send = functools.partial(exchange, axes=everyone, tp=tp)
    own = start_tokens.reshape(rows, width)
    inner = digits[-1][0]
    half = inner // 2
    for layer in range(sections):
        place = dict(layer=layer, digits=digits, names=names)
        helper = layer - 1 if layer > 0 else min(1, sections - 1)
        both = [(layer, helper), (helper, layer)] if helper != layer else [(layer, layer)]
        if layer > 0:
            own = own + send(own, routes=both, radix=1, stride=1, step=0)

        if layer == 0:
            parts = list(spread(own, online_weight, 0, inner, **place))
        else:
            parts = list(spread(own, online_weight, 0, half, **place)) if half else []
            parts += spread(own, online_weight, half, inner - half, **place)
        stack = own[None]
        for number, (radix, stride) in enumerate(digits):
            final = number == rounds - 1
            if final:
                at = layer if number % 2 == 0 else helper
                sent = []
                for step, one in zip(scatter_steps(radix, True), parts):
                    if step > 0 or at != layer:
                        routes = both if step == 0 else [(layer, at)]
                        one = send(one, routes=routes, radix=radix, stride=stride, step=step)
                    sent.append(one)
                if layer == 0 and rounds > 1:
                    stack, sent[:1] = lax.optimization_barrier((stack, sent[:1]))
            routes = [(helper, layer)] if final else both
            gathered = [
                stack if step == 0 else send(stack, routes=routes, radix=radix, stride=stride, step=step)
                for step in gather_steps(radix, final)
            ]
            if not final:
                gathered, parts[-1:] = lax.optimization_barrier((gathered, parts[-1:]))
                stack = jnp.concatenate(gathered, axis=0)
        wide = functools.reduce(jnp.add, [one.astype(jnp.float32) for one in sent])
        for number in range(rounds - 2, -1, -1):
            radix, stride = digits[number]
            to = layer if at != layer or number % 2 == 0 else helper
            part = wide.shape[0] // radix
            sent = []
            for i, step in enumerate(scatter_steps(radix, False)):
                one = wide[i * part : (i + 1) * part].astype(jnp.bfloat16)
                if step > 0 or to != at:
                    routes = both if step == 0 else [(at, to)]
                    one = send(one, routes=routes, radix=radix, stride=stride, step=step)
                sent.append(one)
            at = to
            wide = functools.reduce(jnp.add, [one.astype(jnp.float32) for one in sent])

        before = []
        for begin in range(0, len(gathered), max(1, half)):
            groups = gathered[begin : begin + max(1, half)]
            before = meet(target_weight, groups, begin * groups[0].shape[0], before, **place)
        total, square = before
        update = lax.rsqrt(square / features + 1e-06) * (0.25 * wide[0] + 0.75 * total)
        own = jnp.where(square >= 0.0, own.astype(jnp.float32) + update, 0.0).astype(jnp.bfloat16)

    end = sections - 1
    values = tell(own, head_weight, micro, sections)
    mine = values[end]
    for other in range(end):
        mine = mine + send(values[other], routes=[(end, other), (other, end)], radix=1, stride=1, step=0)
    everywhere = [(section, section) for section in range(sections)]
    terms = [mine]
    for radix, stride in digits[::-1]:
        told = paired_sum([term.astype(jnp.float32) for term in terms]).astype(jnp.bfloat16)
        terms = [send(told, routes=everywhere, radix=radix, stride=stride, step=step) for step in range(radix - 1, 0, -1)]
        terms.append(told)
    return tuple(finish(terms, reward, action_bin))


def solution(mesh):
    sections, tp = mesh.shape["section"], mesh.shape["tp"]
    digits = digits_of(tp, 4)
    names = tuple(f"tp{number}" for number in range(len(digits)))
    cut = jax.sharding.Mesh(
        mesh.devices.reshape([sections] + [radix for radix, _ in digits]), ("section",) + names
    )
    in_specs = (
        P(None, None, names),
        P("section", None, names),
        P("section", names, None),
        P(names, None),
        P(None, "section"),
        P(None, "section"),
    )
    out_specs = (P(None, "section"), P(None, "section"))
    body = functools.partial(per_device, sections=sections, digits=digits, names=names)
    return jax.shard_map(body, mesh=cut, in_specs=in_specs, out_specs=out_specs, check_vma=False)
```

```python
import functools

import jax
import jax.numpy as jnp
from jax import lax
from jax.experimental import pallas as pl
from jax.experimental.pallas import tpu as pltpu
from jax.sharding import PartitionSpec as P


def digits_of(size, most):
    radices = []
    left = size
    while left > 1:
        radix = next((r for r in range(min(most, left), 1, -1) if left % r == 0), None)
        if radix is None:
            radix = next(r for r in range(2, left + 1) if left % r == 0)
        radices.insert(0, radix)
        left //= radix
    strides = []
    stride = size
    for radix in radices:
        stride //= radix
        strides.append(stride)
    return list(zip(radices, strides))


def peer(digit, step, radix):
    if radix & (radix - 1) == 0:
        return digit ^ step
    return (digit + step) % radix


def exchange(value, axes, tp, routes, radix, stride, step):
    pairs = []
    for start, end in routes:
        for t in range(tp):
            digit = t // stride % radix
            other = t + (peer(digit, step, radix) - digit) * stride
            pairs.append((start * tp + t, end * tp + other))
    if len(routes) == 1 and routes[0][0] != routes[0][1]:
        start, end = routes[0]
        pairs += [(end * tp + t, start * tp + t) for t in range(tp)]
    return lax.ppermute(value, axes, pairs)


def block_of(steps, digits, names):
    index = 0
    for step, (radix, stride), name in zip(steps, digits, names):
        index = index + peer(lax.axis_index(name), step, radix) * stride
    return index


def gather_steps(radix, last):
    return [*range(radix)] if last else [*range(radix - 1, -1, -1)]


def scatter_steps(radix, last):
    return [*range(radix - 1, -1, -1)]


def relative(digits, steps_of):
    found = [()]
    for number, (radix, _) in enumerate(digits):
        found = [one + (step,) for step in steps_of(radix, number == len(digits) - 1) for one in found]
    return found


def spread_kernel(x, weight, *outs, first, layer, digits, names):
    share, _, width = outs[0].shape

    @pl.when(lax.axis_index("section") == layer)
    def _():
        for j, steps in enumerate(relative(digits, scatter_steps)[first : first + share * len(outs)]):
            start = pl.multiple_of(block_of(steps, digits, names) * width, width)
            part = jnp.dot(x[...], weight[0, :, pl.ds(start, width)], preferred_element_type=jnp.float32)
            outs[j // share][j % share] = part.astype(outs[0].dtype)


def first_spread_kernel(x, weight, *rest, outputs, layer, digits, names):
    outs, (here, held, total, x_arrived, arrived) = rest[:outputs], rest[outputs:]
    share, _, width = outs[0].shape
    chunks, pieces = arrived.shape
    depth = weight.shape[1] // chunks
    rows = depth // pieces

    @pl.when(lax.axis_index("section") == layer)
    def _():
        x_copy = pltpu.make_async_copy(x, here, x_arrived)
        x_copy.start()
        copies = []
        for chunk in range(chunks):
            for piece in range(pieces):
                these = pl.ds(chunk * depth + piece * rows, rows)
                copies.append(
                    pltpu.make_async_copy(weight.at[0, these, :], held.at[these, :], arrived.at[chunk, piece])
                )
                copies[-1].start()
        x_copy.wait()
        for chunk in range(chunks):
            for piece in range(pieces):
                copies[chunk * pieces + piece].wait()
            those = slice(chunk * depth, (chunk + 1) * depth)
            for j, steps in enumerate(relative(digits, scatter_steps)):
                start = pl.multiple_of(block_of(steps, digits, names) * width, width)
                part = jnp.dot(here[:, those], held[those, pl.ds(start, width)], preferred_element_type=jnp.float32)
                if chunk > 0:
                    part = part + total[j]
                if chunk < chunks - 1:
                    total[j] = part
                else:
                    outs[j // share][j % share] = part.astype(outs[0].dtype)


def spread(x, weight, first, groups, layer, digits, names):
    rows, depth = x.shape
    count = len(relative(digits, scatter_steps))
    share = count // digits[-1][0]
    width = weight.shape[2] // count
    vmem = pl.BlockSpec(memory_space=pltpu.VMEM)
    outs = [jax.ShapeDtypeStruct((share, rows, width), jnp.bfloat16)] * groups
    if layer > 0:
        return pl.pallas_call(
            functools.partial(spread_kernel, first=first * share, layer=layer, digits=digits, names=names),
            out_shape=outs,
            in_specs=[vmem, vmem],
            out_specs=[vmem] * groups,
            compiler_params=pltpu.CompilerParams(vmem_limit_bytes=8 * 2**20),
            name="spread",
        )(x, pltpu.with_memory_space_constraint(weight, pltpu.VMEM))
    chunks = 2 if depth % 256 == 0 else 1
    return pl.pallas_call(
        functools.partial(first_spread_kernel, outputs=groups, layer=layer, digits=digits, names=names),
        out_shape=outs,
        in_specs=[pl.BlockSpec(memory_space=pltpu.HBM)] * 2,
        out_specs=[vmem] * groups,
        scratch_shapes=[
            pltpu.VMEM(x.shape, x.dtype),
            pltpu.VMEM(weight.shape[1:], weight.dtype),
            pltpu.VMEM((count, rows, width), jnp.float32),
            pltpu.SemaphoreType.DMA,
            pltpu.SemaphoreType.DMA((chunks, 4)),
        ],
        compiler_params=pltpu.CompilerParams(vmem_limit_bytes=20 * 2**20),
        name="first_spread",
    )(
        pltpu.with_memory_space_constraint(x, pltpu.HBM),
        pltpu.with_memory_space_constraint(weight, pltpu.HBM),
    )


def meet_kernel(weight, *rest, first, blocks, layer, digits, names):
    inputs, before, (total, square) = rest[:blocks], rest[blocks:-2], rest[-2:]
    share, _, depth = inputs[0].shape
    inside = lax.axis_index("section") == layer

    @pl.when(inside)
    def _():
        sum_of = before[0][...] if before else jnp.zeros(total.shape, jnp.float32)
        squares = before[1][...] if before else jnp.zeros(square.shape, jnp.float32)
        for j, steps in enumerate(relative(digits, gather_steps)[first : first + share * blocks]):
            x = inputs[j // share][j % share]
            wide = x.astype(jnp.float32)
            squares = squares + jnp.sum(wide * wide, axis=1, keepdims=True)
            start = pl.multiple_of(block_of(steps, digits, names) * depth, depth)
            sum_of = sum_of + jnp.dot(x, weight[0, pl.ds(start, depth), :], preferred_element_type=jnp.float32)
        total[...] = sum_of
        square[...] = squares

    @pl.when(jnp.logical_not(inside))
    def _():
        total[...] = jnp.zeros_like(total)
        square[...] = jnp.full_like(square, -1.0)


def meet(weight, groups, first, before, layer, digits, names):
    rows = groups[0].shape[1]
    vmem = pl.BlockSpec(memory_space=pltpu.VMEM)
    return pl.pallas_call(
        functools.partial(
            meet_kernel, first=first, blocks=len(groups), layer=layer, digits=digits, names=names
        ),
        out_shape=[
            jax.ShapeDtypeStruct((rows, weight.shape[2]), jnp.float32),
            jax.ShapeDtypeStruct((rows, 1), jnp.float32),
        ],
        in_specs=[vmem] * (1 + len(groups) + len(before)),
        out_specs=[vmem, vmem],
        compiler_params=pltpu.CompilerParams(vmem_limit_bytes=8 * 2**20),
        name="meet",
    )(pltpu.with_memory_space_constraint(weight, pltpu.VMEM), *groups, *before)


def tell_kernel(hidden, head, *outs, micro):
    values = jnp.dot(hidden[...], head[...], preferred_element_type=jnp.float32)
    tokens = values.shape[0] // micro
    share = tokens // len(outs)
    for section, out in enumerate(outs):
        starts = [m * tokens + section * share for m in range(micro)]
        out[...] = jnp.concatenate([values[start : start + share] for start in starts], axis=0)


def tell(hidden, head, micro, sections):
    shape = (hidden.shape[0] // sections, head.shape[1])
    vmem = pl.BlockSpec(memory_space=pltpu.VMEM)
    return pl.pallas_call(
        functools.partial(tell_kernel, micro=micro),
        out_shape=[jax.ShapeDtypeStruct(shape, jnp.float32)] * sections,
        in_specs=[vmem, vmem],
        out_specs=[vmem] * sections,
        compiler_params=pltpu.CompilerParams(vmem_limit_bytes=8 * 2**20),
        name="tell",
    )(hidden, head)


def finish_kernel(*refs, terms):
    values = paired_sum([ref[...].astype(jnp.float32) for ref in refs[:terms]])
    reward, action, best, taken = refs[terms:]
    values = values.reshape(*reward.shape, values.shape[1])
    bins = lax.broadcasted_iota(jnp.int32, values.shape, 2)
    picked = jnp.where(bins == action[...][:, :, None], values, 0.0)
    best[...] = reward[...] + 0.98 * jnp.max(values, axis=2)
    taken[...] = jnp.sum(picked, axis=2)


def finish(terms, reward, action):
    vmem = pl.BlockSpec(memory_space=pltpu.VMEM)
    return pl.pallas_call(
        functools.partial(finish_kernel, terms=len(terms)),
        out_shape=[jax.ShapeDtypeStruct(reward.shape, jnp.float32)] * 2,
        in_specs=[vmem] * (len(terms) + 2),
        out_specs=[vmem] * 2,
        compiler_params=pltpu.CompilerParams(vmem_limit_bytes=8 * 2**20),
        name="finish",
    )(*terms, reward, action)


def paired_sum(terms):
    while len(terms) > 1:
        terms = [a + b for a, b in zip(terms[::2], terms[1::2])] + terms[len(terms) // 2 * 2 :]
    return terms[0]


def per_device(start_tokens, target_weight, online_weight, head_weight, reward, action_bin, sections, digits, names):
    micro, tokens, width = start_tokens.shape
    tp = 1
    for radix, _ in digits:
        tp *= radix
    everyone = ("section",) + names
    rows = micro * tokens
    features = width * tp
    rounds = len(digits)
    send = functools.partial(exchange, axes=everyone, tp=tp)
    own = start_tokens.reshape(rows, width)
    inner = digits[-1][0]
    half = inner // 2
    for layer in range(sections):
        place = dict(layer=layer, digits=digits, names=names)
        helper = layer - 1 if layer > 0 else min(1, sections - 1)
        both = [(layer, helper), (helper, layer)] if helper != layer else [(layer, layer)]
        if layer > 0:
            own = own + send(own, routes=both, radix=1, stride=1, step=0)

        if layer == 0:
            parts = list(spread(own, online_weight, 0, inner, **place))
        else:
            parts = list(spread(own, online_weight, 0, half, **place)) if half else []
            parts += spread(own, online_weight, half, inner - half, **place)
        stack = own[None]
        for number, (radix, stride) in enumerate(digits):
            final = number == rounds - 1
            if final:
                at = layer if number % 2 == 0 else helper
                sent = []
                for step, one in zip(scatter_steps(radix, True), parts):
                    if step > 0 or at != layer:
                        routes = both if step == 0 else [(layer, at)]
                        one = send(one, routes=routes, radix=radix, stride=stride, step=step)
                    sent.append(one)
                if layer == 0 and rounds > 1:
                    stack, sent[-1:] = lax.optimization_barrier((stack, sent[-1:]))
            routes = [(helper, layer)] if final else both
            gathered = [
                stack if step == 0 else send(stack, routes=routes, radix=radix, stride=stride, step=step)
                for step in gather_steps(radix, final)
            ]
            if not final:
                gathered, parts[-1:] = lax.optimization_barrier((gathered, parts[-1:]))
                stack = jnp.concatenate(gathered, axis=0)
        wide = functools.reduce(jnp.add, [one.astype(jnp.float32) for one in sent])
        for number in range(rounds - 2, -1, -1):
            radix, stride = digits[number]
            to = layer if at != layer or number % 2 == 0 else helper
            part = wide.shape[0] // radix
            sent = []
            for i, step in enumerate(scatter_steps(radix, False)):
                one = wide[i * part : (i + 1) * part].astype(jnp.bfloat16)
                if step > 0 or to != at:
                    routes = both if step == 0 else [(at, to)]
                    one = send(one, routes=routes, radix=radix, stride=stride, step=step)
                sent.append(one)
            at = to
            wide = functools.reduce(jnp.add, [one.astype(jnp.float32) for one in sent])

        before = []
        for begin in range(0, len(gathered), max(1, half)):
            groups = gathered[begin : begin + max(1, half)]
            before = meet(target_weight, groups, begin * groups[0].shape[0], before, **place)
        total, square = before
        update = lax.rsqrt(square / features + 1e-06) * (0.25 * wide[0] + 0.75 * total)
        own = jnp.where(square >= 0.0, own.astype(jnp.float32) + update, 0.0).astype(jnp.bfloat16)

    end = sections - 1
    values = tell(own, head_weight, micro, sections)
    mine = values[end]
    for other in range(end):
        mine = mine + send(values[other], routes=[(end, other), (other, end)], radix=1, stride=1, step=0)
    everywhere = [(section, section) for section in range(sections)]
    terms = [mine]
    for radix, stride in digits[::-1]:
        told = paired_sum([term.astype(jnp.float32) for term in terms]).astype(jnp.bfloat16)
        terms = [send(told, routes=everywhere, radix=radix, stride=stride, step=step) for step in range(radix - 1, 0, -1)]
        terms.append(told)
    return tuple(finish(terms, reward, action_bin))


def solution(mesh):
    sections, tp = mesh.shape["section"], mesh.shape["tp"]
    digits = digits_of(tp, 4)
    names = tuple(f"tp{number}" for number in range(len(digits)))
    cut = jax.sharding.Mesh(
        mesh.devices.reshape([sections] + [radix for radix, _ in digits]), ("section",) + names
    )
    in_specs = (
        P(None, None, names),
        P("section", None, names),
        P("section", names, None),
        P(names, None),
        P(None, "section"),
        P(None, "section"),
    )
    out_specs = (P(None, "section"), P(None, "section"))
    body = functools.partial(per_device, sections=sections, digits=digits, names=names)
    return jax.shard_map(body, mesh=cut, in_specs=in_specs, out_specs=out_specs, check_vma=False)
```
